512 devices in a mesh: branch: 2 (over y_hi), trow: 8 (over z), tcol: 32 (over x, y_lo, core).
Axes of the slice: x: 4, y: 8 (y_hi: 2, y_lo: 4; y = y_hi * 4 + y_lo), z: 8, core: 2. Of those that a mesh axis runs over, the one named last changes fastest.
Arguments:
- latent: bfloat16 [2, 2, 64, 256, 1152], P('branch', None, 'trow', 'tcol'), may hold values from -6 to 6
- modulation: float32 [2, 3, 1152], replicated, may hold values from -2 to 2
- w_query: bfloat16 [2, 1152, 576], P('branch', None, 'tcol'), may hold values from -0.176776695 to 0.176776695
- w_keyval: bfloat16 [2, 1152, 1152], P('branch', None, 'tcol'), may hold values from -3.8301617 to 3.8301617
- w_out: bfloat16 [2, 576, 1152], P('branch', 'tcol'), may hold values from -0.25 to 0.25
- w_zero: bfloat16 [1152, 1152], P(None, 'tcol'), may hold values from -0.1875 to 0.1875
Outputs:
- hidden_out: bfloat16 [2, 2, 64, 256, 1152], P('branch', None, 'trow', 'tcol')
The draws below stay inside these ranges and needn't reach their ends.
All inputs are finite; a program needn't handle non-finite values.
Results may differ from the reference program's by a relative error of at most 0.0075.
Values may be sent and summed in bfloat16 or wider, within the bound.
A program may use at most 128 MiB of HBM per device.

```python
import math
import jax
import jax.numpy as jnp
from jax import lax

D = 1152
HD = 72
HEADS = 8
WIN = 13
IMGS = 2
HW = 576
H = 64
W = 256


def clipped_normal(key, full_shape, bound_abs):
    return jnp.clip(jax.random.normal(key, full_shape, jnp.float32), -bound_abs, bound_abs)


def query_weights(key):
    return clipped_normal(jax.random.fold_in(key, 101), (2, D, HW), 5.0) / math.sqrt(D)


def draw_w_query(key, part):
    return query_weights(key).astype(jnp.bfloat16)


def draw_w_keyval(key, part):
    noise_part = clipped_normal(jax.random.fold_in(key, 102), (2, D, 2 * HW), 5.0) / math.sqrt(D)
    return noise_part.astype(jnp.bfloat16)


def draw_latent(key, part):
    fresh_draw = clipped_normal(jax.random.fold_in(key, 201), (2, IMGS, H, W, D), 6.0)
    return fresh_draw.astype(jnp.bfloat16)


def block_levels(stream_key, extent, shards, least, top_value):
    factor_of, own = 1.0, jax.random.fold_in(stream_key, 6)
    for dim, parts in shards:
        draws = jnp.exp(jax.random.uniform(jax.random.fold_in(own, dim), (parts,), jnp.float32, least / len(shards), top_value / len(shards)))
        factor_of = factor_of * jnp.repeat(draws, extent[dim] // parts).reshape([-1 if axis == dim else 1 for axis in range(len(extent))])
    return factor_of


def scatter_about(own_key, shape, scale, most, cuts=(), held_as=jnp.bfloat16):
    drawn = scale * jax.random.normal(own_key, shape, jnp.float32)
    if cuts:
        drawn = drawn * block_levels(own_key, shape, cuts, -0.22, 0.18)
    return jnp.clip(drawn, -most, most).astype(held_as)


def setup_inputs(seed: int = 0) -> dict:
    arg_keys = jax.random.split(jax.random.key(seed), 7)
    return {
        "latent": draw_latent(jax.random.fold_in(arg_keys[6], 71), 0),
        "modulation": scatter_about(arg_keys[1], (2, 3, D), 0.5, 2.0, (), jnp.float32),
        "w_query": draw_w_query(jax.random.fold_in(arg_keys[6], 71), 0),
        "w_keyval": draw_w_keyval(jax.random.fold_in(arg_keys[6], 71), 0),
        "w_out": scatter_about(arg_keys[4], (2, HW, D), HW ** -0.5, 0.25, ((0, 2), (1, 32))),
        "w_zero": scatter_about(arg_keys[5], (D, D), D ** -0.5, 0.1875, ((1, 32),)),
    }


def modulate(hidden, shift_scale):
    average = lax.optimization_barrier(jnp.mean(hidden, axis=-1, keepdims=True))
    centred = hidden - average
    variance = lax.optimization_barrier(jnp.mean(centred * centred, axis=-1, keepdims=True))
    return (centred * lax.rsqrt(variance + 1e-06) * (1.0 + shift_scale[1]) + shift_scale[0]).astype(jnp.bfloat16)

def neighbor_attention(queries, key_values):
    radius = WIN // 2
    scaling = 1.0 / math.sqrt(HD)
    query_all = queries.astype(jnp.float32).reshape(IMGS, H, W, HEADS, HD)
    key_part = key_values[..., :HW].reshape(IMGS, H, W, HEADS, HD)
    value_part = key_values[..., HW:].reshape(IMGS, H, W, HEADS, HD)
    row_starts = jnp.clip(jnp.arange(H) - radius, 0, H - WIN).astype(jnp.int32)
    col_starts = jnp.clip(jnp.arange(W) - radius, 0, W - WIN).astype(jnp.int32)

    def shifted(source, offset):
        row_offset = (offset // WIN).astype(jnp.int32)
        col_offset = (offset % WIN).astype(jnp.int32)
        picked = jnp.take(source, row_starts + row_offset, axis=1)
        picked = jnp.take(picked, col_starts + col_offset, axis=2)
        return picked.astype(jnp.float32)

    def scores_at(offset):
        return lax.optimization_barrier(jnp.sum(query_all * shifted(key_part, offset), axis=-1)) * scaling

    def first_pass(offset, carry):
        running_max, totals = carry
        current = scores_at(offset)
        new_max = jnp.maximum(running_max, current)
        totals = totals * jnp.exp(running_max - new_max) + jnp.exp(current - new_max)
        return (new_max, totals)
    start_max = jnp.full((IMGS, H, W, HEADS), -1e+30, jnp.float32)
    start_total = jnp.zeros((IMGS, H, W, HEADS), jnp.float32)
    highest, totals = lax.fori_loop(0, WIN * WIN, first_pass, (start_max, start_total))

    def second_pass(offset, accumulated):
        weights = (jnp.exp(scores_at(offset) - highest) / totals).astype(jnp.bfloat16).astype(jnp.float32)
        return accumulated + weights[..., None] * shifted(value_part, offset)
    accumulated = lax.fori_loop(0, WIN * WIN, second_pass, jnp.zeros((IMGS, H, W, HEADS, HD), jnp.float32))
    return accumulated.reshape(IMGS, H, W, HW).astype(jnp.bfloat16)

def run_copy(hidden, shift_scale, weight_q, weight_kv, weight_o):
    flattened = modulate(hidden, shift_scale).reshape(-1, D)
    queries = jnp.dot(flattened, weight_q, preferred_element_type=jnp.float32).astype(jnp.bfloat16)
    key_values = jnp.dot(flattened, weight_kv, preferred_element_type=jnp.float32).astype(jnp.bfloat16)
    attended = neighbor_attention(queries.reshape(IMGS, H, W, HW), key_values.reshape(IMGS, H, W, 2 * HW))
    projected = jnp.dot(attended.reshape(-1, HW), weight_o, preferred_element_type=jnp.float32)
    return (hidden + shift_scale[2] * projected.reshape(hidden.shape)).astype(jnp.bfloat16)

def reference(latent, modulation, w_query, w_keyval, w_out, w_zero):
    base_rows = latent[0].astype(jnp.float32)
    control_in = base_rows + latent[1].astype(jnp.float32)
    control_out = run_copy(control_in, modulation[1], w_query[1], w_keyval[1], w_out[1])
    residual = jnp.dot(control_out.reshape(-1, D), w_zero, preferred_element_type=jnp.float32).astype(jnp.bfloat16)
    base_in = base_rows + residual.reshape(base_rows.shape).astype(jnp.float32)
    base_out = run_copy(base_in, modulation[0], w_query[0], w_keyval[0], w_out[0])
    return jnp.stack([base_out, control_out])
```

```python
import math

import jax
import jax.numpy as jnp
from jax import lax
from jax.experimental import pallas as pl
from jax.experimental.pallas import tpu as pltpu
from jax.sharding import PartitionSpec as P

MESH = pl.DeviceIdType.MESH
F32 = jnp.float32
BF16 = jnp.bfloat16
D = 1152
HD = 72
GP = 24
HP = 96
NEG = -1e30
NT = (((1,), (1,)), ((), ()))
NN = (((1,), (0,)), ((), ()))


def dot(a, b, dims):
    return lax.dot_general(a, b, dims, preferred_element_type=F32)


def pick(rows, cols, pieces):
    r = lax.broadcasted_iota(jnp.int32, (rows, cols), 0)
    c = lax.broadcasted_iota(jnp.int32, (rows, cols), 1)
    hit = None
    for row0, col0, count in pieces:
        one = (r - row0 == c - col0) & (r >= row0) & (r < row0 + count)
        hit = one if hit is None else hit | one
    return jnp.where(hit, 1.0, 0.0).astype(BF16)


def kernel(
    lat, mod, wq, wkv, wo, wz, out,
    wb, g1, g0, gb, kvo, kvl, kvr, ob, ab, bias, hid, rlat, stage, q_s,
    lat_s, lat_r, w1y_s, w1x_s, w1s_s, w1_r, g1y_s, g1x_s, g1s_s, g1y_r, g1x_r, g1s_r,
    g0x_s, g0s_s, g0y_r, g0x_r, g0s_r, z_s, z_r, h_s, h_r, a_s, a_r, o_s, o_r,
):
    b = lax.axis_index("branch")
    z = lax.axis_index("trow")
    t = lax.axis_index("tcol")
    x, y, c = t // 8, (t // 2) % 4, t % 2
    yy = b * 4 + y
    partner = (1 - b, z, t)
    sibling = (b, z, t + 1 - 2 * c)
    left = (b, z, (t + 31) % 32)
    right = (b, z, (t + 1) % 32)
    column = []
    for k in range(1, 8):
        other = (yy + k) % 8
        column.append((other // 4, z, x * 8 + (other % 4) * 2 + c))
    line = [(b, z, ((x + k) % 4) * 8 + y * 2 + c) for k in range(1, 4)]
    ring = [(b, (z + k) % 8, t) for k in range(1, 8)]
    far = jnp.where(c == 0, (t + 31) % 32, (t + 1) % 32)

    def send(src, dst, ss, rs, dev):
        copy = pltpu.make_async_remote_copy(
            src_ref=src, dst_ref=dst, send_sem=ss, recv_sem=rs, device_id=dev, device_id_type=MESH
        )
        copy.start()
        return copy

    def arrived(dst, rs):
        pltpu.make_async_remote_copy(
            src_ref=dst, dst_ref=dst, send_sem=lat_s.at[0], recv_sem=rs, device_id=partner, device_id_type=MESH
        ).wait_recv()

    def sent(src, ss):
        pltpu.make_async_remote_copy(
            src_ref=src, dst_ref=src, send_sem=ss, recv_sem=lat_r.at[0], device_id=partner, device_id_type=MESH
        ).wait_send()

    barrier = pltpu.get_barrier_semaphore()
    for dev in column + line + ring + [sibling, (b, z, far)]:
        pl.semaphore_signal(barrier, inc=1, device_id=dev, device_id_type=MESH)

    rows = (
        dot(pick(144, 18, [(0, 0, 18)]), wq[...], NT)
        + dot(pick(144, 36, [(32, 0, 18), (56, 18, 18)]), wkv[...], NT)
        + dot(pick(144, 36, [(80, 0, 36)]), wz[...], NT)
        + dot(pick(144, 18, [(120, 0, 18)]), wo[...], NN)
    ).astype(BF16)
    own_q, own_kv = t // 4 == z, (t // 2) % 8 == z
    q_row = pl.multiple_of(32 * (t % 4), 16)
    kv_row = pl.multiple_of(128 + 96 * (t // 16) + 48 * c, 16)
    kv_idx = 4 + 2 * (t // 16) + c

    @pl.when(own_q)
    def _():
        wb[b, pl.ds(q_row, 32), :] = rows[0:32]

    @pl.when(own_kv)
    def _():
        wb[b, pl.ds(kv_row, 48), :] = rows[32:80]

    @pl.when(b == 1)
    def _():
        g1[c, x, y] = rows[80:144]

    @pl.when(b == 0)
    def _():
        g0[c, x, y] = jnp.concatenate(
            [rows[120:144].astype(F32), jnp.zeros((8, D), F32)], axis=0
        ).astype(BF16)

    pl.semaphore_wait(barrier, 19)

    lat_copy = send(lat.at[1 - b], rlat, lat_s.at[0], lat_r.at[0], partner)

    def w1_y(start):
        @pl.when(own_q)
        def _():
            piece = wb.at[b, pl.ds(q_row, 32)]
            for k in range(7):
                if start:
                    send(piece, piece, w1y_s.at[0, k], w1_r.at[b * 8 + t % 4], column[k])
                else:
                    sent(piece, w1y_s.at[0, k])

        @pl.when(own_kv)
        def _():
            piece = wb.at[b, pl.ds(kv_row, 48)]
            for k in range(7):
                if start:
                    send(piece, piece, w1y_s.at[1, k], w1_r.at[b * 8 + kv_idx], column[k])
                else:
                    sent(piece, w1y_s.at[1, k])

    def w2_y(start):
        @pl.when(b == 1)
        def _():
            piece = g1.at[c, x, y]
            for k in range(7):
                if start:
                    send(piece, piece, g1y_s.at[k], g1y_r.at[y], column[k])
                else:
                    sent(piece, g1y_s.at[k])

        @pl.when(b == 0)
        def _():
            piece = g0.at[c, x, y]
            for k in range(7):
                if start:
                    send(piece, piece, g1y_s.at[k], g0y_r.at[y], column[k])
                else:
                    sent(piece, g1y_s.at[k])

    w1_y(True)
    w2_y(True)

    for block in range(4):
        first, last = max(block - 1, 0), min(block + 1, 3)
        lanes = (last - first + 1) * 128
        q = lax.broadcasted_iota(jnp.int32, (128, lanes), 0)
        k = lax.broadcasted_iota(jnp.int32, (128, lanes), 1)
        i, j = block * 16 + q // 8, t * 8 + q % 8
        row, col = first * 16 + k // 8, (t - 1) * 8 + k % 8
        row0, col0 = jnp.clip(i - 6, 0, 51), jnp.clip(j - 6, 0, 243)
        row_ok = (row >= row0) & (row < row0 + 13)
        for strip in range(3):
            here = col + 8 * strip
            ok = row_ok & (here >= col0) & (here < col0 + 13)
            bias[block, :, strip * lanes : (strip + 1) * lanes] = jnp.where(ok, 0.0, NEG)
    ob[...] = jnp.zeros_like(ob)

    def normed(hidden, copy):
        average = jnp.mean(hidden, axis=-1, keepdims=True)
        centred = hidden - average
        variance = jnp.mean(centred * centred, axis=-1, keepdims=True)
        shift, scale = mod[copy, 0:1, :], mod[copy, 1:2, :]
        return (centred * lax.rsqrt(variance + 1e-06) * (1.0 + scale) + shift).astype(BF16)

    def slot(copy, index, half=None):
        start = 64 * ((index + 8) % 8)
        if half is None:
            return gb.at[copy, pl.ds(pl.multiple_of(start, 64), 64)]
        return gb.at[copy, pl.ds(pl.multiple_of(start + 32 * half, 32), 32)]

    def ring_step(copy, s):
        if s > 1:
            arrived(slot(copy, z - (s - 1)), z_r.at[copy, 0, s - 2])
        if s < 4:
            up = slot(copy, z - s + 1)
            down = slot(copy, z + s - 1)
        else:
            up = slot(copy, z - 3, 0)
            down = slot(copy, z + 3, 1)
        send(up, up, z_s.at[copy, 0, s - 1], z_r.at[copy, 0, s - 1], ring[0])
        if s > 1:
            arrived(slot(copy, z + (s - 1)), z_r.at[copy, 1, s - 2])
        send(down, down, z_s.at[copy, 1, s - 1], z_r.at[copy, 1, s - 1], ring[6])

    def ring_end(copy):
        arrived(slot(copy, z - 4, 0), z_r.at[copy, 0, 3])
        arrived(slot(copy, z + 4, 1), z_r.at[copy, 1, 3])

    def ring_sent(copy):
        for s in range(1, 4):
            sent(slot(copy, z - s + 1), z_s.at[copy, 0, s - 1])
            sent(slot(copy, z + s - 1), z_s.at[copy, 1, s - 1])
        sent(slot(copy, z - 3, 0), z_s.at[copy, 0, 3])
        sent(slot(copy, z + 3, 1), z_s.at[copy, 1, 3])

    def kinds(core):
        return (
            (32 * core, 32, core, 4 * z + core, z // 2),
            (32 * core + 64, 32, core + 2, 4 * z + core + 2, z // 2),
            (128 + 48 * core, 48, 4 + core, 2 * z + core, z // 4),
            (224 + 48 * core, 48, 6 + core, 16 + 2 * z + core, 2 + z // 4),
        )

    def w1_forward(copy):
        for n, (row, count, index, source, source_x) in enumerate(kinds(c)):
            piece = wb.at[copy, pl.ds(pl.multiple_of(row, 16), count)]

            @pl.when(jnp.logical_not((t == source) & (b == copy)))
            def _():
                arrived(piece, w1_r.at[copy * 8 + index])

            @pl.when(x == source_x)
            def _():
                for k in range(3):
                    send(piece, piece, w1x_s.at[copy, n, k], w1_r.at[copy * 8 + index], line[k])

            send(piece, piece, w1s_s.at[copy, n], w1_r.at[copy * 8 + index], sibling)

    def w1_end(copy):
        for row, count, index, source, source_x in kinds(1 - c):
            piece = wb.at[copy, pl.ds(pl.multiple_of(row, 16), count)]
            arrived(piece, w1_r.at[copy * 8 + index])

    def w1_sent(copy):
        for n, (row, count, index, source, source_x) in enumerate(kinds(c)):
            piece = wb.at[copy, pl.ds(pl.multiple_of(row, 16), count)]

            @pl.when(x == source_x)
            def _():
                for k in range(3):
                    sent(piece, w1x_s.at[copy, n, k])

            sent(piece, w1s_s.at[copy, n])

    def g1_line():
        for yk in range(4):
            piece = g1.at[c, x, yk]

            @pl.when(jnp.logical_not((b == 1) & (y == yk)))
            def _():
                arrived(piece, g1y_r.at[yk])

            for k in range(3):
                send(piece, piece, g1x_s.at[yk, k], g1x_r.at[x, yk], line[k])

    def g1_core():
        send(g1.at[c, x], g1.at[c, x], g1s_s.at[0], g1s_r.at[x], sibling)
        for k in range(1, 4):
            xk = (x + k) % 4
            for yk in range(4):
                arrived(g1.at[c, xk, yk], g1x_r.at[xk, yk])
            send(g1.at[c, xk], g1.at[c, xk], g1s_s.at[k], g1s_r.at[xk], sibling)

    def g1_end():
        for xk in range(4):
            arrived(g1.at[1 - c, xk], g1s_r.at[xk])

    def g1_sent():
        for yk in range(4):
            for k in range(3):
                sent(g1.at[c, x, yk], g1x_s.at[yk, k])
        for k in range(4):
            sent(g1.at[c, (x + k) % 4], g1s_s.at[k])

    def g0_line():
        for yk in range(4):

            @pl.when(jnp.logical_not((b == 0) & (y == yk)))
            def _():
                arrived(g0.at[c, x, yk], g0y_r.at[yk])

        for k in range(3):
            send(g0.at[c, x], g0.at[c, x], g0x_s.at[k], g0x_r.at[x], line[k])

    def g0_core():
        send(g0.at[c, x], g0.at[c, x], g0s_s.at[0], g0s_r.at[x], sibling)
        for k in range(1, 4):
            xk = (x + k) % 4
            arrived(g0.at[c, xk], g0x_r.at[xk])
            send(g0.at[c, xk], g0.at[c, xk], g0s_s.at[k], g0s_r.at[xk], sibling)

    def g0_end():
        for xk in range(4):
            arrived(g0.at[1 - c, xk], g0s_r.at[xk])

    def g0_sent():
        for k in range(3):
            sent(g0.at[c, x], g0x_s.at[k])
        for k in range(4):
            sent(g0.at[c, (x + k) % 4], g0s_s.at[k])

    def project(copy):
        w_q = jnp.concatenate(
            [wb[copy, 32 * n : 32 * n + 32, :].astype(F32)[0:GP] for n in range(4)], axis=0
        ).astype(BF16)
        tokens = gb[copy]
        kvo[copy] = dot(wb[copy, 128:320, :], tokens, NT).astype(BF16)
        send(kvo.at[copy], kvl.at[copy], h_s.at[copy, 0], h_r.at[copy, 0], right)
        send(kvo.at[copy], kvr.at[copy], h_s.at[copy, 1], h_r.at[copy, 1], left)
        q_s[...] = dot(tokens, w_q, NT).astype(BF16)

    def halo_end(copy):
        arrived(kvl.at[copy], h_r.at[copy, 0])
        arrived(kvr.at[copy], h_r.at[copy, 1])

    def attend(copy):
        for block in range(4):
            first, last = max(block - 1, 0), min(block + 1, 3)
            lanes = (last - first + 1) * 128
            span = slice(first * 128, first * 128 + lanes)
            keys = jnp.concatenate([ref[copy, 0:HP, span] for ref in (kvl, kvo, kvr)], axis=1)
            values = jnp.concatenate([ref[copy, HP : 2 * HP, span] for ref in (kvl, kvo, kvr)], axis=1)
            scores = dot(q_s[block * 128 : block * 128 + 128, :], keys, NN) * (1.0 / math.sqrt(HD))
            scores = scores + bias[block, :, 0 : 3 * lanes]
            raised = jnp.exp(scores - jnp.max(scores, axis=-1, keepdims=True))
            weights = (raised * (1.0 / jnp.sum(raised, axis=-1, keepdims=True))).astype(BF16)
            ob[copy, block * 128 : block * 128 + 128, 0:HP] = dot(weights, values, NT).astype(BF16)
            for tile in (2 * block, 2 * block + 1):

                @pl.when(z != tile)
                def _():
                    send(
                        ob.at[copy, pl.ds(64 * tile, 64)], ab.at[copy, z],
                        a_s.at[copy, tile], a_r.at[copy, z], (b, tile, t),
                    )

    def attended(copy):
        ab[copy, z] = ob[copy, pl.ds(pl.multiple_of(64 * z, 64), 64), :]
        for k in range(1, 8):
            head = (z + k) % 8
            arrived(ab.at[copy, head], a_r.at[copy, head])

    def attend_sent(copy):
        sent(kvo.at[copy], h_s.at[copy, 0])
        sent(kvo.at[copy], h_s.at[copy, 1])
        for tile in range(8):

            @pl.when(z != tile)
            def _():
                sent(ob.at[copy, pl.ds(64 * tile, 64)], a_s.at[copy, tile])

    def out_project(copy):
        total = jnp.zeros((64, D), F32)
        for head in range(8):
            parts = []
            for n in range(4):
                at = (n % 2, head // 2, 2 * (head % 2) + n // 2)
                if copy == 1:
                    parts.append(g1[at].astype(F32)[40:64])
                else:
                    parts.append(g0[at].astype(F32)[0:GP])
            w_head = jnp.concatenate(parts, axis=0).astype(BF16)
            total = total + dot(ab[copy, head][:, 0:HP], w_head, NN)
        return total

    def zero_project(control):
        parts = []
        for pair in range(16):
            two = [g1[core, pair // 4, pair % 4].astype(F32)[0:40] for core in range(2)]
            wide = dot(control, jnp.concatenate(two, axis=0).astype(BF16), NT)
            parts += [wide[:, 0:36], wide[:, 40:76]]
        return jnp.concatenate(parts, axis=1).astype(BF16)

    arrived(rlat, lat_r.at[0])
    mine, theirs = lat[b].astype(F32), rlat[...].astype(F32)
    control_in = mine + theirs
    hid[...] = control_in
    gb[1, pl.ds(pl.multiple_of(64 * z, 64), 64), :] = normed(control_in, 1)
    ring_step(1, 1)
    w1_forward(1)
    ring_step(1, 2)
    g1_line()
    ring_step(1, 3)
    w1_forward(0)
    ring_step(1, 4)
    w1_end(1)
    ring_end(1)
    project(1)
    g1_core()
    g0_line()
    halo_end(1)
    attend(1)
    g1_end()
    g0_core()
    attended(1)
    control = (hid[...] + mod[1, 2:3, :] * out_project(1)).astype(BF16)

    @pl.when(b == 0)
    def _():
        stage[...] = control
        send(stage, out.at[0], o_s.at[0], o_r.at[0], partner)

    @pl.when(b == 1)
    def _():
        out[1] = control

    residual = zero_project(control).astype(F32)
    base_in = jnp.where(b == 0, lat[b].astype(F32), rlat[...].astype(F32)) + residual
    hid[...] = base_in
    gb[0, pl.ds(pl.multiple_of(64 * z, 64), 64), :] = normed(base_in, 0)
    ring_step(0, 1)
    ring_step(0, 2)
    ring_step(0, 3)
    ring_step(0, 4)
    w1_end(0)
    ring_end(0)
    project(0)
    halo_end(0)
    attend(0)
    g0_end()
    attended(0)
    base = (hid[...] + mod[0, 2:3, :] * out_project(0)).astype(BF16)

    @pl.when(b == 1)
    def _():
        stage[...] = base
        send(stage, out.at[1], o_s.at[0], o_r.at[0], partner)

    @pl.when(b == 0)
    def _():
        out[0] = base

    lat_copy.wait_send()
    w1_y(False)
    w2_y(False)
    g1_sent()
    g0_sent()
    for copy in (1, 0):
        w1_sent(copy)
        ring_sent(copy)
        attend_sent(copy)
    sent(stage, o_s.at[0])
    arrived(out.at[1 - b], o_r.at[0])


def on_device(latent, modulation, w_query, w_keyval, w_out, w_zero):
    dma = pltpu.SemaphoreType.DMA
    vmem = pltpu.VMEM
    result = pl.pallas_call(
        kernel,
        out_shape=jax.ShapeDtypeStruct((2, 64, D), BF16),
        in_specs=[pl.BlockSpec(memory_space=pltpu.VMEM)] * 6,
        out_specs=pl.BlockSpec(memory_space=pltpu.VMEM),
        scratch_shapes=[
            vmem((2, 320, D), BF16),
            vmem((2, 4, 4, 64, D), BF16),
            vmem((2, 4, 4, 32, D), BF16),
            vmem((2, 512, D), BF16),
            vmem((2, 2 * HP, 512), BF16),
            vmem((2, 2 * HP, 512), BF16),
            vmem((2, 2 * HP, 512), BF16),
            vmem((2, 512, 128), BF16),
            vmem((2, 8, 64, 128), BF16),
            vmem((4, 128, D), F32),
            vmem((64, D), F32),
            vmem((64, D), BF16),
            vmem((64, D), BF16),
            vmem((512, HP), BF16),
            dma((1,)), dma((1,)),
            dma((2, 7)), dma((2, 4, 3)), dma((2, 4)), dma((16,)),
            dma((7,)), dma((4, 3)), dma((4,)), dma((4,)), dma((4, 4)), dma((4,)),
            dma((3,)), dma((4,)), dma((4,)), dma((4,)), dma((4,)),
            dma((2, 2, 4)), dma((2, 2, 4)), dma((2, 2)), dma((2, 2)),
            dma((2, 8)), dma((2, 8)), dma((1,)), dma((1,)),
        ],
        compiler_params=pltpu.CompilerParams(
            collective_id=0, has_side_effects=True, vmem_limit_bytes=56 * 1024 * 1024
        ),
    )(
        latent.reshape(2, 64, D), modulation, w_query[0], w_keyval[0], w_out[0], w_zero,
    )
    return result.reshape(latent.shape)


def solution(mesh):
    placed = (
        P("branch", None, "trow", "tcol", None),
        P(),
        P("branch", None, "tcol"),
        P("branch", None, "tcol"),
        P("branch", "tcol", None),
        P(None, "tcol"),
    )
    return jax.shard_map(
        on_device,
        mesh=mesh,
        in_specs=placed,
        out_specs=P("branch", None, "trow", "tcol", None),
        check_vma=False,
    )
```

```python
import math

import jax
import jax.numpy as jnp
from jax import lax
from jax.experimental import pallas as pl
from jax.experimental.pallas import tpu as pltpu
from jax.sharding import PartitionSpec as P

MESH = pl.DeviceIdType.MESH
F32 = jnp.float32
BF16 = jnp.bfloat16
D = 1152
HD = 72
GP = 24
HP = 96
NEG = -1e30
NT = (((1,), (1,)), ((), ()))
NN = (((1,), (0,)), ((), ()))


def dot(a, b, dims):
    return lax.dot_general(a, b, dims, preferred_element_type=F32)


def pick(rows, cols, pieces):
    r = lax.broadcasted_iota(jnp.int32, (rows, cols), 0)
    c = lax.broadcasted_iota(jnp.int32, (rows, cols), 1)
    hit = None
    for row0, col0, count in pieces:
        one = (r - row0 == c - col0) & (r >= row0) & (r < row0 + count)
        hit = one if hit is None else hit | one
    return jnp.where(hit, 1.0, 0.0).astype(BF16)


def kernel(
    lat_h, mod_h, wq_h, wkv_h, wo_h, wz_h, out,
    lat, mod, wq, wkv, wo, wz,
    wb, g1, g0, gb, kvo, kvl, kvr, ob, ab, ab0, bias, hid, rlat, rres, stage, res_s, q_s, wq_s,
    in_s, lat_s, lat_r, w1y_s, w1x_s, w1s_s, w1_r, g1y_s, g1x_s, g1s_s, g1y_r, g1x_r, g1s_r,
    g0y_s, g0x_s, g0s_s, g0y_r, g0x_r, g0s_r, z_s, z_r, h_s, h_r, a_s, a_r, a0_r, o_s, o_r, r_s, r_r,
):
    b = lax.axis_index("branch")
    z = lax.axis_index("trow")
    t = lax.axis_index("tcol")
    x, y, c = t // 8, (t // 2) % 4, t % 2
    yy = b * 4 + y
    partner = (1 - b, z, t)
    sibling = (b, z, t + 1 - 2 * c)
    left = (b, z, (t + 31) % 32)
    right = (b, z, (t + 1) % 32)
    column = []
    for k in range(1, 8):
        other = (yy + k) % 8
        column.append((other // 4, z, x * 8 + (other % 4) * 2 + c))
    line = [(b, z, ((x + k) % 4) * 8 + y * 2 + c) for k in range(1, 4)]
    ring = [(b, (z + k) % 8, t) for k in range(1, 8)]
    far = jnp.where(c == 0, (t + 31) % 32, (t + 1) % 32)

    def send(src, dst, ss, rs, dev):
        copy = pltpu.make_async_remote_copy(
            src_ref=src, dst_ref=dst, send_sem=ss, recv_sem=rs, device_id=dev, device_id_type=MESH
        )
        copy.start()
        return copy

    def arrived(dst, rs):
        pltpu.make_async_remote_copy(
            src_ref=dst, dst_ref=dst, send_sem=lat_s.at[0], recv_sem=rs, device_id=partner, device_id_type=MESH
        ).wait_recv()

    def sent(src, ss):
        pltpu.make_async_remote_copy(
            src_ref=src, dst_ref=src, send_sem=ss, recv_sem=lat_r.at[0], device_id=partner, device_id_type=MESH
        ).wait_send()

    barrier = pltpu.get_barrier_semaphore()
    across = [(1 - b, (z + k) % 8, t) for k in range(1, 8)]
    peers = column + line + ring + across + [sibling, (b, z, far)]
    for dev in peers:
        pl.semaphore_signal(barrier, inc=1, device_id=dev, device_id_type=MESH)

    loads = [
        pltpu.make_async_copy(src, dst, in_s.at[n])
        for n, (src, dst) in enumerate(
            ((wq_h, wq), (wkv_h, wkv), (wo_h, wo), (wz_h, wz), (lat_h, lat), (mod_h, mod))
        )
    ]
    for load in loads:
        load.start()
    for load in loads[:4]:
        load.wait()

    rows = (
        dot(pick(144, 18, [(0, 0, 18)]), wq[...], NN)
        + dot(pick(144, 36, [(32, 0, 18), (56, 18, 18)]), wkv[...], NN)
        + dot(pick(144, 36, [(80, 0, 36)]), wz[...], NN)
        + dot(pick(144, 18, [(120, 0, 18)]), wo[...], NN)
    ).astype(BF16)
    own_q, own_kv = t // 4 == z, (t // 2) % 8 == z
    q_row = pl.multiple_of(32 * (t % 4), 16)
    kv_row = pl.multiple_of(128 + 96 * (t // 16) + 48 * c, 16)
    kv_idx = 4 + 2 * (t // 16) + c

    @pl.when(own_q)
    def _():
        wb[b, pl.ds(q_row, 32), :] = rows[0:32]

    @pl.when(own_kv)
    def _():
        wb[b, pl.ds(kv_row, 48), :] = rows[32:80]

    @pl.when(b == 1)
    def _():
        g1[c, x, y] = rows[80:144]

    @pl.when(b == 0)
    def _():
        g0[c, x, y] = jnp.concatenate(
            [rows[120:144].astype(F32), jnp.zeros((8, D), F32)], axis=0
        ).astype(BF16)

    pl.semaphore_wait(barrier, len(peers))

    def lat_half(h):
        return send(
            lat_h.at[1 - b, pl.ds(32 * h, 32)], rlat.at[pl.ds(32 * h, 32)], lat_s.at[h], lat_r.at[h], partner
        )

    lat_copies = [lat_half(0), lat_half(1)]

    def w1_y(copy, start):
        @pl.when(own_q & (b == copy))
        def _():
            piece = wb.at[copy, pl.ds(q_row, 32)]
            for k in range(7):
                if start:
                    send(piece, piece, w1y_s.at[0, k], w1_r.at[copy * 8 + t % 4], column[k])
                else:
                    sent(piece, w1y_s.at[0, k])

        @pl.when(own_kv & (b == copy))
        def _():
            piece = wb.at[copy, pl.ds(kv_row, 48)]
            for k in range(7):
                if start:
                    send(piece, piece, w1y_s.at[1, k], w1_r.at[copy * 8 + kv_idx], column[k])
                else:
                    sent(piece, w1y_s.at[1, k])

    def g1_y(start):
        @pl.when(b == 1)
        def _():
            piece = g1.at[c, x, y]
            for k in range(7):
                if start:
                    send(piece, piece, g1y_s.at[k], g1y_r.at[y], column[k])
                else:
                    sent(piece, g1y_s.at[k])

    def g0_y(start):
        @pl.when(b == 0)
        def _():
            piece = g0.at[c, x, y]
            for k in range(1, 4):
                if start:
                    send(piece, piece, g0y_s.at[k - 1], g0y_r.at[y], (b, z, x * 8 + ((y + k) % 4) * 2 + c))
                else:
                    sent(piece, g0y_s.at[k - 1])

    w1_y(1, True)

    for block in range(4):
        first, last = max(block - 1, 0), min(block + 1, 3)
        lanes = (last - first + 1) * 128
        q = lax.broadcasted_iota(jnp.int32, (128, lanes), 0)
        k = lax.broadcasted_iota(jnp.int32, (128, lanes), 1)
        i, j = block * 16 + q // 8, t * 8 + q % 8
        row, col = first * 16 + k // 8, (t - 1) * 8 + k % 8
        row0, col0 = jnp.clip(i - 6, 0, 51), jnp.clip(j - 6, 0, 243)
        row_ok = (row >= row0) & (row < row0 + 13)
        for strip in range(3):
            here = col + 8 * strip
            ok = row_ok & (here >= col0) & (here < col0 + 13)
            bias[block, :, strip * lanes : (strip + 1) * lanes] = jnp.where(ok, 0.0, NEG)
    ob[...] = jnp.zeros_like(ob)

    def normed(hidden, copy):
        average = jnp.mean(hidden, axis=-1, keepdims=True)
        centred = hidden - average
        variance = jnp.mean(centred * centred, axis=-1, keepdims=True)
        shift, scale = mod[0, copy : copy + 1, :], mod[1, copy : copy + 1, :]
        return (centred * lax.rsqrt(variance + 1e-06) * (1.0 + scale) + shift).astype(BF16)

    def half_tile(copy, index, h):
        start = 64 * ((index + 8) % 8) + 32 * h
        return gb.at[copy, pl.ds(pl.multiple_of(start, 32), 32)]

    def ring_send(copy, s, way, h):
        tile = half_tile(copy, z - s + 1 if way == 0 else z + s - 1, h)
        send(tile, tile, z_s.at[copy, way, s - 1, h], z_r.at[copy, way, s - 1, h], ring[0] if way == 0 else ring[6])

    def ring_take(copy, s, way, h):
        arrived(half_tile(copy, z - s if way == 0 else z + s, h), z_r.at[copy, way, s - 1, h])

    def ring_start(copy, h):
        ring_send(copy, 1, 0, h)
        ring_send(copy, 1, 1, h)

    def ring_step(copy, s):
        for h in range(2):
            for way in range(2):
                ring_take(copy, s - 1, way, h)
                if s < 4 or h == way:
                    ring_send(copy, s, way, h)

    def ring_end(copy):
        ring_take(copy, 4, 0, 0)
        ring_take(copy, 4, 1, 1)

    def ring_sent(copy):
        for s in range(1, 5):
            for h in range(2):
                for way in range(2):
                    if s < 4 or h == way:
                        sent(half_tile(copy, z, h), z_s.at[copy, way, s - 1, h])

    def kinds(core):
        return (
            (32 * core, 32, core, 4 * z + core, z // 2),
            (32 * core + 64, 32, core + 2, 4 * z + core + 2, z // 2),
            (128 + 48 * core, 48, 4 + core, 2 * z + core, z // 4),
            (224 + 48 * core, 48, 6 + core, 16 + 2 * z + core, 2 + z // 4),
        )

    def w1_forward(copy):
        for n, (row, count, index, source, source_x) in enumerate(kinds(c)):
            piece = wb.at[copy, pl.ds(pl.multiple_of(row, 16), count)]

            @pl.when(jnp.logical_not((t == source) & (b == copy)))
            def _():
                arrived(piece, w1_r.at[copy * 8 + index])

            @pl.when(x == source_x)
            def _():
                for k in range(3):
                    send(piece, piece, w1x_s.at[copy, n, k], w1_r.at[copy * 8 + index], line[k])

            send(piece, piece, w1s_s.at[copy, n], w1_r.at[copy * 8 + index], sibling)

    def w1_end(copy):
        for row, count, index, source, source_x in kinds(1 - c):
            piece = wb.at[copy, pl.ds(pl.multiple_of(row, 16), count)]
            arrived(piece, w1_r.at[copy * 8 + index])

    def w1_sent(copy):
        for n, (row, count, index, source, source_x) in enumerate(kinds(c)):
            piece = wb.at[copy, pl.ds(pl.multiple_of(row, 16), count)]

            @pl.when(x == source_x)
            def _():
                for k in range(3):
                    sent(piece, w1x_s.at[copy, n, k])

            sent(piece, w1s_s.at[copy, n])

    def g1_line(k):
        yk = (y + k) % 4
        piece = g1.at[c, x, yk]
        if k == 0:

            @pl.when(b == 0)
            def _():
                arrived(piece, g1y_r.at[yk])
        else:
            arrived(piece, g1y_r.at[yk])
        for n in range(3):
            send(piece, piece, g1x_s.at[k, n], g1x_r.at[x, yk], line[n])

    def g1_core():
        send(g1.at[c, x], g1.at[c, x], g1s_s.at[0], g1s_r.at[x], sibling)
        for k in range(1, 4):
            xk = (x + k) % 4
            for yk in range(4):
                arrived(g1.at[c, xk, yk], g1x_r.at[xk, yk])
            send(g1.at[c, xk], g1.at[c, xk], g1s_s.at[k], g1s_r.at[xk], sibling)

    def g1_end():
        for xk in range(4):
            arrived(g1.at[1 - c, xk], g1s_r.at[xk])

    def g1_sent():
        for yk in range(4):
            for k in range(3):
                sent(g1.at[c, x, yk], g1x_s.at[yk, k])
        for k in range(4):
            sent(g1.at[c, (x + k) % 4], g1s_s.at[k])

    def g0_line():
        for k in range(1, 4):
            yk = (y + k) % 4
            arrived(g0.at[c, x, yk], g0y_r.at[yk])
        for k in range(3):
            send(g0.at[c, x], g0.at[c, x], g0x_s.at[k], g0x_r.at[x], line[k])
        send(g0.at[c, x], g0.at[c, x], g0s_s.at[0], g0s_r.at[x], sibling)

    def g0_core():
        for k in range(1, 4):
            xk = (x + k) % 4
            arrived(g0.at[c, xk], g0x_r.at[xk])
            send(g0.at[c, xk], g0.at[c, xk], g0s_s.at[k], g0s_r.at[xk], sibling)

    def g0_end():
        for xk in range(4):
            arrived(g0.at[1 - c, xk], g0s_r.at[xk])

    def g0_sent():
        for k in range(3):
            sent(g0.at[c, x], g0x_s.at[k])
        for k in range(4):
            sent(g0.at[c, (x + k) % 4], g0s_s.at[k])

    side = 1 - 2 * (z % 2)
    order = [z // 2, (z // 2 + 4 - side) % 4, (z // 2 + 4 + side) % 4, (z // 2 + 2) % 4]

    def pack_query(copy):
        wq_s[...] = jnp.concatenate(
            [wb[copy, 32 * n : 32 * n + 32, :].astype(F32)[0:GP] for n in range(4)], axis=0
        ).astype(BF16)

    def project(copy, s):
        pair = order[s - 1]
        span = pl.ds(pl.multiple_of(128 * pair, 128), 128)
        tokens = gb[copy, span, :]
        kvo[copy, pair] = dot(wb[copy, 128:320, :], tokens, NT).astype(BF16)
        send(kvo.at[copy, pair], kvl.at[copy, pair], h_s.at[copy, 0, s - 1], h_r.at[copy, 0, s - 1], right)
        send(kvo.at[copy, pair], kvr.at[copy, pair], h_s.at[copy, 1, s - 1], h_r.at[copy, 1, s - 1], left)
        q_s[span, :] = dot(tokens, wq_s[...], NT).astype(BF16)

    def halo_end(copy):
        for s in range(4):
            arrived(kvl.at[copy, order[s]], h_r.at[copy, 0, s])
            arrived(kvr.at[copy, order[s]], h_r.at[copy, 1, s])

    def attend(copy):
        for block in range(4):
            first, last = max(block - 1, 0), min(block + 1, 3)
            lanes = (last - first + 1) * 128
            pieces = [ref[copy, n] for ref in (kvl, kvo, kvr) for n in range(first, last + 1)]
            keys = jnp.concatenate([piece[0:HP] for piece in pieces], axis=1)
            values = jnp.concatenate([piece[HP : 2 * HP] for piece in pieces], axis=1)
            scores = dot(q_s[block * 128 : block * 128 + 128, :], keys, NN) * (1.0 / math.sqrt(HD))
            scores = scores + bias[block, :, 0 : 3 * lanes]
            raised = jnp.exp(scores - jnp.max(scores, axis=-1, keepdims=True))
            weights = (raised * (1.0 / jnp.sum(raised, axis=-1, keepdims=True))).astype(BF16)
            ob[copy, block * 128 : block * 128 + 128, 0:HP] = dot(weights, values, NT).astype(BF16)
            for tile in (2 * block, 2 * block + 1):
                piece = ob.at[copy, pl.ds(64 * tile, 64)]
                if copy == 1:

                    @pl.when(z != tile)
                    def _():
                        send(piece, ab.at[z], a_s.at[copy, tile], a_r.at[z], (b, tile, t))
                else:

                    @pl.when((z != tile) | (b == 1))
                    def _():
                        send(piece, ab0.at[b, z], a_s.at[copy, tile], a0_r.at[b, z], (0, tile, t))

    def own_tile(copy):
        return ob[copy, pl.ds(pl.multiple_of(64 * z, 64), 64), :]

    def attended():
        ab[z] = own_tile(1)
        for k in range(1, 8):
            head = (z + k) % 8
            arrived(ab.at[head], a_r.at[head])

    def attended_base():
        ab0[0, z] = own_tile(0)
        for k in range(8):
            head = (z + k) % 8
            if k > 0:
                arrived(ab0.at[0, head], a0_r.at[0, head])
            arrived(ab0.at[1, head], a0_r.at[1, head])

    def attend_sent(copy):
        for s in range(4):
            sent(kvo.at[copy, order[s]], h_s.at[copy, 0, s])
            sent(kvo.at[copy, order[s]], h_s.at[copy, 1, s])
        for tile in range(8):

            @pl.when((z != tile) | ((b == 1) & (copy == 0)))
            def _():
                sent(ob.at[copy, pl.ds(64 * tile, 64)], a_s.at[copy, tile])

    def out_project(copy):
        total = None
        for head in range(8):
            parts = []
            for n in range(4):
                at = (n % 2, head // 2, 2 * (head % 2) + n // 2)
                if copy == 1:
                    parts.append(g1[at].astype(F32)[40:64])
                else:
                    parts.append(g0[at].astype(F32)[0:GP])
            w_head = jnp.concatenate(parts, axis=0).astype(BF16)
            if copy == 1:
                mixed = ab[head][:, 0:HP]
            else:
                mixed = jnp.concatenate([ab0[0, head][:, 0:HP], ab0[1, head][:, 0:HP]], axis=0)
            part = dot(mixed, w_head, NN)
            total = part if total is None else total + part
        return total

    def zero_project(control):
        parts = []
        for pair in range(16):
            two = [g1[core, pair // 4, pair % 4].astype(F32)[0:40] for core in range(2)]
            wide = dot(control, jnp.concatenate(two, axis=0).astype(BF16), NT)
            parts += [wide[:, 0:36], wide[:, 40:76]]
        return jnp.concatenate(parts, axis=1).astype(BF16)

    for load in loads[4:]:
        load.wait()
    for h in range(2):
        part = pl.ds(32 * h, 32)
        arrived(rlat.at[part], lat_r.at[h])
        control_in = lat[b, part, :].astype(F32) + rlat[part, :].astype(F32)
        hid[part, :] = control_in
        gb[1, pl.ds(pl.multiple_of(64 * z + 32 * h, 32), 32), :] = normed(control_in, 1)
        ring_start(1, h)
    w1_forward(1)
    g1_y(True)

    @pl.when(b == 1)
    def _():
        g1_line(0)

    ring_step(1, 2)
    w1_end(1)
    pack_query(1)
    project(1, 1)
    ring_step(1, 3)
    project(1, 2)
    ring_step(1, 4)
    project(1, 3)
    ring_end(1)
    project(1, 4)
    g1_line(1)
    g1_line(2)
    g1_line(3)

    @pl.when(b == 0)
    def _():
        g1_line(0)

    w1_y(0, True)
    halo_end(1)
    attend(1)
    w1_forward(0)
    g1_core()
    g0_y(True)
    attended()
    g1_end()
    control = (hid[...] + mod[2, 1:2, :] * out_project(1)).astype(BF16)

    @pl.when(b == 0)
    def _():
        stage[...] = control
        send(stage, out.at[0], o_s.at[0], o_r.at[0], partner)

    @pl.when(b == 1)
    def _():
        out[1] = control

    residual = zero_project(control)
    base_in = jnp.where(b == 0, lat[b].astype(F32), rlat[...].astype(F32)) + residual.astype(F32)
    hid[...] = base_in
    gb[0, pl.ds(pl.multiple_of(64 * z, 64), 64), :] = normed(base_in, 0)
    ring_start(0, 0)
    ring_start(0, 1)

    @pl.when(b == 1)
    def _():
        res_s[...] = residual
        send(res_s, rres, r_s.at[0], r_r.at[0], partner)

    w1_end(0)
    pack_query(0)
    ring_step(0, 2)
    project(0, 1)
    ring_step(0, 3)
    project(0, 2)
    ring_step(0, 4)
    project(0, 3)
    ring_end(0)
    project(0, 4)

    @pl.when(b == 0)
    def _():
        g0_line()

    halo_end(0)
    attend(0)

    @pl.when(b == 0)
    def _():
        g0_core()
        arrived(rres, r_r.at[0])
        attended_base()
        g0_end()
        second = lat[1].astype(F32) + rres[...].astype(F32)
        gated = mod[2, 0:1, :] * out_project(0)
        out[0] = (hid[...] + gated[0:64]).astype(BF16)
        out[1] = (second + gated[64:128]).astype(BF16)
        sent(stage, o_s.at[0])
        g0_sent()

    @pl.when(b == 1)
    def _():
        arrived(out.at[0], o_r.at[0])
        sent(res_s, r_s.at[0])

    for copy in lat_copies:
        copy.wait_send()
    g1_y(False)
    g0_y(False)
    g1_sent()
    for copy in (1, 0):
        w1_y(copy, False)
        w1_sent(copy)
        ring_sent(copy)
        attend_sent(copy)


def on_device(latent, modulation, w_query, w_keyval, w_out, w_zero):
    dma = pltpu.SemaphoreType.DMA
    vmem = pltpu.VMEM
    result = pl.pallas_call(
        kernel,
        out_shape=jax.ShapeDtypeStruct((2, 64, D), BF16),
        in_specs=[pl.BlockSpec(memory_space=pl.ANY)] * 6,
        out_specs=pl.BlockSpec(memory_space=pltpu.VMEM),
        scratch_shapes=[
            vmem((2, 64, D), BF16),
            vmem((3, 2, D), F32),
            vmem((18, D), BF16),
            vmem((36, D), BF16),
            vmem((18, D), BF16),
            vmem((36, D), BF16),
            vmem((2, 320, D), BF16),
            vmem((2, 4, 4, 64, D), BF16),
            vmem((2, 4, 4, 32, D), BF16),
            vmem((2, 512, D), BF16),
            vmem((2, 4, 2 * HP, 128), BF16),
            vmem((2, 4, 2 * HP, 128), BF16),
            vmem((2, 4, 2 * HP, 128), BF16),
            vmem((2, 512, 128), BF16),
            vmem((8, 64, 128), BF16),
            vmem((2, 8, 64, 128), BF16),
            vmem((4, 128, D), F32),
            vmem((64, D), F32),
            vmem((64, D), BF16),
            vmem((64, D), BF16),
            vmem((64, D), BF16),
            vmem((64, D), BF16),
            vmem((512, HP), BF16),
            vmem((HP, D), BF16),
            dma((6,)), dma((2,)), dma((2,)),
            dma((2, 7)), dma((2, 4, 3)), dma((2, 4)), dma((16,)),
            dma((7,)), dma((4, 3)), dma((4,)), dma((4,)), dma((4, 4)), dma((4,)),
            dma((3,)), dma((3,)), dma((4,)), dma((4,)), dma((4,)), dma((4,)),
            dma((2, 2, 4, 2)), dma((2, 2, 4, 2)), dma((2, 2, 4)), dma((2, 2, 4)),
            dma((2, 8)), dma((8,)), dma((2, 8)), dma((1,)), dma((1,)), dma((1,)), dma((1,)),
        ],
        compiler_params=pltpu.CompilerParams(
            collective_id=0, has_side_effects=True, vmem_limit_bytes=56 * 1024 * 1024
        ),
    )(
        latent.reshape(2, 64, D), modulation.swapaxes(0, 1), w_query[0].T, w_keyval[0].T, w_out[0], w_zero.T,
    )
    return result.reshape(latent.shape)


def solution(mesh):
    placed = (
        P("branch", None, "trow", "tcol", None),
        P(),
        P("branch", None, "tcol"),
        P("branch", None, "tcol"),
        P("branch", "tcol", None),
        P(None, "tcol"),
    )
    return jax.shard_map(
        on_device,
        mesh=mesh,
        in_specs=placed,
        out_specs=P("branch", None, "trow", "tcol", None),
        check_vma=False,
    )
```

```python
import math

import jax
import jax.numpy as jnp
from jax import lax
from jax.experimental import pallas as pl
from jax.experimental.pallas import tpu as pltpu
from jax.sharding import PartitionSpec as P

MESH = pl.DeviceIdType.MESH
F32 = jnp.float32
BF16 = jnp.bfloat16
D = 1152
HD = 72
GP = 24
HP = 96
NEG = -1e30
NT = (((1,), (1,)), ((), ()))
NN = (((1,), (0,)), ((), ()))


def dot(a, b, dims):
    return lax.dot_general(a, b, dims, preferred_element_type=F32)


def pick(rows, cols, pieces):
    r = lax.broadcasted_iota(jnp.int32, (rows, cols), 0)
    c = lax.broadcasted_iota(jnp.int32, (rows, cols), 1)
    hit = None
    for row0, col0, count in pieces:
        one = (r - row0 == c - col0) & (r >= row0) & (r < row0 + count)
        hit = one if hit is None else hit | one
    return jnp.where(hit, 1.0, 0.0).astype(BF16)


def kernel(
    lat_h, mod_h, wq_h, wkv_h, wo_h, wz_h, out,
    lat, mod, wq, wkv, wo, wz,
    wb, g1, g0, gb, kvo, kvl, kvr, ob, ab, ab0, bias, hid, rlat, rres, stage, res_s, q_s, wq_s,
    in_s, lat_s, lat_r, w1y_s, w1t_s, w1x_s, w1s_s, w1_r, g1y_s, g1x_s, g1s_s, g1y_r, g1x_r, g1s_r,
    g0y_s, g0x_s, g0s_s, g0y_r, g0x_r, g0s_r, z_s, z_r, h_s, h_r, a_s, a_r, a0_r, o_s, o_r, r_s, r_r,
):
    b = lax.axis_index("branch")
    z = lax.axis_index("trow")
    t = lax.axis_index("tcol")
    x, y, c = t // 8, (t // 2) % 4, t % 2
    yy = b * 4 + y
    partner = (1 - b, z, t)
    sibling = (b, z, t + 1 - 2 * c)
    left = (b, z, (t + 31) % 32)
    right = (b, z, (t + 1) % 32)
    column = []
    for k in range(1, 8):
        other = (yy + k) % 8
        column.append((other // 4, z, x * 8 + (other % 4) * 2 + c))
    line = [(b, z, ((x + k) % 4) * 8 + y * 2 + c) for k in range(1, 4)]
    ring = [(b, (z + k) % 8, t) for k in range(1, 8)]
    far = jnp.where(c == 0, (t + 31) % 32, (t + 1) % 32)

    def send(src, dst, ss, rs, dev):
        copy = pltpu.make_async_remote_copy(
            src_ref=src, dst_ref=dst, send_sem=ss, recv_sem=rs, device_id=dev, device_id_type=MESH
        )
        copy.start()
        return copy

    def arrived(dst, rs):
        pltpu.make_async_remote_copy(
            src_ref=dst, dst_ref=dst, send_sem=lat_s.at[0], recv_sem=rs, device_id=partner, device_id_type=MESH
        ).wait_recv()

    def sent(src, ss):
        pltpu.make_async_remote_copy(
            src_ref=src, dst_ref=src, send_sem=ss, recv_sem=lat_r.at[0], device_id=partner, device_id_type=MESH
        ).wait_send()

    barrier = pltpu.get_barrier_semaphore()
    across = [(1 - b, (z + k) % 8, t) for k in range(1, 8)]
    peers = column + line + ring + across + [sibling, (b, z, far)]
    for dev in peers:
        pl.semaphore_signal(barrier, inc=1, device_id=dev, device_id_type=MESH)

    loads = [
        pltpu.make_async_copy(src, dst, in_s.at[n])
        for n, (src, dst) in enumerate(
            ((wq_h, wq), (wkv_h, wkv), (wo_h, wo), (wz_h, wz), (lat_h, lat), (mod_h, mod))
        )
    ]
    for load in loads:
        load.start()
    for load in loads[:4]:
        load.wait()

    rows = (
        dot(pick(144, 18, [(0, 0, 18)]), wq[...], NN)
        + dot(pick(144, 36, [(32, 0, 18), (56, 18, 18)]), wkv[...], NN)
        + dot(pick(144, 36, [(80, 0, 36)]), wz[...], NN)
        + dot(pick(144, 18, [(120, 0, 18)]), wo[...], NN)
    ).astype(BF16)
    own_q, own_kv = t // 4 == z, (t // 2) % 8 == z
    q_row = pl.multiple_of(32 * (t % 4), 16)
    kv_row = pl.multiple_of(128 + 96 * (t // 16) + 48 * c, 16)
    kv_idx = 4 + 2 * (t // 16) + c

    @pl.when(own_q)
    def _():
        wb[b, pl.ds(q_row, 32), :] = rows[0:32]

    @pl.when(own_kv)
    def _():
        wb[b, pl.ds(kv_row, 48), :] = rows[32:80]

    @pl.when(b == 1)
    def _():
        g1[c, x, y] = rows[80:144]

    @pl.when(b == 0)
    def _():
        g0[c, x, y] = jnp.concatenate(
            [rows[120:144].astype(F32), jnp.zeros((8, D), F32)], axis=0
        ).astype(BF16)

    pl.semaphore_wait(barrier, len(peers))

    def lat_half(h):
        return send(
            lat_h.at[1 - b, pl.ds(32 * h, 32)], rlat.at[pl.ds(32 * h, 32)], lat_s.at[h], lat_r.at[h], partner
        )

    lat_copies = [lat_half(0), lat_half(1)]

    def w1_y(copy, start):
        @pl.when(own_q & (b == copy))
        def _():
            piece = wb.at[copy, pl.ds(q_row, 32)]
            for n, k in enumerate((2, 6, 1, 7)):
                if start:
                    send(piece, piece, w1y_s.at[0, n], w1_r.at[copy * 8 + t % 4], column[k - 1])
                else:
                    sent(piece, w1y_s.at[0, n])

        @pl.when(own_kv & (b == copy))
        def _():
            piece = wb.at[copy, pl.ds(kv_row, 48)]
            for n, k in enumerate((2, 6, 1, 7)):
                if start:
                    send(piece, piece, w1y_s.at[1, n], w1_r.at[copy * 8 + kv_idx], column[k - 1])
                else:
                    sent(piece, w1y_s.at[1, n])

    def g0_y(start):
        @pl.when(b == 0)
        def _():
            piece = g0.at[c, x, y]
            for k in range(1, 4):
                if start:
                    send(piece, piece, g0y_s.at[k - 1], g0y_r.at[y], (b, z, x * 8 + ((y + k) % 4) * 2 + c))
                else:
                    sent(piece, g0y_s.at[k - 1])

    w1_y(1, True)

    for block in range(4):
        first, last = max(block - 1, 0), min(block + 1, 3)
        lanes = (last - first + 1) * 128
        q = lax.broadcasted_iota(jnp.int32, (128, lanes), 0)
        k = lax.broadcasted_iota(jnp.int32, (128, lanes), 1)
        i, j = block * 16 + q // 8, t * 8 + q % 8
        row, col = first * 16 + k // 8, (t - 1) * 8 + k % 8
        row0, col0 = jnp.clip(i - 6, 0, 51), jnp.clip(j - 6, 0, 243)
        row_ok = (row >= row0) & (row < row0 + 13)
        for strip in range(3):
            here = col + 8 * strip
            ok = row_ok & (here >= col0) & (here < col0 + 13)
            bias[block, :, strip * lanes : (strip + 1) * lanes] = jnp.where(ok, 0.0, NEG)
    ob[...] = jnp.zeros_like(ob)

    def normed(hidden, copy):
        average = jnp.mean(hidden, axis=-1, keepdims=True)
        centred = hidden - average
        variance = jnp.mean(centred * centred, axis=-1, keepdims=True)
        shift, scale = mod[0, copy : copy + 1, :], mod[1, copy : copy + 1, :]
        return (centred * lax.rsqrt(variance + 1e-06) * (1.0 + scale) + shift).astype(BF16)

    def half_tile(copy, index, h):
        start = 64 * ((index + 8) % 8) + 32 * h
        return gb.at[copy, pl.ds(pl.multiple_of(start, 32), 32)]

    def ring_send(copy, s, way, h):
        tile = half_tile(copy, z - s + 1 if way == 0 else z + s - 1, h)
        send(tile, tile, z_s.at[copy, way, s - 1, h], z_r.at[copy, way, s - 1, h], ring[0] if way == 0 else ring[6])

    def ring_take(copy, s, way, h):
        arrived(half_tile(copy, z - s if way == 0 else z + s, h), z_r.at[copy, way, s - 1, h])

    def ring_start(copy, h):
        ring_send(copy, 1, 0, h)
        ring_send(copy, 1, 1, h)

    def ring_step(copy, s):
        for h in range(2):
            for way in range(2):
                ring_take(copy, s - 1, way, h)
                if s < 4 or h == way:
                    ring_send(copy, s, way, h)

    def ring_end(copy):
        ring_take(copy, 4, 0, 0)
        ring_take(copy, 4, 1, 1)

    def ring_sent(copy):
        for s in range(1, 5):
            for h in range(2):
                for way in range(2):
                    if s < 4 or h == way:
                        sent(half_tile(copy, z, h), z_s.at[copy, way, s - 1, h])

    def kinds(core):
        return (
            (32 * core, 32, core, 4 * z + core, z // 2),
            (32 * core + 64, 32, core + 2, 4 * z + core + 2, z // 2),
            (128 + 48 * core, 48, 4 + core, 2 * z + core, z // 4),
            (224 + 48 * core, 48, 6 + core, 16 + 2 * z + core, 2 + z // 4),
        )

    def w1_tree(copy, start):
        for n, (row, count, index, source, source_x) in enumerate(kinds(c)):
            piece = wb.at[copy, pl.ds(pl.multiple_of(row, 16), count)]
            away = (yy + 8 - (copy * 4 + (source // 2) % 4)) % 8
            for here, steps in ((2, (2, 1)), (6, (7,))):

                @pl.when((x == source_x) & (away == here))
                def _():
                    if start:
                        arrived(piece, w1_r.at[copy * 8 + index])
                    for m, k in enumerate(steps):
                        if start:
                            send(piece, piece, w1t_s.at[copy, n, m], w1_r.at[copy * 8 + index], column[k - 1])
                        else:
                            sent(piece, w1t_s.at[copy, n, m])

    def w1_line(copy):
        for n, (row, count, index, source, source_x) in enumerate(kinds(c)):
            piece = wb.at[copy, pl.ds(pl.multiple_of(row, 16), count)]
            away = (yy + 8 - (copy * 4 + (source // 2) % 4)) % 8

            @pl.when(x == source_x)
            def _():
                @pl.when((away != 0) & (away != 2) & (away != 6))
                def _():
                    arrived(piece, w1_r.at[copy * 8 + index])

                for k in range(3):
                    send(piece, piece, w1x_s.at[copy, n, k], w1_r.at[copy * 8 + index], line[k])
                send(piece, piece, w1s_s.at[copy, n], w1_r.at[copy * 8 + index], sibling)

    def w1_core(copy):
        for n, (row, count, index, source, source_x) in enumerate(kinds(c)):
            piece = wb.at[copy, pl.ds(pl.multiple_of(row, 16), count)]

            @pl.when(x != source_x)
            def _():
                arrived(piece, w1_r.at[copy * 8 + index])
                send(piece, piece, w1s_s.at[copy, n], w1_r.at[copy * 8 + index], sibling)

    def w1_end(copy):
        for row, count, index, source, source_x in kinds(1 - c):
            piece = wb.at[copy, pl.ds(pl.multiple_of(row, 16), count)]
            arrived(piece, w1_r.at[copy * 8 + index])

    def w1_sent(copy):
        for n, (row, count, index, source, source_x) in enumerate(kinds(c)):
            piece = wb.at[copy, pl.ds(pl.multiple_of(row, 16), count)]

            @pl.when(x == source_x)
            def _():
                for k in range(3):
                    sent(piece, w1x_s.at[copy, n, k])

            sent(piece, w1s_s.at[copy, n])

    def g1_line(yk):
        for n in range(3):
            send(g1.at[c, x, yk], g1.at[c, x, yk], g1x_s.at[yk, n], g1x_r.at[x, yk], line[n])

    def g1_send(s, way):
        at = (yy + 9 - s if way == 0 else yy + s - 1) % 8
        piece = g1.at[c, x, at % 4]

        @pl.when(at >= 4)
        def _():
            send(piece, piece, g1y_s.at[way, s - 1], g1y_r.at[at % 4], column[0 if way == 0 else 6])

    def g1_take(s, way):
        at = (yy + 8 - s if way == 0 else yy + s) % 8

        @pl.when(at >= 4)
        def _():
            arrived(g1.at[c, x, at % 4], g1y_r.at[at % 4])
            if s < (4 if way == 0 else 3):
                g1_pass(s + 1, way)
            g1_line(at % 4)

    def g1_pass(s, way):
        at = (yy + 9 - s if way == 0 else yy + s - 1) % 8
        piece = g1.at[c, x, at % 4]
        send(piece, piece, g1y_s.at[way, s - 1], g1y_r.at[at % 4], column[0 if way == 0 else 6])

    def g1_y_sent():
        for way in range(2):
            for s in range(1, 5 - way):
                at = (yy + 9 - s if way == 0 else yy + s - 1) % 8

                @pl.when(at >= 4)
                def _():
                    sent(g1.at[c, x, at % 4], g1y_s.at[way, s - 1])

    def g1_core():
        send(g1.at[c, x], g1.at[c, x], g1s_s.at[0], g1s_r.at[x], sibling)
        for k in range(1, 4):
            xk = (x + k) % 4
            for yk in range(4):
                arrived(g1.at[c, xk, yk], g1x_r.at[xk, yk])
            send(g1.at[c, xk], g1.at[c, xk], g1s_s.at[k], g1s_r.at[xk], sibling)

    def g1_end():
        for xk in range(4):
            arrived(g1.at[1 - c, xk], g1s_r.at[xk])

    def g1_sent():
        for yk in range(4):
            for k in range(3):
                sent(g1.at[c, x, yk], g1x_s.at[yk, k])
        for k in range(4):
            sent(g1.at[c, (x + k) % 4], g1s_s.at[k])

    def g0_line():
        for k in range(1, 4):
            yk = (y + k) % 4
            arrived(g0.at[c, x, yk], g0y_r.at[yk])
        for k in range(3):
            send(g0.at[c, x], g0.at[c, x], g0x_s.at[k], g0x_r.at[x], line[k])
        send(g0.at[c, x], g0.at[c, x], g0s_s.at[0], g0s_r.at[x], sibling)

    def g0_core():
        for k in range(1, 4):
            xk = (x + k) % 4
            arrived(g0.at[c, xk], g0x_r.at[xk])
            send(g0.at[c, xk], g0.at[c, xk], g0s_s.at[k], g0s_r.at[xk], sibling)

    def g0_end():
        for xk in range(4):
            arrived(g0.at[1 - c, xk], g0s_r.at[xk])

    def g0_sent():
        for k in range(3):
            sent(g0.at[c, x], g0x_s.at[k])
        for k in range(4):
            sent(g0.at[c, (x + k) % 4], g0s_s.at[k])

    side = 1 - 2 * (z % 2)
    order = [z // 2, (z // 2 + 4 - side) % 4, (z // 2 + 4 + side) % 4, (z // 2 + 2) % 4]

    def pack_query(copy):
        wq_s[...] = jnp.concatenate(
            [wb[copy, 32 * n : 32 * n + 32, :].astype(F32)[0:GP] for n in range(4)], axis=0
        ).astype(BF16)

    def project(copy, s):
        pair = order[s - 1]
        span = pl.ds(pl.multiple_of(128 * pair, 128), 128)
        tokens = gb[copy, span, :]
        kvo[copy, pair] = dot(wb[copy, 128:320, :], tokens, NT).astype(BF16)
        send(kvo.at[copy, pair], kvl.at[copy, pair], h_s.at[copy, 0, s - 1], h_r.at[copy, 0, s - 1], right)
        send(kvo.at[copy, pair], kvr.at[copy, pair], h_s.at[copy, 1, s - 1], h_r.at[copy, 1, s - 1], left)
        q_s[span, :] = dot(tokens, wq_s[...], NT).astype(BF16)

    def halo_end(copy):
        for s in range(4):
            arrived(kvl.at[copy, order[s]], h_r.at[copy, 0, s])
            arrived(kvr.at[copy, order[s]], h_r.at[copy, 1, s])

    def attend(copy):
        for block in range(4):
            first, last = max(block - 1, 0), min(block + 1, 3)
            lanes = (last - first + 1) * 128
            pieces = [ref[copy, n] for ref in (kvl, kvo, kvr) for n in range(first, last + 1)]
            keys = jnp.concatenate([piece[0:HP] for piece in pieces], axis=1)
            values = jnp.concatenate([piece[HP : 2 * HP] for piece in pieces], axis=1)
            scores = dot(q_s[block * 128 : block * 128 + 128, :], keys, NN) * (1.0 / math.sqrt(HD))
            scores = scores + bias[block, :, 0 : 3 * lanes]
            raised = jnp.exp(scores - jnp.max(scores, axis=-1, keepdims=True))
            weights = (raised * (1.0 / jnp.sum(raised, axis=-1, keepdims=True))).astype(BF16)
            ob[copy, block * 128 : block * 128 + 128, 0:HP] = dot(weights, values, NT).astype(BF16)
            for tile in (2 * block, 2 * block + 1):
                piece = ob.at[copy, pl.ds(64 * tile, 64)]
                if copy == 1:

                    @pl.when(z != tile)
                    def _():
                        send(piece, ab.at[z], a_s.at[copy, tile], a_r.at[z], (b, tile, t))
                else:

                    @pl.when((z != tile) | (b == 1))
                    def _():
                        send(piece, ab0.at[b, z], a_s.at[copy, tile], a0_r.at[b, z], (0, tile, t))

    def own_tile(copy):
        return ob[copy, pl.ds(pl.multiple_of(64 * z, 64), 64), :]

    def attended():
        ab[z] = own_tile(1)
        for k in range(1, 8):
            head = (z + k) % 8
            arrived(ab.at[head], a_r.at[head])

    def attended_base():
        ab0[0, z] = own_tile(0)
        for k in range(8):
            head = (z + k) % 8
            if k > 0:
                arrived(ab0.at[0, head], a0_r.at[0, head])
            arrived(ab0.at[1, head], a0_r.at[1, head])

    def attend_sent(copy):
        for s in range(4):
            sent(kvo.at[copy, order[s]], h_s.at[copy, 0, s])
            sent(kvo.at[copy, order[s]], h_s.at[copy, 1, s])
        for tile in range(8):

            @pl.when((z != tile) | ((b == 1) & (copy == 0)))
            def _():
                sent(ob.at[copy, pl.ds(64 * tile, 64)], a_s.at[copy, tile])

    def out_project(copy):
        total = None
        for head in range(8):
            parts = []
            for n in range(4):
                at = (n % 2, head // 2, 2 * (head % 2) + n // 2)
                if copy == 1:
                    parts.append(g1[at].astype(F32)[40:64])
                else:
                    parts.append(g0[at].astype(F32)[0:GP])
            w_head = jnp.concatenate(parts, axis=0).astype(BF16)
            if copy == 1:
                mixed = ab[head][:, 0:HP]
            else:
                mixed = jnp.concatenate([ab0[0, head][:, 0:HP], ab0[1, head][:, 0:HP]], axis=0)
            part = dot(mixed, w_head, NN)
            total = part if total is None else total + part
        return total

    def zero_project(control):
        parts = []
        for pair in range(16):
            two = [g1[core, pair // 4, pair % 4].astype(F32)[0:40] for core in range(2)]
            wide = dot(control, jnp.concatenate(two, axis=0).astype(BF16), NT)
            parts += [wide[:, 0:36], wide[:, 40:76]]
        return jnp.concatenate(parts, axis=1).astype(BF16)

    for load in loads[4:]:
        load.wait()
    for h in range(2):
        part = pl.ds(32 * h, 32)
        arrived(rlat.at[part], lat_r.at[h])
        control_in = lat[b, part, :].astype(F32) + rlat[part, :].astype(F32)
        hid[part, :] = control_in
        gb[1, pl.ds(pl.multiple_of(64 * z + 32 * h, 32), 32), :] = normed(control_in, 1)
        ring_start(1, h)

    w1_tree(1, True)
    g1_send(1, 0)
    g1_send(1, 1)

    @pl.when(b == 1)
    def _():
        g1_line(y)

    ring_step(1, 2)
    w1_line(1)
    g1_take(1, 0)
    g1_take(1, 1)
    ring_step(1, 3)
    g1_take(2, 0)
    g1_take(2, 1)
    ring_step(1, 4)
    ring_end(1)
    w1_core(1)
    w1_end(1)
    pack_query(1)
    for s in range(1, 5):
        project(1, s)
    g1_take(3, 0)
    g1_take(3, 1)
    w1_y(0, True)
    halo_end(1)
    attend(1)
    g1_take(4, 0)
    w1_tree(0, True)
    g1_core()
    g0_y(True)
    attended()
    g1_end()
    control = (hid[...] + mod[2, 1:2, :] * out_project(1)).astype(BF16)

    @pl.when(b == 0)
    def _():
        stage[...] = control
        send(stage, out.at[0], o_s.at[0], o_r.at[0], partner)

    @pl.when(b == 1)
    def _():
        out[1] = control

    residual = zero_project(control)
    base_in = jnp.where(b == 0, lat[b].astype(F32), rlat[...].astype(F32)) + residual.astype(F32)
    hid[...] = base_in
    gb[0, pl.ds(pl.multiple_of(64 * z, 64), 64), :] = normed(base_in, 0)
    ring_start(0, 0)
    ring_start(0, 1)
    w1_line(0)

    @pl.when(b == 1)
    def _():
        res_s[...] = residual
        send(res_s, rres, r_s.at[0], r_r.at[0], partner)

    ring_step(0, 2)
    w1_core(0)
    w1_end(0)
    pack_query(0)
    project(0, 1)
    ring_step(0, 3)
    project(0, 2)
    ring_step(0, 4)
    project(0, 3)
    ring_end(0)
    project(0, 4)

    @pl.when(b == 0)
    def _():
        g0_line()

    halo_end(0)
    attend(0)

    @pl.when(b == 0)
    def _():
        g0_core()
        arrived(rres, r_r.at[0])
        attended_base()
        g0_end()
        second = lat[1].astype(F32) + rres[...].astype(F32)
        gated = mod[2, 0:1, :] * out_project(0)
        out[0] = (hid[...] + gated[0:64]).astype(BF16)
        out[1] = (second + gated[64:128]).astype(BF16)
        sent(stage, o_s.at[0])
        g0_sent()

    @pl.when(b == 1)
    def _():
        arrived(out.at[0], o_r.at[0])
        sent(res_s, r_s.at[0])

    for copy in lat_copies:
        copy.wait_send()
    g1_y_sent()
    g0_y(False)
    g1_sent()
    for copy in (1, 0):
        w1_y(copy, False)
        w1_tree(copy, False)
        w1_sent(copy)
        ring_sent(copy)
        attend_sent(copy)


def on_device(latent, modulation, w_query, w_keyval, w_out, w_zero):
    dma = pltpu.SemaphoreType.DMA
    vmem = pltpu.VMEM
    result = pl.pallas_call(
        kernel,
        out_shape=jax.ShapeDtypeStruct((2, 64, D), BF16),
        in_specs=[pl.BlockSpec(memory_space=pl.ANY)] * 6,
        out_specs=pl.BlockSpec(memory_space=pltpu.VMEM),
        scratch_shapes=[
            vmem((2, 64, D), BF16),
            vmem((3, 2, D), F32),
            vmem((18, D), BF16),
            vmem((36, D), BF16),
            vmem((18, D), BF16),
            vmem((36, D), BF16),
            vmem((2, 320, D), BF16),
            vmem((2, 4, 4, 64, D), BF16),
            vmem((2, 4, 4, 32, D), BF16),
            vmem((2, 512, D), BF16),
            vmem((2, 4, 2 * HP, 128), BF16),
            vmem((2, 4, 2 * HP, 128), BF16),
            vmem((2, 4, 2 * HP, 128), BF16),
            vmem((2, 512, 128), BF16),
            vmem((8, 64, 128), BF16),
            vmem((2, 8, 64, 128), BF16),
            vmem((4, 128, D), F32),
            vmem((64, D), F32),
            vmem((64, D), BF16),
            vmem((64, D), BF16),
            vmem((64, D), BF16),
            vmem((64, D), BF16),
            vmem((512, HP), BF16),
            vmem((HP, D), BF16),
            dma((6,)), dma((2,)), dma((2,)),
            dma((2, 4)), dma((2, 4, 2)), dma((2, 4, 3)), dma((2, 4)), dma((16,)),
            dma((2, 4)), dma((4, 3)), dma((4,)), dma((4,)), dma((4, 4)), dma((4,)),
            dma((3,)), dma((3,)), dma((4,)), dma((4,)), dma((4,)), dma((4,)),
            dma((2, 2, 4, 2)), dma((2, 2, 4, 2)), dma((2, 2, 4)), dma((2, 2, 4)),
            dma((2, 8)), dma((8,)), dma((2, 8)), dma((1,)), dma((1,)), dma((1,)), dma((1,)),
        ],
        compiler_params=pltpu.CompilerParams(
            collective_id=0, has_side_effects=True, vmem_limit_bytes=56 * 1024 * 1024
        ),
    )(
        latent.reshape(2, 64, D), modulation.swapaxes(0, 1), w_query[0].T, w_keyval[0].T, w_out[0], w_zero.T,
    )
    return result.reshape(latent.shape)


def solution(mesh):
    placed = (
        P("branch", None, "trow", "tcol", None),
        P(),
        P("branch", None, "tcol"),
        P("branch", None, "tcol"),
        P("branch", "tcol", None),
        P(None, "tcol"),
    )
    return jax.shard_map(
        on_device,
        mesh=mesh,
        in_specs=placed,
        out_specs=P("branch", None, "trow", "tcol", None),
        check_vma=False,
    )
```

```python
import math

import jax
import jax.numpy as jnp
from jax import lax
from jax.experimental import pallas as pl
from jax.experimental.pallas import tpu as pltpu
from jax.sharding import PartitionSpec as P

MESH = pl.DeviceIdType.MESH
F32 = jnp.float32
BF16 = jnp.bfloat16
D = 1152
HD = 72
GP = 24
HP = 96
NEG = -1e30
NT = (((1,), (1,)), ((), ()))
NN = (((1,), (0,)), ((), ()))


def dot(a, b, dims):
    return lax.dot_general(a, b, dims, preferred_element_type=F32)


def pick(rows, cols, pieces):
    r = lax.broadcasted_iota(jnp.int32, (rows, cols), 0)
    c = lax.broadcasted_iota(jnp.int32, (rows, cols), 1)
    hit = None
    for row0, col0, count in pieces:
        one = (r - row0 == c - col0) & (r >= row0) & (r < row0 + count)
        hit = one if hit is None else hit | one
    return jnp.where(hit, 1.0, 0.0).astype(BF16)


def kernel(
    lat_h, mod_h, wq_h, wkv_h, wo_h, wz_h, out,
    lat, mod, wq, wkv, wo, wz,
    wb, g1, g0, gb, kvo, kvl, kvr, ob, ab, ab0, bias, hid, rlat, rres, stage, res_s, q_s, wq_s,
    in_s, lat_s, lat_r, w1y_s, w1t_s, w1x_s, w1s_s, w1_r, g1y_s, g1x_s, g1s_s, g1y_r, g1x_r, g1s_r, g1o_s, g1o_r,
    g0y_s, g0x_s, g0s_s, g0y_r, g0x_r, g0s_r, z_s, z_r, h_s, h_r, a_s, a_r, a0_r, o_s, o_r, r_s, r_r,
):
    b = lax.axis_index("branch")
    z = lax.axis_index("trow")
    t = lax.axis_index("tcol")
    x, y, c = t // 8, (t // 2) % 4, t % 2
    yy = b * 4 + y
    partner = (1 - b, z, t)
    sibling = (b, z, t + 1 - 2 * c)
    left = (b, z, (t + 31) % 32)
    right = (b, z, (t + 1) % 32)
    column = []
    for k in range(1, 8):
        other = (yy + k) % 8
        column.append((other // 4, z, x * 8 + (other % 4) * 2 + c))
    line = [(b, z, ((x + k) % 4) * 8 + y * 2 + c) for k in range(1, 4)]
    ring = [(b, (z + k) % 8, t) for k in range(1, 8)]
    far = jnp.where(c == 0, (t + 31) % 32, (t + 1) % 32)

    def send(src, dst, ss, rs, dev):
        copy = pltpu.make_async_remote_copy(
            src_ref=src, dst_ref=dst, send_sem=ss, recv_sem=rs, device_id=dev, device_id_type=MESH
        )
        copy.start()
        return copy

    def arrived(dst, rs):
        pltpu.make_async_remote_copy(
            src_ref=dst, dst_ref=dst, send_sem=lat_s.at[0], recv_sem=rs, device_id=partner, device_id_type=MESH
        ).wait_recv()

    def sent(src, ss):
        pltpu.make_async_remote_copy(
            src_ref=src, dst_ref=src, send_sem=ss, recv_sem=lat_r.at[0], device_id=partner, device_id_type=MESH
        ).wait_send()

    barrier = pltpu.get_barrier_semaphore()
    across = [(1 - b, (z + k) % 8, t) for k in range(1, 8)]
    peers = column + line + ring + across + [sibling, (b, z, far)]
    for dev in peers:
        pl.semaphore_signal(barrier, inc=1, device_id=dev, device_id_type=MESH)

    loads = [
        pltpu.make_async_copy(src, dst, in_s.at[n])
        for n, (src, dst) in enumerate(
            ((wq_h, wq), (wkv_h, wkv), (wo_h, wo), (wz_h, wz), (lat_h, lat), (mod_h, mod))
        )
    ]
    for load in loads:
        load.start()
    for load in loads[:4]:
        load.wait()

    rows = (
        dot(pick(144, 18, [(0, 0, 18)]), wq[...], NN)
        + dot(pick(144, 36, [(32, 0, 18), (56, 18, 18)]), wkv[...], NN)
        + dot(pick(144, 36, [(80, 0, 36)]), wz[...], NN)
        + dot(pick(144, 18, [(120, 0, 18)]), wo[...], NN)
    ).astype(BF16)
    own_q, own_kv = t // 4 == z, (t // 2) % 8 == z
    q_row = pl.multiple_of(32 * (t % 4), 16)
    kv_row = pl.multiple_of(128 + 96 * (t // 16) + 48 * c, 16)
    kv_idx = 4 + 2 * (t // 16) + c

    @pl.when(own_q)
    def _():
        wb[b, pl.ds(q_row, 32), :] = rows[0:32]

    @pl.when(own_kv)
    def _():
        wb[b, pl.ds(kv_row, 48), :] = rows[32:80]

    @pl.when(b == 1)
    def _():
        g1[c, x, y] = rows[80:144]

    @pl.when(b == 0)
    def _():
        g0[c, x, y] = jnp.concatenate(
            [rows[120:144].astype(F32), jnp.zeros((8, D), F32)], axis=0
        ).astype(BF16)

    pl.semaphore_wait(barrier, len(peers))

    def lat_half(h):
        return send(
            lat_h.at[1 - b, pl.ds(32 * h, 32)], rlat.at[pl.ds(32 * h, 32)], lat_s.at[h], lat_r.at[h], partner
        )

    lat_copies = [lat_half(0), lat_half(1)]

    def w1_y(copy, start):
        @pl.when(own_q & (b == copy))
        def _():
            piece = wb.at[copy, pl.ds(q_row, 32)]
            for n, k in enumerate((2, 6, 1, 7)):
                if start:
                    send(piece, piece, w1y_s.at[0, n], w1_r.at[copy * 8 + t % 4], column[k - 1])
                else:
                    sent(piece, w1y_s.at[0, n])

        @pl.when(own_kv & (b == copy))
        def _():
            piece = wb.at[copy, pl.ds(kv_row, 48)]
            for n, k in enumerate((2, 6, 1, 7)):
                if start:
                    send(piece, piece, w1y_s.at[1, n], w1_r.at[copy * 8 + kv_idx], column[k - 1])
                else:
                    sent(piece, w1y_s.at[1, n])

    def g0_y(start):
        @pl.when(b == 0)
        def _():
            piece = g0.at[c, x, y]
            for k in range(1, 4):
                if start:
                    send(piece, piece, g0y_s.at[k - 1], g0y_r.at[y], (b, z, x * 8 + ((y + k) % 4) * 2 + c))
                else:
                    sent(piece, g0y_s.at[k - 1])

    w1_y(1, True)

    for block in range(4):
        first, last = max(block - 1, 0), min(block + 1, 3)
        lanes = (last - first + 1) * 128
        q = lax.broadcasted_iota(jnp.int32, (128, lanes), 0)
        k = lax.broadcasted_iota(jnp.int32, (128, lanes), 1)
        i, j = block * 16 + q // 8, t * 8 + q % 8
        row, col = first * 16 + k // 8, (t - 1) * 8 + k % 8
        row0, col0 = jnp.clip(i - 6, 0, 51), jnp.clip(j - 6, 0, 243)
        row_ok = (row >= row0) & (row < row0 + 13)
        for strip in range(3):
            here = col + 8 * strip
            ok = row_ok & (here >= col0) & (here < col0 + 13)
            bias[block, :, strip * lanes : (strip + 1) * lanes] = jnp.where(ok, 0.0, NEG)
    ob[...] = jnp.zeros_like(ob)

    def normed(hidden, copy):
        average = jnp.mean(hidden, axis=-1, keepdims=True)
        centred = hidden - average
        variance = jnp.mean(centred * centred, axis=-1, keepdims=True)
        shift, scale = mod[0, copy : copy + 1, :], mod[1, copy : copy + 1, :]
        return (centred * lax.rsqrt(variance + 1e-06) * (1.0 + scale) + shift).astype(BF16)

    def half_tile(copy, index, h):
        start = 64 * ((index + 8) % 8) + 32 * h
        return gb.at[copy, pl.ds(pl.multiple_of(start, 32), 32)]

    def ring_send(copy, s, way, h):
        tile = half_tile(copy, z - s + 1 if way == 0 else z + s - 1, h)
        send(tile, tile, z_s.at[copy, way, s - 1, h], z_r.at[copy, way, s - 1, h], ring[0] if way == 0 else ring[6])

    def ring_take(copy, s, way, h):
        arrived(half_tile(copy, z - s if way == 0 else z + s, h), z_r.at[copy, way, s - 1, h])

    def ring_start(copy, h):
        ring_send(copy, 1, 0, h)
        ring_send(copy, 1, 1, h)

    def ring_step(copy, s):
        for h in range(2):
            for way in range(2):
                ring_take(copy, s - 1, way, h)
                if s < 4 or h == way:
                    ring_send(copy, s, way, h)

    def ring_end(copy):
        ring_take(copy, 4, 0, 0)
        ring_take(copy, 4, 1, 1)

    def ring_sent(copy):
        for s in range(1, 5):
            for h in range(2):
                for way in range(2):
                    if s < 4 or h == way:
                        sent(half_tile(copy, z, h), z_s.at[copy, way, s - 1, h])

    def kinds(core):
        return (
            (32 * core, 32, core, 4 * z + core, z // 2),
            (32 * core + 64, 32, core + 2, 4 * z + core + 2, z // 2),
            (128 + 48 * core, 48, 4 + core, 2 * z + core, z // 4),
            (224 + 48 * core, 48, 6 + core, 16 + 2 * z + core, 2 + z // 4),
        )

    def w1_tree(copy, start):
        for n, (row, count, index, source, source_x) in enumerate(kinds(c)):
            piece = wb.at[copy, pl.ds(pl.multiple_of(row, 16), count)]
            away = (yy + 8 - (copy * 4 + (source // 2) % 4)) % 8
            for here, steps in ((2, (2, 1)), (6, (7,))):

                @pl.when((x == source_x) & (away == here))
                def _():
                    if start:
                        arrived(piece, w1_r.at[copy * 8 + index])
                    for m, k in enumerate(steps):
                        if start:
                            send(piece, piece, w1t_s.at[copy, n, m], w1_r.at[copy * 8 + index], column[k - 1])
                        else:
                            sent(piece, w1t_s.at[copy, n, m])

    def w1_line(copy):
        for n, (row, count, index, source, source_x) in enumerate(kinds(c)):
            piece = wb.at[copy, pl.ds(pl.multiple_of(row, 16), count)]
            away = (yy + 8 - (copy * 4 + (source // 2) % 4)) % 8

            @pl.when(x == source_x)
            def _():
                @pl.when((away != 0) & (away != 2) & (away != 6))
                def _():
                    arrived(piece, w1_r.at[copy * 8 + index])

                for k in range(3):
                    send(piece, piece, w1x_s.at[copy, n, k], w1_r.at[copy * 8 + index], line[k])
                send(piece, piece, w1s_s.at[copy, n], w1_r.at[copy * 8 + index], sibling)

    def w1_core(copy):
        for n, (row, count, index, source, source_x) in enumerate(kinds(c)):
            piece = wb.at[copy, pl.ds(pl.multiple_of(row, 16), count)]

            @pl.when(x != source_x)
            def _():
                arrived(piece, w1_r.at[copy * 8 + index])
                send(piece, piece, w1s_s.at[copy, n], w1_r.at[copy * 8 + index], sibling)

    def w1_end(copy):
        for row, count, index, source, source_x in kinds(1 - c):
            piece = wb.at[copy, pl.ds(pl.multiple_of(row, 16), count)]
            arrived(piece, w1_r.at[copy * 8 + index])

    def w1_sent(copy):
        for n, (row, count, index, source, source_x) in enumerate(kinds(c)):
            piece = wb.at[copy, pl.ds(pl.multiple_of(row, 16), count)]

            @pl.when(x == source_x)
            def _():
                for k in range(3):
                    sent(piece, w1x_s.at[copy, n, k])

            sent(piece, w1s_s.at[copy, n])

    def g1_line(yk):
        for n in range(3):
            send(g1.at[c, x, yk], g1.at[c, x, yk], g1x_s.at[yk, n], g1x_r.at[x, yk], line[n])
        send(g1.at[c, x, yk], g1.at[c, x, yk], g1o_s.at[yk], g1o_r.at[yk], sibling)

    def g1_send(s, way):
        at = (yy + 9 - s if way == 0 else yy + s - 1) % 8
        piece = g1.at[c, x, at % 4]

        @pl.when(at >= 4)
        def _():
            send(piece, piece, g1y_s.at[way, s - 1], g1y_r.at[at % 4], column[0 if way == 0 else 6])

    def g1_take(s, way):
        at = (yy + 8 - s if way == 0 else yy + s) % 8

        @pl.when(at >= 4)
        def _():
            arrived(g1.at[c, x, at % 4], g1y_r.at[at % 4])
            if s < (4 if way == 0 else 3):
                g1_pass(s + 1, way)
            g1_line(at % 4)

    def g1_pass(s, way):
        at = (yy + 9 - s if way == 0 else yy + s - 1) % 8
        piece = g1.at[c, x, at % 4]
        send(piece, piece, g1y_s.at[way, s - 1], g1y_r.at[at % 4], column[0 if way == 0 else 6])

    def g1_y_sent():
        for way in range(2):
            for s in range(1, 5 - way):
                at = (yy + 9 - s if way == 0 else yy + s - 1) % 8

                @pl.when(at >= 4)
                def _():
                    sent(g1.at[c, x, at % 4], g1y_s.at[way, s - 1])

    def g1_core():
        for k in range(1, 4):
            xk = (x + k) % 4
            for yk in range(4):
                arrived(g1.at[c, xk, yk], g1x_r.at[xk, yk])
            send(g1.at[c, xk], g1.at[c, xk], g1s_s.at[k], g1s_r.at[xk], sibling)

    def g1_end():
        for yk in range(4):
            arrived(g1.at[1 - c, x, yk], g1o_r.at[yk])
        for k in range(1, 4):
            arrived(g1.at[1 - c, (x + k) % 4], g1s_r.at[(x + k) % 4])

    def g1_sent():
        for yk in range(4):
            for k in range(3):
                sent(g1.at[c, x, yk], g1x_s.at[yk, k])
            sent(g1.at[c, x, yk], g1o_s.at[yk])
        for k in range(1, 4):
            sent(g1.at[c, (x + k) % 4], g1s_s.at[k])

    def g0_line():
        for k in range(1, 4):
            yk = (y + k) % 4
            arrived(g0.at[c, x, yk], g0y_r.at[yk])
        for k in range(3):
            send(g0.at[c, x], g0.at[c, x], g0x_s.at[k], g0x_r.at[x], line[k])
        send(g0.at[c, x], g0.at[c, x], g0s_s.at[0], g0s_r.at[x], sibling)

    def g0_core():
        for k in range(1, 4):
            xk = (x + k) % 4
            arrived(g0.at[c, xk], g0x_r.at[xk])
            send(g0.at[c, xk], g0.at[c, xk], g0s_s.at[k], g0s_r.at[xk], sibling)

    def g0_end():
        for xk in range(4):
            arrived(g0.at[1 - c, xk], g0s_r.at[xk])

    def g0_sent():
        for k in range(3):
            sent(g0.at[c, x], g0x_s.at[k])
        for k in range(4):
            sent(g0.at[c, (x + k) % 4], g0s_s.at[k])

    side = 1 - 2 * (z % 2)
    order = [z // 2, (z // 2 + 4 - side) % 4, (z // 2 + 4 + side) % 4, (z // 2 + 2) % 4]

    def pack_query(copy):
        wq_s[...] = jnp.concatenate(
            [wb[copy, 32 * n : 32 * n + 32, :].astype(F32)[0:GP] for n in range(4)], axis=0
        ).astype(BF16)

    def project(copy, s):
        pair = order[s - 1]
        span = pl.ds(pl.multiple_of(128 * pair, 128), 128)
        tokens = gb[copy, span, :]
        kvo[copy, pair] = dot(wb[copy, 128:320, :], tokens, NT).astype(BF16)
        send(kvo.at[copy, pair], kvl.at[copy, pair], h_s.at[copy, 0, s - 1], h_r.at[copy, 0, s - 1], right)
        send(kvo.at[copy, pair], kvr.at[copy, pair], h_s.at[copy, 1, s - 1], h_r.at[copy, 1, s - 1], left)
        q_s[span, :] = dot(tokens, wq_s[...], NT).astype(BF16)

    def halo_end(copy):
        for s in range(4):
            arrived(kvl.at[copy, order[s]], h_r.at[copy, 0, s])
            arrived(kvr.at[copy, order[s]], h_r.at[copy, 1, s])

    def attend(copy):
        for block in range(4):
            first, last = max(block - 1, 0), min(block + 1, 3)
            lanes = (last - first + 1) * 128
            pieces = [ref[copy, n] for ref in (kvl, kvo, kvr) for n in range(first, last + 1)]
            keys = jnp.concatenate([piece[0:HP] for piece in pieces], axis=1)
            values = jnp.concatenate([piece[HP : 2 * HP] for piece in pieces], axis=1)
            scores = dot(q_s[block * 128 : block * 128 + 128, :], keys, NN) * (1.0 / math.sqrt(HD))
            scores = scores + bias[block, :, 0 : 3 * lanes]
            raised = jnp.exp(scores - jnp.max(scores, axis=-1, keepdims=True))
            weights = (raised * (1.0 / jnp.sum(raised, axis=-1, keepdims=True))).astype(BF16)
            ob[copy, block * 128 : block * 128 + 128, 0:HP] = dot(weights, values, NT).astype(BF16)
            for tile in (2 * block, 2 * block + 1):
                piece = ob.at[copy, pl.ds(64 * tile, 64)]
                if copy == 1:

                    @pl.when(z != tile)
                    def _():
                        send(piece, ab.at[z], a_s.at[copy, tile], a_r.at[z], (b, tile, t))
                else:

                    @pl.when((z != tile) | (b == 1))
                    def _():
                        send(piece, ab0.at[b, z], a_s.at[copy, tile], a0_r.at[b, z], (0, tile, t))

    def own_tile(copy):
        return ob[copy, pl.ds(pl.multiple_of(64 * z, 64), 64), :]

    def attended():
        ab[z] = own_tile(1)
        for k in range(1, 8):
            head = (z + k) % 8
            arrived(ab.at[head], a_r.at[head])

    def attended_base():
        ab0[0, z] = own_tile(0)
        for k in range(8):
            head = (z + k) % 8
            if k > 0:
                arrived(ab0.at[0, head], a0_r.at[0, head])
            arrived(ab0.at[1, head], a0_r.at[1, head])

    def attend_sent(copy):
        for s in range(4):
            sent(kvo.at[copy, order[s]], h_s.at[copy, 0, s])
            sent(kvo.at[copy, order[s]], h_s.at[copy, 1, s])
        for tile in range(8):

            @pl.when((z != tile) | ((b == 1) & (copy == 0)))
            def _():
                sent(ob.at[copy, pl.ds(64 * tile, 64)], a_s.at[copy, tile])

    def out_project(copy):
        total = None
        for head in range(8):
            parts = []
            for n in range(4):
                at = (n % 2, head // 2, 2 * (head % 2) + n // 2)
                if copy == 1:
                    parts.append(g1[at].astype(F32)[40:64])
                else:
                    parts.append(g0[at].astype(F32)[0:GP])
            w_head = jnp.concatenate(parts, axis=0).astype(BF16)
            if copy == 1:
                mixed = ab[head][:, 0:HP]
            else:
                mixed = jnp.concatenate([ab0[0, head][:, 0:HP], ab0[1, head][:, 0:HP]], axis=0)
            part = dot(mixed, w_head, NN)
            total = part if total is None else total + part
        return total

    def zero_project(control):
        parts = []
        for pair in range(16):
            two = [g1[core, pair // 4, pair % 4].astype(F32)[0:40] for core in range(2)]
            wide = dot(control, jnp.concatenate(two, axis=0).astype(BF16), NT)
            parts += [wide[:, 0:36], wide[:, 40:76]]
        return jnp.concatenate(parts, axis=1).astype(BF16)

    for load in loads[4:]:
        load.wait()
    for h in range(2):
        part = pl.ds(32 * h, 32)
        arrived(rlat.at[part], lat_r.at[h])
        control_in = lat[b, part, :].astype(F32) + rlat[part, :].astype(F32)
        hid[part, :] = control_in
        gb[1, pl.ds(pl.multiple_of(64 * z + 32 * h, 32), 32), :] = normed(control_in, 1)
        ring_start(1, h)

    w1_tree(1, True)
    g1_send(1, 0)
    g1_send(1, 1)

    @pl.when(b == 1)
    def _():
        g1_line(y)

    ring_step(1, 2)
    w1_line(1)
    ring_step(1, 3)
    g1_take(1, 0)
    g1_take(1, 1)
    ring_step(1, 4)
    g1_take(2, 0)
    g1_take(2, 1)
    w1_core(1)
    ring_end(1)
    w1_y(0, True)
    w1_end(1)
    pack_query(1)
    project(1, 1)
    project(1, 2)
    g1_take(3, 0)
    g1_take(3, 1)
    project(1, 3)
    project(1, 4)
    g1_take(4, 0)
    halo_end(1)
    w1_tree(0, True)
    g0_y(True)
    attend(1)
    w1_line(0)
    g1_core()
    attended()
    g1_end()
    control = (hid[...] + mod[2, 1:2, :] * out_project(1)).astype(BF16)

    @pl.when(b == 0)
    def _():
        stage[...] = control
        send(stage, out.at[0], o_s.at[0], o_r.at[0], partner)

    @pl.when(b == 1)
    def _():
        out[1] = control

    residual = zero_project(control)
    base_in = jnp.where(b == 0, lat[b].astype(F32), rlat[...].astype(F32)) + residual.astype(F32)
    hid[...] = base_in
    gb[0, pl.ds(pl.multiple_of(64 * z, 64), 64), :] = normed(base_in, 0)
    ring_start(0, 0)
    ring_start(0, 1)
    w1_core(0)

    @pl.when(b == 0)
    def _():
        g0_line()


    @pl.when(b == 1)
    def _():
        res_s[...] = residual
        send(res_s, rres, r_s.at[0], r_r.at[0], partner)

    ring_step(0, 2)
    w1_end(0)
    pack_query(0)
    project(0, 1)
    ring_step(0, 3)
    project(0, 2)
    ring_step(0, 4)
    project(0, 3)
    ring_end(0)
    project(0, 4)

    @pl.when(b == 0)
    def _():
        g0_core()

    halo_end(0)
    attend(0)

    @pl.when(b == 0)
    def _():
        arrived(rres, r_r.at[0])
        attended_base()
        g0_end()
        second = lat[1].astype(F32) + rres[...].astype(F32)
        gated = mod[2, 0:1, :] * out_project(0)
        out[0] = (hid[...] + gated[0:64]).astype(BF16)
        out[1] = (second + gated[64:128]).astype(BF16)
        sent(stage, o_s.at[0])
        g0_sent()

    @pl.when(b == 1)
    def _():
        arrived(out.at[0], o_r.at[0])
        sent(res_s, r_s.at[0])

    for copy in lat_copies:
        copy.wait_send()
    g1_y_sent()
    g0_y(False)
    g1_sent()
    for copy in (1, 0):
        w1_y(copy, False)
        w1_tree(copy, False)
        w1_sent(copy)
        ring_sent(copy)
        attend_sent(copy)


def on_device(latent, modulation, w_query, w_keyval, w_out, w_zero):
    dma = pltpu.SemaphoreType.DMA
    vmem = pltpu.VMEM
    result = pl.pallas_call(
        kernel,
        out_shape=jax.ShapeDtypeStruct((2, 64, D), BF16),
        in_specs=[pl.BlockSpec(memory_space=pl.ANY)] * 6,
        out_specs=pl.BlockSpec(memory_space=pltpu.VMEM),
        scratch_shapes=[
            vmem((2, 64, D), BF16),
            vmem((3, 2, D), F32),
            vmem((18, D), BF16),
            vmem((36, D), BF16),
            vmem((18, D), BF16),
            vmem((36, D), BF16),
            vmem((2, 320, D), BF16),
            vmem((2, 4, 4, 64, D), BF16),
            vmem((2, 4, 4, 32, D), BF16),
            vmem((2, 512, D), BF16),
            vmem((2, 4, 2 * HP, 128), BF16),
            vmem((2, 4, 2 * HP, 128), BF16),
            vmem((2, 4, 2 * HP, 128), BF16),
            vmem((2, 512, 128), BF16),
            vmem((8, 64, 128), BF16),
            vmem((2, 8, 64, 128), BF16),
            vmem((4, 128, D), F32),
            vmem((64, D), F32),
            vmem((64, D), BF16),
            vmem((64, D), BF16),
            vmem((64, D), BF16),
            vmem((64, D), BF16),
            vmem((512, HP), BF16),
            vmem((HP, D), BF16),
            dma((6,)), dma((2,)), dma((2,)),
            dma((2, 4)), dma((2, 4, 2)), dma((2, 4, 3)), dma((2, 4)), dma((16,)),
            dma((2, 4)), dma((4, 3)), dma((4,)), dma((4,)), dma((4, 4)), dma((4,)), dma((4,)), dma((4,)),
            dma((3,)), dma((3,)), dma((4,)), dma((4,)), dma((4,)), dma((4,)),
            dma((2, 2, 4, 2)), dma((2, 2, 4, 2)), dma((2, 2, 4)), dma((2, 2, 4)),
            dma((2, 8)), dma((8,)), dma((2, 8)), dma((1,)), dma((1,)), dma((1,)), dma((1,)),
        ],
        compiler_params=pltpu.CompilerParams(
            collective_id=0, has_side_effects=True, vmem_limit_bytes=56 * 1024 * 1024
        ),
    )(
        latent.reshape(2, 64, D), modulation.swapaxes(0, 1), w_query[0].T, w_keyval[0].T, w_out[0], w_zero.T,
    )
    return result.reshape(latent.shape)


def solution(mesh):
    placed = (
        P("branch", None, "trow", "tcol", None),
        P(),
        P("branch", None, "tcol"),
        P("branch", None, "tcol"),
        P("branch", "tcol", None),
        P(None, "tcol"),
    )
    return jax.shard_map(
        on_device,
        mesh=mesh,
        in_specs=placed,
        out_specs=P("branch", None, "trow", "tcol", None),
        check_vma=False,
    )
```

```python
import math

import jax
import jax.numpy as jnp
from jax import lax
from jax.experimental import pallas as pl
from jax.experimental.pallas import tpu as pltpu
from jax.sharding import PartitionSpec as P

MESH = pl.DeviceIdType.MESH
F32 = jnp.float32
BF16 = jnp.bfloat16
D = 1152
HD = 72
GP = 24
HP = 96
NEG = -1e30
NT = (((1,), (1,)), ((), ()))
NN = (((1,), (0,)), ((), ()))


def dot(a, b, dims):
    return lax.dot_general(a, b, dims, preferred_element_type=F32)


def pick(rows, cols, pieces):
    r = lax.broadcasted_iota(jnp.int32, (rows, cols), 0)
    c = lax.broadcasted_iota(jnp.int32, (rows, cols), 1)
    hit = None
    for row0, col0, count in pieces:
        one = (r - row0 == c - col0) & (r >= row0) & (r < row0 + count)
        hit = one if hit is None else hit | one
    return jnp.where(hit, 1.0, 0.0).astype(BF16)


def kernel(
    lat_h, mod_h, wq_h, wkv_h, wo_h, wz_h, out,
    lat, mod, wq, wkv, wo, wz,
    wb, g1, g0, gb, kvo, kvl, kvr, ob, ab, ab0, bias, hid, rlat, rres, stage, res_s, q_s, wq_s, wo_s,
    in_s, lat_s, lat_r, w1y_s, w1t_s, w1x_s, w1s_s, w1_r, g1y_s, g1x_s, g1s_s, g1y_r, g1x_r, g1s_r, g1o_s, g1o_r,
    g0y_s, g0x_s, g0s_s, g0y_r, g0x_r, g0s_r, z_s, z_r, h_s, h_r, a_s, a_r, a0_r, o_s, o_r, r_s, r_r,
):
    b = lax.axis_index("branch")
    z = lax.axis_index("trow")
    t = lax.axis_index("tcol")
    x, y, c = t // 8, (t // 2) % 4, t % 2
    yy = b * 4 + y
    partner = (1 - b, z, t)
    sibling = (b, z, t + 1 - 2 * c)
    left = (b, z, (t + 31) % 32)
    right = (b, z, (t + 1) % 32)
    column = []
    for k in range(1, 8):
        other = (yy + k) % 8
        column.append((other // 4, z, x * 8 + (other % 4) * 2 + c))
    line = [(b, z, ((x + k) % 4) * 8 + y * 2 + c) for k in range(1, 4)]
    ring = [(b, (z + k) % 8, t) for k in range(1, 8)]
    far = jnp.where(c == 0, (t + 31) % 32, (t + 1) % 32)

    def send(src, dst, ss, rs, dev):
        copy = pltpu.make_async_remote_copy(
            src_ref=src, dst_ref=dst, send_sem=ss, recv_sem=rs, device_id=dev, device_id_type=MESH
        )
        copy.start()
        return copy

    def arrived(dst, rs):
        pltpu.make_async_remote_copy(
            src_ref=dst, dst_ref=dst, send_sem=lat_s.at[0], recv_sem=rs, device_id=partner, device_id_type=MESH
        ).wait_recv()

    def sent(src, ss):
        pltpu.make_async_remote_copy(
            src_ref=src, dst_ref=src, send_sem=ss, recv_sem=lat_r.at[0], device_id=partner, device_id_type=MESH
        ).wait_send()

    barrier = pltpu.get_barrier_semaphore()
    near = [column[k - 1] for k in (1, 2, 4, 6, 7)]
    peers = near + line + [ring[0], ring[6], sibling, (b, z, far)]
    for dev in peers:
        pl.semaphore_signal(barrier, inc=1, device_id=dev, device_id_type=MESH)

    loads = [
        pltpu.make_async_copy(src, dst, in_s.at[n])
        for n, (src, dst) in enumerate(
            ((wq_h, wq), (wkv_h, wkv), (wo_h, wo), (wz_h, wz), (lat_h, lat), (mod_h, mod))
        )
    ]
    for load in loads:
        load.start()
    for load in loads[:4]:
        load.wait()

    rows = (
        dot(pick(144, 18, [(0, 0, 18)]), wq[...], NN)
        + dot(pick(144, 36, [(32, 0, 18), (56, 18, 18)]), wkv[...], NN)
        + dot(pick(144, 36, [(80, 0, 36)]), wz[...], NN)
        + dot(pick(144, 18, [(120, 0, 18)]), wo[...], NN)
    ).astype(BF16)
    own_q, own_kv = t // 4 == z, (t // 2) % 8 == z
    q_row = pl.multiple_of(32 * (t % 4), 16)
    kv_row = pl.multiple_of(128 + 96 * (t // 16) + 48 * c, 16)
    kv_idx = 4 + 2 * (t // 16) + c

    @pl.when(own_q)
    def _():
        wb[b, pl.ds(q_row, 32), :] = rows[0:32]

    @pl.when(own_kv)
    def _():
        wb[b, pl.ds(kv_row, 48), :] = rows[32:80]

    @pl.when(b == 1)
    def _():
        g1[c, x, y] = rows[80:144]

    @pl.when(b == 0)
    def _():
        g0[c, x, y] = jnp.concatenate(
            [rows[120:144].astype(F32), jnp.zeros((8, D), F32)], axis=0
        ).astype(BF16)

    pl.semaphore_wait(barrier, len(peers))

    def lat_half(h):
        return send(
            lat_h.at[1 - b, pl.ds(32 * h, 32)], rlat.at[pl.ds(32 * h, 32)], lat_s.at[h], lat_r.at[h], partner
        )

    lat_copies = [lat_half(0), lat_half(1)]

    def w1_y(copy, start):
        @pl.when(own_q & (b == copy))
        def _():
            piece = wb.at[copy, pl.ds(q_row, 32)]
            for n, k in enumerate((2, 6, 1, 7)):
                if start:
                    send(piece, piece, w1y_s.at[0, n], w1_r.at[copy * 8 + t % 4], column[k - 1])
                else:
                    sent(piece, w1y_s.at[0, n])

        @pl.when(own_kv & (b == copy))
        def _():
            piece = wb.at[copy, pl.ds(kv_row, 48)]
            for n, k in enumerate((2, 6, 1, 7)):
                if start:
                    send(piece, piece, w1y_s.at[1, n], w1_r.at[copy * 8 + kv_idx], column[k - 1])
                else:
                    sent(piece, w1y_s.at[1, n])

    def g0_y(start):
        @pl.when(b == 0)
        def _():
            piece = g0.at[c, x, y]
            for k in range(1, 4):
                if start:
                    send(piece, piece, g0y_s.at[k - 1], g0y_r.at[y], (b, z, x * 8 + ((y + k) % 4) * 2 + c))
                else:
                    sent(piece, g0y_s.at[k - 1])

    w1_y(1, True)

    for block in range(4):
        first, last = max(block - 1, 0), min(block + 1, 3)
        lanes = (last - first + 1) * 128
        q = lax.broadcasted_iota(jnp.int32, (128, lanes), 0)
        k = lax.broadcasted_iota(jnp.int32, (128, lanes), 1)
        i, j = block * 16 + q // 8, t * 8 + q % 8
        row, col = first * 16 + k // 8, (t - 1) * 8 + k % 8
        row0, col0 = jnp.clip(i - 6, 0, 51), jnp.clip(j - 6, 0, 243)
        row_ok = (row >= row0) & (row < row0 + 13)
        for strip in range(3):
            here = col + 8 * strip
            ok = row_ok & (here >= col0) & (here < col0 + 13)
            bias[block, :, strip * lanes : (strip + 1) * lanes] = jnp.where(ok, 0.0, NEG)
    ob[...] = jnp.zeros_like(ob)

    def normed(hidden, copy):
        average = jnp.mean(hidden, axis=-1, keepdims=True)
        centred = hidden - average
        variance = jnp.mean(centred * centred, axis=-1, keepdims=True)
        shift, scale = mod[0, copy : copy + 1, :], mod[1, copy : copy + 1, :]
        return (centred * lax.rsqrt(variance + 1e-06) * (1.0 + scale) + shift).astype(BF16)

    def half_tile(copy, index, h):
        start = 64 * ((index + 8) % 8) + 32 * h
        return gb.at[copy, pl.ds(pl.multiple_of(start, 32), 32)]

    def ring_send(copy, s, way, h):
        tile = half_tile(copy, z - s + 1 if way == 0 else z + s - 1, h)
        send(tile, tile, z_s.at[copy, way, s - 1, h], z_r.at[copy, way, s - 1, h], ring[0] if way == 0 else ring[6])

    def ring_take(copy, s, way, h):
        arrived(half_tile(copy, z - s if way == 0 else z + s, h), z_r.at[copy, way, s - 1, h])

    def ring_start(copy, h):
        ring_send(copy, 1, 0, h)
        ring_send(copy, 1, 1, h)

    def ring_step(copy, s):
        for h in range(2):
            for way in range(2):
                ring_take(copy, s - 1, way, h)
                if s < 4 or h == way:
                    ring_send(copy, s, way, h)

    def ring_end(copy):
        ring_take(copy, 4, 0, 0)
        ring_take(copy, 4, 1, 1)

    def ring_sent(copy):
        for s in range(1, 5):
            for h in range(2):
                for way in range(2):
                    if s < 4 or h == way:
                        sent(half_tile(copy, z, h), z_s.at[copy, way, s - 1, h])

    def kinds(core):
        return (
            (32 * core, 32, core, 4 * z + core, z // 2),
            (32 * core + 64, 32, core + 2, 4 * z + core + 2, z // 2),
            (128 + 48 * core, 48, 4 + core, 2 * z + core, z // 4),
            (224 + 48 * core, 48, 6 + core, 16 + 2 * z + core, 2 + z // 4),
        )

    def w1_tree(copy, start):
        for n, (row, count, index, source, source_x) in enumerate(kinds(c)):
            piece = wb.at[copy, pl.ds(pl.multiple_of(row, 16), count)]
            away = (yy + 8 - (copy * 4 + (source // 2) % 4)) % 8
            for here, steps in ((2, (2, 1)), (6, (7,))):

                @pl.when((x == source_x) & (away == here))
                def _():
                    if start:
                        arrived(piece, w1_r.at[copy * 8 + index])
                    for m, k in enumerate(steps):
                        if start:
                            send(piece, piece, w1t_s.at[copy, n, m], w1_r.at[copy * 8 + index], column[k - 1])
                        else:
                            sent(piece, w1t_s.at[copy, n, m])

    def w1_line(copy):
        for n, (row, count, index, source, source_x) in enumerate(kinds(c)):
            piece = wb.at[copy, pl.ds(pl.multiple_of(row, 16), count)]
            away = (yy + 8 - (copy * 4 + (source // 2) % 4)) % 8

            @pl.when(x == source_x)
            def _():
                @pl.when((away != 0) & (away != 2) & (away != 6))
                def _():
                    arrived(piece, w1_r.at[copy * 8 + index])

                for k in range(3):
                    send(piece, piece, w1x_s.at[copy, n, k], w1_r.at[copy * 8 + index], line[k])
                send(piece, piece, w1s_s.at[copy, n], w1_r.at[copy * 8 + index], sibling)

    def w1_core(copy):
        for n, (row, count, index, source, source_x) in enumerate(kinds(c)):
            piece = wb.at[copy, pl.ds(pl.multiple_of(row, 16), count)]

            @pl.when(x != source_x)
            def _():
                arrived(piece, w1_r.at[copy * 8 + index])
                send(piece, piece, w1s_s.at[copy, n], w1_r.at[copy * 8 + index], sibling)

    def w1_end(copy):
        for row, count, index, source, source_x in kinds(1 - c):
            piece = wb.at[copy, pl.ds(pl.multiple_of(row, 16), count)]
            arrived(piece, w1_r.at[copy * 8 + index])

    def w1_sent(copy):
        for n, (row, count, index, source, source_x) in enumerate(kinds(c)):
            piece = wb.at[copy, pl.ds(pl.multiple_of(row, 16), count)]

            @pl.when(x == source_x)
            def _():
                for k in range(3):
                    sent(piece, w1x_s.at[copy, n, k])

            sent(piece, w1s_s.at[copy, n])

    def g1_line(yk):
        for n in range(3):
            send(g1.at[c, x, yk], g1.at[c, x, yk], g1x_s.at[yk, n], g1x_r.at[x, yk], line[n])
        send(g1.at[c, x, yk], g1.at[c, x, yk], g1o_s.at[yk], g1o_r.at[yk], sibling)

    def g1_send(s, way):
        at = (yy + 9 - s if way == 0 else yy + s - 1) % 8
        piece = g1.at[c, x, at % 4]

        @pl.when(at >= 4)
        def _():
            send(piece, piece, g1y_s.at[way, s - 1], g1y_r.at[at % 4], column[0 if way == 0 else 6])

    def g1_take(s, way):
        at = (yy + 8 - s if way == 0 else yy + s) % 8

        @pl.when(at >= 4)
        def _():
            arrived(g1.at[c, x, at % 4], g1y_r.at[at % 4])
            if s < (4 if way == 0 else 3):
                g1_pass(s + 1, way)
            g1_line(at % 4)

    def g1_pass(s, way):
        at = (yy + 9 - s if way == 0 else yy + s - 1) % 8
        piece = g1.at[c, x, at % 4]
        send(piece, piece, g1y_s.at[way, s - 1], g1y_r.at[at % 4], column[0 if way == 0 else 6])

    def g1_y_sent():
        for way in range(2):
            for s in range(1, 5 - way):
                at = (yy + 9 - s if way == 0 else yy + s - 1) % 8

                @pl.when(at >= 4)
                def _():
                    sent(g1.at[c, x, at % 4], g1y_s.at[way, s - 1])

    def g1_core():
        for k in range(1, 4):
            xk = (x + k) % 4
            for yk in range(4):
                arrived(g1.at[c, xk, yk], g1x_r.at[xk, yk])
            send(g1.at[c, xk], g1.at[c, xk], g1s_s.at[k], g1s_r.at[xk], sibling)

    def g1_end():
        for yk in range(4):
            arrived(g1.at[1 - c, x, yk], g1o_r.at[yk])
        for k in range(1, 4):
            arrived(g1.at[1 - c, (x + k) % 4], g1s_r.at[(x + k) % 4])

    def g1_sent():
        for yk in range(4):
            for k in range(3):
                sent(g1.at[c, x, yk], g1x_s.at[yk, k])
            sent(g1.at[c, x, yk], g1o_s.at[yk])
        for k in range(1, 4):
            sent(g1.at[c, (x + k) % 4], g1s_s.at[k])

    def g0_line():
        for k in range(1, 4):
            yk = (y + k) % 4
            arrived(g0.at[c, x, yk], g0y_r.at[yk])
        for k in range(3):
            send(g0.at[c, x], g0.at[c, x], g0x_s.at[k], g0x_r.at[x], line[k])
        send(g0.at[c, x], g0.at[c, x], g0s_s.at[0], g0s_r.at[x], sibling)

    def g0_core():
        for k in range(1, 4):
            xk = (x + k) % 4
            arrived(g0.at[c, xk], g0x_r.at[xk])
            send(g0.at[c, xk], g0.at[c, xk], g0s_s.at[k], g0s_r.at[xk], sibling)

    def g0_end():
        for xk in range(4):
            arrived(g0.at[1 - c, xk], g0s_r.at[xk])

    def g0_sent():
        for k in range(3):
            sent(g0.at[c, x], g0x_s.at[k])
        for k in range(4):
            sent(g0.at[c, (x + k) % 4], g0s_s.at[k])

    side = 1 - 2 * (z % 2)
    order = [z // 2, (z // 2 + 4 - side) % 4, (z // 2 + 4 + side) % 4, (z // 2 + 2) % 4]

    def pack_query(copy):
        wq_s[...] = jnp.concatenate(
            [wb[copy, 32 * n : 32 * n + 32, :].astype(F32)[0:GP] for n in range(4)], axis=0
        ).astype(BF16)

    def project(copy, s):
        pair = order[s - 1]
        span = pl.ds(pl.multiple_of(128 * pair, 128), 128)
        tokens = gb[copy, span, :]
        kvo[copy, pair] = dot(wb[copy, 128:320, :], tokens, NT).astype(BF16)
        send(kvo.at[copy, pair], kvl.at[copy, pair], h_s.at[copy, 0, s - 1], h_r.at[copy, 0, s - 1], right)
        send(kvo.at[copy, pair], kvr.at[copy, pair], h_s.at[copy, 1, s - 1], h_r.at[copy, 1, s - 1], left)
        q_s[span, :] = dot(tokens, wq_s[...], NT).astype(BF16)

    def halo_end(copy):
        for s in range(4):
            arrived(kvl.at[copy, order[s]], h_r.at[copy, 0, s])
            arrived(kvr.at[copy, order[s]], h_r.at[copy, 1, s])

    def attend(copy):
        for block in range(4):
            first, last = max(block - 1, 0), min(block + 1, 3)
            lanes = (last - first + 1) * 128
            pieces = [ref[copy, n] for ref in (kvl, kvo, kvr) for n in range(first, last + 1)]
            keys = jnp.concatenate([piece[0:HP] for piece in pieces], axis=1)
            values = jnp.concatenate([piece[HP : 2 * HP] for piece in pieces], axis=1)
            scores = dot(q_s[block * 128 : block * 128 + 128, :], keys, NN) * (1.0 / math.sqrt(HD))
            scores = scores + bias[block, :, 0 : 3 * lanes]
            raised = jnp.exp(scores - jnp.max(scores, axis=-1, keepdims=True))
            weights = (raised * (1.0 / jnp.sum(raised, axis=-1, keepdims=True))).astype(BF16)
            ob[copy, block * 128 : block * 128 + 128, 0:HP] = dot(weights, values, NT).astype(BF16)
            for tile in (2 * block, 2 * block + 1):
                piece = ob.at[copy, pl.ds(64 * tile, 64)]
                if copy == 1:

                    @pl.when(z != tile)
                    def _():
                        send(piece, ab.at[z], a_s.at[copy, tile], a_r.at[z], (b, tile, t))
                else:

                    @pl.when((z != tile) | (b == 1))
                    def _():
                        send(piece, ab0.at[b, z], a_s.at[copy, tile], a0_r.at[b, z], (0, tile, t))

    def own_tile(copy):
        return ob[copy, pl.ds(pl.multiple_of(64 * z, 64), 64), :]

    def attended():
        ab[z] = own_tile(1)
        for k in range(1, 8):
            head = (z + k) % 8
            arrived(ab.at[head], a_r.at[head])

    def attended_base():
        ab0[0, z] = own_tile(0)
        for k in range(8):
            head = (z + k) % 8
            if k > 0:
                arrived(ab0.at[0, head], a0_r.at[0, head])
            arrived(ab0.at[1, head], a0_r.at[1, head])

    def attend_sent(copy):
        for s in range(4):
            sent(kvo.at[copy, order[s]], h_s.at[copy, 0, s])
            sent(kvo.at[copy, order[s]], h_s.at[copy, 1, s])
        for tile in range(8):

            @pl.when((z != tile) | ((b == 1) & (copy == 0)))
            def _():
                sent(ob.at[copy, pl.ds(64 * tile, 64)], a_s.at[copy, tile])

    def pack_out(copy):
        for head in range(8):
            parts = []
            for n in range(4):
                at = (n % 2, head // 2, 2 * (head % 2) + n // 2)
                if copy == 1:
                    parts.append(g1[at].astype(F32)[40:64])
                else:
                    parts.append(g0[at].astype(F32)[0:GP])
            wo_s[HP * head : HP * head + HP, :] = jnp.concatenate(parts, axis=0).astype(BF16)

    def out_project(copy):
        total = None
        for head in range(8):
            if copy == 1:
                mixed = ab[head][:, 0:HP]
            else:
                mixed = jnp.concatenate([ab0[0, head][:, 0:HP], ab0[1, head][:, 0:HP]], axis=0)
            part = dot(mixed, wo_s[HP * head : HP * head + HP, :], NN)
            total = part if total is None else total + part
        return total

    def zero_project(control):
        parts = []
        for pair in range(16):
            two = [g1[core, pair // 4, pair % 4].astype(F32)[0:40] for core in range(2)]
            wide = dot(control, jnp.concatenate(two, axis=0).astype(BF16), NT)
            parts += [wide[:, 0:36], wide[:, 40:76]]
        return jnp.concatenate(parts, axis=1).astype(BF16)

    for load in loads[4:]:
        load.wait()
    for h in range(2):
        part = pl.ds(32 * h, 32)
        arrived(rlat.at[part], lat_r.at[h])
        control_in = lat[b, part, :].astype(F32) + rlat[part, :].astype(F32)
        hid[part, :] = control_in
        gb[1, pl.ds(pl.multiple_of(64 * z + 32 * h, 32), 32), :] = normed(control_in, 1)
        ring_start(1, h)

    w1_tree(1, True)
    g1_send(1, 0)
    g1_send(1, 1)

    @pl.when(b == 1)
    def _():
        g1_line(y)

    ring_step(1, 2)
    w1_line(1)
    ring_step(1, 3)
    g1_take(1, 0)
    g1_take(1, 1)
    ring_step(1, 4)
    g1_take(2, 0)
    g1_take(2, 1)
    w1_core(1)
    ring_end(1)
    w1_y(0, True)
    w1_end(1)
    pack_query(1)
    project(1, 1)
    project(1, 2)
    g1_take(3, 0)
    g1_take(3, 1)
    project(1, 3)
    project(1, 4)
    g1_take(4, 0)
    halo_end(1)
    w1_tree(0, True)
    g0_y(True)
    attend(1)
    w1_line(0)
    g1_core()
    g1_end()
    pack_out(1)
    attended()
    control = (hid[...] + mod[2, 1:2, :] * out_project(1)).astype(BF16)

    @pl.when(b == 0)
    def _():
        stage[...] = control
        send(stage, out.at[0], o_s.at[0], o_r.at[0], partner)

    @pl.when(b == 1)
    def _():
        out[1] = control

    residual = zero_project(control)
    base_in = jnp.where(b == 0, lat[b].astype(F32), rlat[...].astype(F32)) + residual.astype(F32)
    hid[...] = base_in
    gb[0, pl.ds(pl.multiple_of(64 * z, 64), 64), :] = normed(base_in, 0)
    ring_start(0, 0)
    ring_start(0, 1)
    w1_core(0)

    @pl.when(b == 0)
    def _():
        g0_line()


    @pl.when(b == 1)
    def _():
        res_s[...] = residual
        send(res_s, rres, r_s.at[0], r_r.at[0], partner)

    ring_step(0, 2)
    w1_end(0)
    pack_query(0)
    project(0, 1)
    ring_step(0, 3)
    project(0, 2)
    ring_step(0, 4)
    project(0, 3)
    ring_end(0)
    project(0, 4)

    @pl.when(b == 0)
    def _():
        g0_core()

    halo_end(0)
    attend(0)

    @pl.when(b == 0)
    def _():
        g0_end()
        pack_out(0)
        arrived(rres, r_r.at[0])
        attended_base()
        second = lat[1].astype(F32) + rres[...].astype(F32)
        gated = mod[2, 0:1, :] * out_project(0)
        out[0] = (hid[...] + gated[0:64]).astype(BF16)
        out[1] = (second + gated[64:128]).astype(BF16)
        sent(stage, o_s.at[0])
        g0_sent()

    @pl.when(b == 1)
    def _():
        arrived(out.at[0], o_r.at[0])
        sent(res_s, r_s.at[0])

    for copy in lat_copies:
        copy.wait_send()
    g1_y_sent()
    g0_y(False)
    g1_sent()
    for copy in (1, 0):
        w1_y(copy, False)
        w1_tree(copy, False)
        w1_sent(copy)
        ring_sent(copy)
        attend_sent(copy)


def on_device(latent, modulation, w_query, w_keyval, w_out, w_zero):
    dma = pltpu.SemaphoreType.DMA
    vmem = pltpu.VMEM
    result = pl.pallas_call(
        kernel,
        out_shape=jax.ShapeDtypeStruct((2, 64, D), BF16),
        in_specs=[pl.BlockSpec(memory_space=pl.ANY)] * 6,
        out_specs=pl.BlockSpec(memory_space=pltpu.VMEM),
        scratch_shapes=[
            vmem((2, 64, D), BF16),
            vmem((3, 2, D), F32),
            vmem((18, D), BF16),
            vmem((36, D), BF16),
            vmem((18, D), BF16),
            vmem((36, D), BF16),
            vmem((2, 320, D), BF16),
            vmem((2, 4, 4, 64, D), BF16),
            vmem((2, 4, 4, 32, D), BF16),
            vmem((2, 512, D), BF16),
            vmem((2, 4, 2 * HP, 128), BF16),
            vmem((2, 4, 2 * HP, 128), BF16),
            vmem((2, 4, 2 * HP, 128), BF16),
            vmem((2, 512, 128), BF16),
            vmem((8, 64, 128), BF16),
            vmem((2, 8, 64, 128), BF16),
            vmem((4, 128, D), F32),
            vmem((64, D), F32),
            vmem((64, D), BF16),
            vmem((64, D), BF16),
            vmem((64, D), BF16),
            vmem((64, D), BF16),
            vmem((512, HP), BF16),
            vmem((HP, D), BF16),
            vmem((8 * HP, D), BF16),
            dma((6,)), dma((2,)), dma((2,)),
            dma((2, 4)), dma((2, 4, 2)), dma((2, 4, 3)), dma((2, 4)), dma((16,)),
            dma((2, 4)), dma((4, 3)), dma((4,)), dma((4,)), dma((4, 4)), dma((4,)), dma((4,)), dma((4,)),
            dma((3,)), dma((3,)), dma((4,)), dma((4,)), dma((4,)), dma((4,)),
            dma((2, 2, 4, 2)), dma((2, 2, 4, 2)), dma((2, 2, 4)), dma((2, 2, 4)),
            dma((2, 8)), dma((8,)), dma((2, 8)), dma((1,)), dma((1,)), dma((1,)), dma((1,)),
        ],
        compiler_params=pltpu.CompilerParams(
            collective_id=0, has_side_effects=True, vmem_limit_bytes=56 * 1024 * 1024
        ),
    )(
        latent.reshape(2, 64, D), modulation.swapaxes(0, 1), w_query[0].T, w_keyval[0].T, w_out[0], w_zero.T,
    )
    return result.reshape(latent.shape)


def solution(mesh):
    placed = (
        P("branch", None, "trow", "tcol", None),
        P(),
        P("branch", None, "tcol"),
        P("branch", None, "tcol"),
        P("branch", "tcol", None),
        P(None, "tcol"),
    )
    return jax.shard_map(
        on_device,
        mesh=mesh,
        in_specs=placed,
        out_specs=P("branch", None, "trow", "tcol", None),
        check_vma=False,
    )
```

```python
import math

import jax
import jax.numpy as jnp
from jax import lax
from jax.experimental import pallas as pl
from jax.experimental.pallas import tpu as pltpu
from jax.sharding import PartitionSpec as P

MESH = pl.DeviceIdType.MESH
F32 = jnp.float32
BF16 = jnp.bfloat16
D = 1152
HD = 72
GP = 24
HP = 96
NEG = -1e30
NT = (((1,), (1,)), ((), ()))
NN = (((1,), (0,)), ((), ()))


def dot(a, b, dims):
    return lax.dot_general(a, b, dims, preferred_element_type=F32)


def pick(rows, cols, pieces):
    r = lax.broadcasted_iota(jnp.int32, (rows, cols), 0)
    c = lax.broadcasted_iota(jnp.int32, (rows, cols), 1)
    hit = None
    for row0, col0, count in pieces:
        one = (r - row0 == c - col0) & (r >= row0) & (r < row0 + count)
        hit = one if hit is None else hit | one
    return jnp.where(hit, 1.0, 0.0).astype(BF16)


def kernel(
    lat_h, mod_h, wq_h, wkv_h, wo_h, wz_h, out,
    lat, mod, wq, wkv, wo, wz,
    wb, g1, g0, gb, kvo, kvl, kvr, ob, ab, ab0, bias, hid, rlat, rres, stage, res_s, q_s, wq_s, wo_s, wz_s,
    in_s, lat_s, lat_r, w1y_s, w1t_s, w1x_s, w1s_s, w1_r, g1y_s, g1x_s, g1s_s, g1y_r, g1x_r, g1s_r, g1o_s, g1o_r,
    g0y_s, g0x_s, g0s_s, g0y_r, g0x_r, g0s_r, z_s, z_r, h_s, h_r, a_s, a_r, a0_r, o_s, o_r, r_s, r_r,
):
    b = lax.axis_index("branch")
    z = lax.axis_index("trow")
    t = lax.axis_index("tcol")
    x, y, c = t // 8, (t // 2) % 4, t % 2
    yy = b * 4 + y
    partner = (1 - b, z, t)
    sibling = (b, z, t + 1 - 2 * c)
    left = (b, z, (t + 31) % 32)
    right = (b, z, (t + 1) % 32)
    column = []
    for k in range(1, 8):
        other = (yy + k) % 8
        column.append((other // 4, z, x * 8 + (other % 4) * 2 + c))
    line = [(b, z, ((x + k) % 4) * 8 + y * 2 + c) for k in range(1, 4)]
    ring = [(b, (z + k) % 8, t) for k in range(1, 8)]
    far = jnp.where(c == 0, (t + 31) % 32, (t + 1) % 32)

    def send(src, dst, ss, rs, dev):
        copy = pltpu.make_async_remote_copy(
            src_ref=src, dst_ref=dst, send_sem=ss, recv_sem=rs, device_id=dev, device_id_type=MESH
        )
        copy.start()
        return copy

    def arrived(dst, rs):
        pltpu.make_async_remote_copy(
            src_ref=dst, dst_ref=dst, send_sem=lat_s.at[0], recv_sem=rs, device_id=partner, device_id_type=MESH
        ).wait_recv()

    def sent(src, ss):
        pltpu.make_async_remote_copy(
            src_ref=src, dst_ref=src, send_sem=ss, recv_sem=lat_r.at[0], device_id=partner, device_id_type=MESH
        ).wait_send()

    barrier = pltpu.get_barrier_semaphore()
    near = [column[k - 1] for k in (1, 2, 4, 6, 7)]
    peers = near + line + [ring[0], ring[6], sibling, (b, z, far)]
    for dev in peers:
        pl.semaphore_signal(barrier, inc=1, device_id=dev, device_id_type=MESH)

    loads = [
        pltpu.make_async_copy(src, dst, in_s.at[n])
        for n, (src, dst) in enumerate(
            ((wq_h, wq), (wkv_h, wkv), (wo_h, wo), (wz_h, wz), (lat_h, lat), (mod_h, mod))
        )
    ]
    for load in loads:
        load.start()
    for load in loads[:4]:
        load.wait()

    rows = (
        dot(pick(144, 18, [(0, 0, 18)]), wq[...], NN)
        + dot(pick(144, 36, [(32, 0, 18), (56, 18, 18)]), wkv[...], NN)
        + dot(pick(144, 36, [(80, 0, 36)]), wz[...], NN)
        + dot(pick(144, 18, [(120, 0, 18)]), wo[...], NN)
    ).astype(BF16)
    own_q, own_kv = t // 4 == z, (t // 2) % 8 == z
    q_row = pl.multiple_of(32 * (t % 4), 16)
    kv_row = pl.multiple_of(128 + 96 * (t // 16) + 48 * c, 16)
    kv_idx = 4 + 2 * (t // 16) + c

    @pl.when(own_q)
    def _():
        wb[b, pl.ds(q_row, 32), :] = rows[0:32]

    @pl.when(own_kv)
    def _():
        wb[b, pl.ds(kv_row, 48), :] = rows[32:80]

    @pl.when(b == 1)
    def _():
        g1[c, x, y] = rows[80:144]

    @pl.when(b == 0)
    def _():
        g0[c, x, y] = jnp.concatenate(
            [rows[120:144].astype(F32), jnp.zeros((8, D), F32)], axis=0
        ).astype(BF16)

    pl.semaphore_wait(barrier, len(peers))

    def lat_half(h):
        return send(
            lat_h.at[1 - b, pl.ds(32 * h, 32)], rlat.at[pl.ds(32 * h, 32)], lat_s.at[h], lat_r.at[h], partner
        )

    lat_copies = [lat_half(0), lat_half(1)]

    def w1_y(copy, start):
        @pl.when(own_q & (b == copy))
        def _():
            piece = wb.at[copy, pl.ds(q_row, 32)]
            for n, k in enumerate((2, 6, 1, 7)):
                if start:
                    send(piece, piece, w1y_s.at[0, n], w1_r.at[copy * 8 + t % 4], column[k - 1])
                else:
                    sent(piece, w1y_s.at[0, n])

        @pl.when(own_kv & (b == copy))
        def _():
            piece = wb.at[copy, pl.ds(kv_row, 48)]
            for n, k in enumerate((2, 6, 1, 7)):
                if start:
                    send(piece, piece, w1y_s.at[1, n], w1_r.at[copy * 8 + kv_idx], column[k - 1])
                else:
                    sent(piece, w1y_s.at[1, n])

    def g0_y(start):
        @pl.when(b == 0)
        def _():
            piece = g0.at[c, x, y]
            for k in range(1, 4):
                if start:
                    send(piece, piece, g0y_s.at[k - 1], g0y_r.at[y], (b, z, x * 8 + ((y + k) % 4) * 2 + c))
                else:
                    sent(piece, g0y_s.at[k - 1])

    w1_y(1, True)

    for block in range(4):
        first, last = max(block - 1, 0), min(block + 1, 3)
        lanes = (last - first + 1) * 128
        q = lax.broadcasted_iota(jnp.int32, (128, lanes), 0)
        k = lax.broadcasted_iota(jnp.int32, (128, lanes), 1)
        i, j = block * 16 + q // 8, t * 8 + q % 8
        row, col = first * 16 + k // 8, (t - 1) * 8 + k % 8
        row0, col0 = jnp.clip(i - 6, 0, 51), jnp.clip(j - 6, 0, 243)
        row_ok = (row >= row0) & (row < row0 + 13)
        for strip in range(3):
            here = col + 8 * strip
            ok = row_ok & (here >= col0) & (here < col0 + 13)
            bias[block, :, strip * lanes : (strip + 1) * lanes] = jnp.where(ok, 0.0, NEG)
    ob[...] = jnp.zeros_like(ob)

    def normed(hidden, copy):
        average = jnp.mean(hidden, axis=-1, keepdims=True)
        centred = hidden - average
        variance = jnp.mean(centred * centred, axis=-1, keepdims=True)
        shift, scale = mod[0, copy : copy + 1, :], mod[1, copy : copy + 1, :]
        return (centred * lax.rsqrt(variance + 1e-06) * (1.0 + scale) + shift).astype(BF16)

    def half_tile(copy, index, h):
        start = 64 * ((index + 8) % 8) + 32 * h
        return gb.at[copy, pl.ds(pl.multiple_of(start, 32), 32)]

    def ring_send(copy, s, way, h):
        tile = half_tile(copy, z - s + 1 if way == 0 else z + s - 1, h)
        send(tile, tile, z_s.at[copy, way, s - 1, h], z_r.at[copy, way, s - 1, h], ring[0] if way == 0 else ring[6])

    def ring_take(copy, s, way, h):
        arrived(half_tile(copy, z - s if way == 0 else z + s, h), z_r.at[copy, way, s - 1, h])

    def ring_start(copy, h):
        ring_send(copy, 1, 0, h)
        ring_send(copy, 1, 1, h)

    def ring_step(copy, s):
        for h in range(2):
            for way in range(2):
                ring_take(copy, s - 1, way, h)
                if s < 4 or h == way:
                    ring_send(copy, s, way, h)

    def ring_end(copy):
        ring_take(copy, 4, 0, 0)
        ring_take(copy, 4, 1, 1)

    def ring_sent(copy):
        for s in range(1, 5):
            for h in range(2):
                for way in range(2):
                    if s < 4 or h == way:
                        sent(half_tile(copy, z, h), z_s.at[copy, way, s - 1, h])

    def kinds(core):
        return (
            (32 * core, 32, core, 4 * z + core, z // 2),
            (32 * core + 64, 32, core + 2, 4 * z + core + 2, z // 2),
            (128 + 48 * core, 48, 4 + core, 2 * z + core, z // 4),
            (224 + 48 * core, 48, 6 + core, 16 + 2 * z + core, 2 + z // 4),
        )

    def w1_tree(copy, start):
        for n, (row, count, index, source, source_x) in enumerate(kinds(c)):
            piece = wb.at[copy, pl.ds(pl.multiple_of(row, 16), count)]
            away = (yy + 8 - (copy * 4 + (source // 2) % 4)) % 8
            for here, steps in ((2, (2, 1)), (6, (7,))):

                @pl.when((x == source_x) & (away == here))
                def _():
                    if start:
                        arrived(piece, w1_r.at[copy * 8 + index])
                    for m, k in enumerate(steps):
                        if start:
                            send(piece, piece, w1t_s.at[copy, n, m], w1_r.at[copy * 8 + index], column[k - 1])
                        else:
                            sent(piece, w1t_s.at[copy, n, m])

    def w1_line(copy):
        for n, (row, count, index, source, source_x) in enumerate(kinds(c)):
            piece = wb.at[copy, pl.ds(pl.multiple_of(row, 16), count)]
            away = (yy + 8 - (copy * 4 + (source // 2) % 4)) % 8

            @pl.when(x == source_x)
            def _():
                @pl.when((away != 0) & (away != 2) & (away != 6))
                def _():
                    arrived(piece, w1_r.at[copy * 8 + index])

                for k in range(3):
                    send(piece, piece, w1x_s.at[copy, n, k], w1_r.at[copy * 8 + index], line[k])
                send(piece, piece, w1s_s.at[copy, n], w1_r.at[copy * 8 + index], sibling)

    def w1_core(copy):
        for n, (row, count, index, source, source_x) in enumerate(kinds(c)):
            piece = wb.at[copy, pl.ds(pl.multiple_of(row, 16), count)]

            @pl.when(x != source_x)
            def _():
                arrived(piece, w1_r.at[copy * 8 + index])
                send(piece, piece, w1s_s.at[copy, n], w1_r.at[copy * 8 + index], sibling)

    def w1_end(copy):
        for row, count, index, source, source_x in kinds(1 - c):
            piece = wb.at[copy, pl.ds(pl.multiple_of(row, 16), count)]
            arrived(piece, w1_r.at[copy * 8 + index])

    def w1_sent(copy):
        for n, (row, count, index, source, source_x) in enumerate(kinds(c)):
            piece = wb.at[copy, pl.ds(pl.multiple_of(row, 16), count)]

            @pl.when(x == source_x)
            def _():
                for k in range(3):
                    sent(piece, w1x_s.at[copy, n, k])

            sent(piece, w1s_s.at[copy, n])

    def g1_line(yk):
        for n in range(3):
            send(g1.at[c, x, yk], g1.at[c, x, yk], g1x_s.at[yk, n], g1x_r.at[x, yk], line[n])
        send(g1.at[c, x, yk], g1.at[c, x, yk], g1o_s.at[yk], g1o_r.at[yk], sibling)

    def g1_send(s, way):
        at = (yy + 9 - s if way == 0 else yy + s - 1) % 8
        piece = g1.at[c, x, at % 4]

        @pl.when(at >= 4)
        def _():
            send(piece, piece, g1y_s.at[way, s - 1], g1y_r.at[at % 4], column[0 if way == 0 else 6])

    def g1_take(s, way):
        at = (yy + 8 - s if way == 0 else yy + s) % 8

        @pl.when(at >= 4)
        def _():
            arrived(g1.at[c, x, at % 4], g1y_r.at[at % 4])
            if s < (4 if way == 0 else 3):
                g1_pass(s + 1, way)
            g1_line(at % 4)

    def g1_pass(s, way):
        at = (yy + 9 - s if way == 0 else yy + s - 1) % 8
        piece = g1.at[c, x, at % 4]
        send(piece, piece, g1y_s.at[way, s - 1], g1y_r.at[at % 4], column[0 if way == 0 else 6])

    def g1_y_sent():
        for way in range(2):
            for s in range(1, 5 - way):
                at = (yy + 9 - s if way == 0 else yy + s - 1) % 8

                @pl.when(at >= 4)
                def _():
                    sent(g1.at[c, x, at % 4], g1y_s.at[way, s - 1])

    def g1_core():
        for k in range(1, 4):
            xk = (x + k) % 4
            for yk in range(4):
                arrived(g1.at[c, xk, yk], g1x_r.at[xk, yk])
            send(g1.at[c, xk], g1.at[c, xk], g1s_s.at[k], g1s_r.at[xk], sibling)

    def g1_end():
        for yk in range(4):
            arrived(g1.at[1 - c, x, yk], g1o_r.at[yk])
        for k in range(1, 4):
            arrived(g1.at[1 - c, (x + k) % 4], g1s_r.at[(x + k) % 4])

    def g1_sent():
        for yk in range(4):
            for k in range(3):
                sent(g1.at[c, x, yk], g1x_s.at[yk, k])
            sent(g1.at[c, x, yk], g1o_s.at[yk])
        for k in range(1, 4):
            sent(g1.at[c, (x + k) % 4], g1s_s.at[k])

    def g0_line():
        for k in range(1, 4):
            yk = (y + k) % 4
            arrived(g0.at[c, x, yk], g0y_r.at[yk])
        for k in range(3):
            send(g0.at[c, x], g0.at[c, x], g0x_s.at[k], g0x_r.at[x], line[k])
        send(g0.at[c, x], g0.at[c, x], g0s_s.at[0], g0s_r.at[x], sibling)

    def g0_core():
        for k in range(1, 4):
            xk = (x + k) % 4
            arrived(g0.at[c, xk], g0x_r.at[xk])
            send(g0.at[c, xk], g0.at[c, xk], g0s_s.at[k], g0s_r.at[xk], sibling)

    def g0_end():
        for xk in range(4):
            arrived(g0.at[1 - c, xk], g0s_r.at[xk])

    def g0_sent():
        for k in range(3):
            sent(g0.at[c, x], g0x_s.at[k])
        for k in range(4):
            sent(g0.at[c, (x + k) % 4], g0s_s.at[k])

    side = 1 - 2 * (z % 2)
    order = [z // 2, (z // 2 + 4 - side) % 4, (z // 2 + 4 + side) % 4, (z // 2 + 2) % 4]

    def pack_query(copy):
        wq_s[...] = jnp.concatenate(
            [wb[copy, 32 * n : 32 * n + 32, :].astype(F32)[0:GP] for n in range(4)], axis=0
        ).astype(BF16)

    def project(copy, s):
        pair = order[s - 1]
        span = pl.ds(pl.multiple_of(128 * pair, 128), 128)
        tokens = gb[copy, span, :]
        kvo[copy, pair] = dot(wb[copy, 128:320, :], tokens, NT).astype(BF16)
        send(kvo.at[copy, pair], kvl.at[copy, pair], h_s.at[copy, 0, s - 1], h_r.at[copy, 0, s - 1], right)
        send(kvo.at[copy, pair], kvr.at[copy, pair], h_s.at[copy, 1, s - 1], h_r.at[copy, 1, s - 1], left)
        q_s[span, :] = dot(tokens, wq_s[...], NT).astype(BF16)

    def halo_end(copy):
        for s in range(4):
            arrived(kvl.at[copy, order[s]], h_r.at[copy, 0, s])
            arrived(kvr.at[copy, order[s]], h_r.at[copy, 1, s])

    def attend(copy):
        for block in range(4):
            first, last = max(block - 1, 0), min(block + 1, 3)
            lanes = (last - first + 1) * 128
            pieces = [ref[copy, n] for ref in (kvl, kvo, kvr) for n in range(first, last + 1)]
            keys = jnp.concatenate([piece[0:HP] for piece in pieces], axis=1)
            values = jnp.concatenate([piece[HP : 2 * HP] for piece in pieces], axis=1)
            scores = dot(q_s[block * 128 : block * 128 + 128, :], keys, NN) * (1.0 / math.sqrt(HD))
            scores = scores + bias[block, :, 0 : 3 * lanes]
            raised = jnp.exp(scores - jnp.max(scores, axis=-1, keepdims=True))
            weights = (raised * (1.0 / jnp.sum(raised, axis=-1, keepdims=True))).astype(BF16)
            ob[copy, block * 128 : block * 128 + 128, 0:HP] = dot(weights, values, NT).astype(BF16)
            for tile in (2 * block, 2 * block + 1):
                piece = ob.at[copy, pl.ds(64 * tile, 64)]
                if copy == 1:

                    @pl.when(z != tile)
                    def _():
                        send(piece, ab.at[z], a_s.at[copy, tile], a_r.at[z], (b, tile, t))
                else:

                    @pl.when((z != tile) | (b == 1))
                    def _():
                        send(piece, ab0.at[b, z], a_s.at[copy, tile], a0_r.at[b, z], (0, tile, t))

    def own_tile(copy):
        return ob[copy, pl.ds(pl.multiple_of(64 * z, 64), 64), :]

    def attended():
        ab[z] = own_tile(1)
        for k in range(1, 8):
            head = (z + k) % 8
            arrived(ab.at[head], a_r.at[head])

    def attended_base():
        ab0[0, z] = own_tile(0)
        for k in range(8):
            head = (z + k) % 8
            if k > 0:
                arrived(ab0.at[0, head], a0_r.at[0, head])
            arrived(ab0.at[1, head], a0_r.at[1, head])

    def attend_sent(copy):
        for s in range(4):
            sent(kvo.at[copy, order[s]], h_s.at[copy, 0, s])
            sent(kvo.at[copy, order[s]], h_s.at[copy, 1, s])
        for tile in range(8):

            @pl.when((z != tile) | ((b == 1) & (copy == 0)))
            def _():
                sent(ob.at[copy, pl.ds(64 * tile, 64)], a_s.at[copy, tile])

    def pack_out(copy):
        for head in range(8):
            parts = []
            for n in range(4):
                at = (n % 2, head // 2, 2 * (head % 2) + n // 2)
                if copy == 1:
                    parts.append(g1[at].astype(F32)[40:64])
                else:
                    parts.append(g0[at].astype(F32)[0:GP])
            wo_s[HP * head : HP * head + HP, :] = jnp.concatenate(parts, axis=0).astype(BF16)

    def out_project(copy):
        if copy == 1:
            mixed = jnp.concatenate([ab[head][:, 0:HP] for head in range(8)], axis=1)
        else:
            mixed = jnp.concatenate(
                [
                    jnp.concatenate([ab0[image, head][:, 0:HP] for head in range(8)], axis=1)
                    for image in range(2)
                ],
                axis=0,
            )
        return dot(mixed, wo_s[...], NN)

    def pack_zero():
        for pair in range(16):
            two = [g1[core, pair // 4, pair % 4].astype(F32)[0:40] for core in range(2)]
            wz_s[80 * pair : 80 * pair + 80, :] = jnp.concatenate(two, axis=0).astype(BF16)

    def zero_project(control):
        wide = dot(control, wz_s[...], NT)
        return jnp.concatenate([wide[:, 40 * n : 40 * n + 36] for n in range(32)], axis=1).astype(BF16)

    for load in loads[4:]:
        load.wait()
    for h in range(2):
        part = pl.ds(32 * h, 32)
        arrived(rlat.at[part], lat_r.at[h])
        control_in = lat[b, part, :].astype(F32) + rlat[part, :].astype(F32)
        hid[part, :] = control_in
        gb[1, pl.ds(pl.multiple_of(64 * z + 32 * h, 32), 32), :] = normed(control_in, 1)
        ring_start(1, h)

    w1_tree(1, True)
    g1_send(1, 0)
    g1_send(1, 1)

    @pl.when(b == 1)
    def _():
        g1_line(y)

    ring_step(1, 2)
    w1_line(1)
    ring_step(1, 3)
    g1_take(1, 0)
    g1_take(1, 1)
    ring_step(1, 4)
    g1_take(2, 0)
    g1_take(2, 1)
    w1_core(1)
    ring_end(1)
    w1_y(0, True)
    w1_end(1)
    pack_query(1)
    project(1, 1)
    project(1, 2)
    g1_take(3, 0)
    g1_take(3, 1)
    project(1, 3)
    project(1, 4)
    g1_take(4, 0)
    halo_end(1)
    w1_tree(0, True)
    g0_y(True)
    attend(1)
    w1_line(0)
    g1_core()
    g1_end()
    pack_out(1)
    pack_zero()
    attended()
    control = (hid[...] + mod[2, 1:2, :] * out_project(1)).astype(BF16)

    @pl.when(b == 0)
    def _():
        stage[...] = control
        send(stage, out.at[0], o_s.at[0], o_r.at[0], partner)

    @pl.when(b == 1)
    def _():
        out[1] = control

    residual = zero_project(control)
    base_in = jnp.where(b == 0, lat[b].astype(F32), rlat[...].astype(F32)) + residual.astype(F32)
    hid[...] = base_in
    gb[0, pl.ds(pl.multiple_of(64 * z, 64), 64), :] = normed(base_in, 0)
    ring_start(0, 0)
    ring_start(0, 1)
    w1_core(0)

    @pl.when(b == 0)
    def _():
        g0_line()


    @pl.when(b == 1)
    def _():
        res_s[...] = residual
        send(res_s, rres, r_s.at[0], r_r.at[0], partner)

    ring_step(0, 2)
    w1_end(0)
    pack_query(0)
    project(0, 1)
    ring_step(0, 3)
    project(0, 2)
    ring_step(0, 4)
    project(0, 3)
    ring_end(0)
    project(0, 4)

    @pl.when(b == 0)
    def _():
        g0_core()

    halo_end(0)
    attend(0)

    @pl.when(b == 0)
    def _():
        g0_end()
        pack_out(0)
        arrived(rres, r_r.at[0])
        attended_base()
        second = lat[1].astype(F32) + rres[...].astype(F32)
        gated = mod[2, 0:1, :] * out_project(0)
        out[0] = (hid[...] + gated[0:64]).astype(BF16)
        out[1] = (second + gated[64:128]).astype(BF16)
        sent(stage, o_s.at[0])
        g0_sent()

    @pl.when(b == 1)
    def _():
        arrived(out.at[0], o_r.at[0])
        sent(res_s, r_s.at[0])

    for copy in lat_copies:
        copy.wait_send()
    g1_y_sent()
    g0_y(False)
    g1_sent()
    for copy in (1, 0):
        w1_y(copy, False)
        w1_tree(copy, False)
        w1_sent(copy)
        ring_sent(copy)
        attend_sent(copy)


def on_device(latent, modulation, w_query, w_keyval, w_out, w_zero):
    dma = pltpu.SemaphoreType.DMA
    vmem = pltpu.VMEM
    result = pl.pallas_call(
        kernel,
        out_shape=jax.ShapeDtypeStruct((2, 64, D), BF16),
        in_specs=[pl.BlockSpec(memory_space=pl.ANY)] * 6,
        out_specs=pl.BlockSpec(memory_space=pltpu.VMEM),
        scratch_shapes=[
            vmem((2, 64, D), BF16),
            vmem((3, 2, D), F32),
            vmem((18, D), BF16),
            vmem((36, D), BF16),
            vmem((18, D), BF16),
            vmem((36, D), BF16),
            vmem((2, 320, D), BF16),
            vmem((2, 4, 4, 64, D), BF16),
            vmem((2, 4, 4, 32, D), BF16),
            vmem((2, 512, D), BF16),
            vmem((2, 4, 2 * HP, 128), BF16),
            vmem((2, 4, 2 * HP, 128), BF16),
            vmem((2, 4, 2 * HP, 128), BF16),
            vmem((2, 512, 128), BF16),
            vmem((8, 64, 128), BF16),
            vmem((2, 8, 64, 128), BF16),
            vmem((4, 128, D), F32),
            vmem((64, D), F32),
            vmem((64, D), BF16),
            vmem((64, D), BF16),
            vmem((64, D), BF16),
            vmem((64, D), BF16),
            vmem((512, HP), BF16),
            vmem((HP, D), BF16),
            vmem((8 * HP, D), BF16),
            vmem((1280, D), BF16),
            dma((6,)), dma((2,)), dma((2,)),
            dma((2, 4)), dma((2, 4, 2)), dma((2, 4, 3)), dma((2, 4)), dma((16,)),
            dma((2, 4)), dma((4, 3)), dma((4,)), dma((4,)), dma((4, 4)), dma((4,)), dma((4,)), dma((4,)),
            dma((3,)), dma((3,)), dma((4,)), dma((4,)), dma((4,)), dma((4,)),
            dma((2, 2, 4, 2)), dma((2, 2, 4, 2)), dma((2, 2, 4)), dma((2, 2, 4)),
            dma((2, 8)), dma((8,)), dma((2, 8)), dma((1,)), dma((1,)), dma((1,)), dma((1,)),
        ],
        compiler_params=pltpu.CompilerParams(
            collective_id=0, has_side_effects=True, vmem_limit_bytes=56 * 1024 * 1024
        ),
    )(
        latent.reshape(2, 64, D), modulation.swapaxes(0, 1), w_query[0].T, w_keyval[0].T, w_out[0], w_zero.T,
    )
    return result.reshape(latent.shape)


def solution(mesh):
    placed = (
        P("branch", None, "trow", "tcol", None),
        P(),
        P("branch", None, "tcol"),
        P("branch", None, "tcol"),
        P("branch", "tcol", None),
        P(None, "tcol"),
    )
    return jax.shard_map(
        on_device,
        mesh=mesh,
        in_specs=placed,
        out_specs=P("branch", None, "trow", "tcol", None),
        check_vma=False,
    )
```

```python
import math

import jax
import jax.numpy as jnp
from jax import lax
from jax.experimental import pallas as pl
from jax.experimental.pallas import tpu as pltpu
from jax.sharding import PartitionSpec as P

MESH = pl.DeviceIdType.MESH
F32 = jnp.float32
BF16 = jnp.bfloat16
D = 1152
HD = 72
GP = 24
HP = 96
NEG = -1e30
NT = (((1,), (1,)), ((), ()))
NN = (((1,), (0,)), ((), ()))


def dot(a, b, dims):
    return lax.dot_general(a, b, dims, preferred_element_type=F32)


def pick(rows, cols, pieces):
    r = lax.broadcasted_iota(jnp.int32, (rows, cols), 0)
    c = lax.broadcasted_iota(jnp.int32, (rows, cols), 1)
    hit = None
    for row0, col0, count in pieces:
        one = (r - row0 == c - col0) & (r >= row0) & (r < row0 + count)
        hit = one if hit is None else hit | one
    return jnp.where(hit, 1.0, 0.0).astype(BF16)


def kernel(
    lat_h, mod, wq, wkv, wo, wz, out,
    lat,
    wb, g1, g0, gb, kvo, kvl, kvr, ob, ab, ab0, bias, hid, rlat, rres, stage, res_s, q_s, wq_s, wo_s, wz_s,
    in_s, lat_s, lat_r, w1y_s, w1t_s, w1x_s, w1s_s, w1_r, g1y_s, g1x_s, g1s_s, g1y_r, g1x_r, g1s_r, g1o_s, g1o_r,
    g0y_s, g0x_s, g0s_s, g0y_r, g0x_r, g0s_r, z_s, z_r, h_s, h_r, a_s, a_r, a0_r, o_s, o_r, r_s, r_r,
):
    b = lax.axis_index("branch")
    z = lax.axis_index("trow")
    t = lax.axis_index("tcol")
    x, y, c = t // 8, (t // 2) % 4, t % 2
    yy = b * 4 + y
    partner = (1 - b, z, t)
    sibling = (b, z, t + 1 - 2 * c)
    left = (b, z, (t + 31) % 32)
    right = (b, z, (t + 1) % 32)
    column = []
    for k in range(1, 8):
        other = (yy + k) % 8
        column.append((other // 4, z, x * 8 + (other % 4) * 2 + c))
    line = [(b, z, ((x + k) % 4) * 8 + y * 2 + c) for k in range(1, 4)]
    ring = [(b, (z + k) % 8, t) for k in range(1, 8)]
    far = jnp.where(c == 0, (t + 31) % 32, (t + 1) % 32)

    def send(src, dst, ss, rs, dev):
        copy = pltpu.make_async_remote_copy(
            src_ref=src, dst_ref=dst, send_sem=ss, recv_sem=rs, device_id=dev, device_id_type=MESH
        )
        copy.start()
        return copy

    def arrived(dst, rs):
        pltpu.make_async_remote_copy(
            src_ref=dst, dst_ref=dst, send_sem=lat_s.at[0], recv_sem=rs, device_id=partner, device_id_type=MESH
        ).wait_recv()

    def sent(src, ss):
        pltpu.make_async_remote_copy(
            src_ref=src, dst_ref=src, send_sem=ss, recv_sem=lat_r.at[0], device_id=partner, device_id_type=MESH
        ).wait_send()

    barrier = pltpu.get_barrier_semaphore()
    near = [column[k - 1] for k in (1, 2, 4, 6, 7)]
    peers = near + line + [ring[0], ring[6], sibling, (b, z, far)]
    for dev in peers:
        pl.semaphore_signal(barrier, inc=1, device_id=dev, device_id_type=MESH)

    load = pltpu.make_async_copy(lat_h, lat, in_s.at[0])
    load.start()

    rows = (
        dot(pick(144, 18, [(0, 0, 18)]), wq[...], NN)
        + dot(pick(144, 36, [(32, 0, 18), (56, 18, 18)]), wkv[...], NN)
        + dot(pick(144, 36, [(80, 0, 36)]), wz[...], NN)
        + dot(pick(144, 18, [(120, 0, 18)]), wo[...], NN)
    ).astype(BF16)
    own_q, own_kv = t // 4 == z, (t // 2) % 8 == z
    q_row = pl.multiple_of(32 * (t % 4), 16)
    kv_row = pl.multiple_of(128 + 96 * (t // 16) + 48 * c, 16)
    kv_idx = 4 + 2 * (t // 16) + c

    @pl.when(own_q)
    def _():
        wb[b, pl.ds(q_row, 32), :] = rows[0:32]

    @pl.when(own_kv)
    def _():
        wb[b, pl.ds(kv_row, 48), :] = rows[32:80]

    @pl.when(b == 1)
    def _():
        g1[c, x, y] = rows[80:144]

    @pl.when(b == 0)
    def _():
        g0[c, x, y] = jnp.concatenate(
            [rows[120:144].astype(F32), jnp.zeros((8, D), F32)], axis=0
        ).astype(BF16)

    pl.semaphore_wait(barrier, len(peers))

    def lat_half(h):
        return send(
            lat_h.at[1 - b, pl.ds(32 * h, 32)], rlat.at[pl.ds(32 * h, 32)], lat_s.at[h], lat_r.at[h], partner
        )

    lat_copies = [lat_half(0), lat_half(1)]

    def w1_y(copy, start):
        @pl.when(own_q & (b == copy))
        def _():
            piece = wb.at[copy, pl.ds(q_row, 32)]
            for n, k in enumerate((2, 6, 1, 7)):
                if start:
                    send(piece, piece, w1y_s.at[0, n], w1_r.at[copy * 8 + t % 4], column[k - 1])
                else:
                    sent(piece, w1y_s.at[0, n])

        @pl.when(own_kv & (b == copy))
        def _():
            piece = wb.at[copy, pl.ds(kv_row, 48)]
            for n, k in enumerate((2, 6, 1, 7)):
                if start:
                    send(piece, piece, w1y_s.at[1, n], w1_r.at[copy * 8 + kv_idx], column[k - 1])
                else:
                    sent(piece, w1y_s.at[1, n])

    def g0_y(start):
        @pl.when(b == 0)
        def _():
            piece = g0.at[c, x, y]
            for k in range(1, 4):
                if start:
                    send(piece, piece, g0y_s.at[k - 1], g0y_r.at[y], (b, z, x * 8 + ((y + k) % 4) * 2 + c))
                else:
                    sent(piece, g0y_s.at[k - 1])

    w1_y(1, True)

    for block in range(4):
        first, last = max(block - 1, 0), min(block + 1, 3)
        lanes = (last - first + 1) * 128
        q = lax.broadcasted_iota(jnp.int32, (128, lanes), 0)
        k = lax.broadcasted_iota(jnp.int32, (128, lanes), 1)
        i, j = block * 16 + q // 8, t * 8 + q % 8
        row, col = first * 16 + k // 8, (t - 1) * 8 + k % 8
        row0, col0 = jnp.clip(i - 6, 0, 51), jnp.clip(j - 6, 0, 243)
        row_ok = (row >= row0) & (row < row0 + 13)
        for strip in range(3):
            here = col + 8 * strip
            ok = row_ok & (here >= col0) & (here < col0 + 13)
            bias[block, :, strip * lanes : (strip + 1) * lanes] = jnp.where(ok, 0.0, NEG)
    ob[...] = jnp.zeros_like(ob)

    def normed(hidden, copy):
        average = jnp.mean(hidden, axis=-1, keepdims=True)
        centred = hidden - average
        variance = jnp.mean(centred * centred, axis=-1, keepdims=True)
        shift, scale = mod[0, copy : copy + 1, :], mod[1, copy : copy + 1, :]
        return (centred * lax.rsqrt(variance + 1e-06) * (1.0 + scale) + shift).astype(BF16)

    def half_tile(copy, index, h):
        start = 64 * ((index + 8) % 8) + 32 * h
        return gb.at[copy, pl.ds(pl.multiple_of(start, 32), 32)]

    def ring_send(copy, s, way, h):
        tile = half_tile(copy, z - s + 1 if way == 0 else z + s - 1, h)
        send(tile, tile, z_s.at[copy, way, s - 1, h], z_r.at[copy, way, s - 1, h], ring[0] if way == 0 else ring[6])

    def ring_take(copy, s, way, h):
        arrived(half_tile(copy, z - s if way == 0 else z + s, h), z_r.at[copy, way, s - 1, h])

    def ring_start(copy, h):
        ring_send(copy, 1, 0, h)
        ring_send(copy, 1, 1, h)

    def ring_step(copy, s):
        for h in range(2):
            for way in range(2):
                ring_take(copy, s - 1, way, h)
                if s < 4 or h == way:
                    ring_send(copy, s, way, h)

    def ring_end(copy):
        ring_take(copy, 4, 0, 0)
        ring_take(copy, 4, 1, 1)

    def ring_sent(copy):
        for s in range(1, 5):
            for h in range(2):
                for way in range(2):
                    if s < 4 or h == way:
                        sent(half_tile(copy, z, h), z_s.at[copy, way, s - 1, h])

    def kinds(core):
        return (
            (32 * core, 32, core, 4 * z + core, z // 2),
            (32 * core + 64, 32, core + 2, 4 * z + core + 2, z // 2),
            (128 + 48 * core, 48, 4 + core, 2 * z + core, z // 4),
            (224 + 48 * core, 48, 6 + core, 16 + 2 * z + core, 2 + z // 4),
        )

    def w1_tree(copy, start):
        for n, (row, count, index, source, source_x) in enumerate(kinds(c)):
            piece = wb.at[copy, pl.ds(pl.multiple_of(row, 16), count)]
            away = (yy + 8 - (copy * 4 + (source // 2) % 4)) % 8
            for here, steps in ((2, (2, 1)), (6, (7,))):

                @pl.when((x == source_x) & (away == here))
                def _():
                    if start:
                        arrived(piece, w1_r.at[copy * 8 + index])
                    for m, k in enumerate(steps):
                        if start:
                            send(piece, piece, w1t_s.at[copy, n, m], w1_r.at[copy * 8 + index], column[k - 1])
                        else:
                            sent(piece, w1t_s.at[copy, n, m])

    def w1_line(copy):
        for n, (row, count, index, source, source_x) in enumerate(kinds(c)):
            piece = wb.at[copy, pl.ds(pl.multiple_of(row, 16), count)]
            away = (yy + 8 - (copy * 4 + (source // 2) % 4)) % 8

            @pl.when(x == source_x)
            def _():
                @pl.when((away != 0) & (away != 2) & (away != 6))
                def _():
                    arrived(piece, w1_r.at[copy * 8 + index])

                for k in range(3):
                    send(piece, piece, w1x_s.at[copy, n, k], w1_r.at[copy * 8 + index], line[k])
                send(piece, piece, w1s_s.at[copy, n], w1_r.at[copy * 8 + index], sibling)

    def w1_core(copy):
        for n, (row, count, index, source, source_x) in enumerate(kinds(c)):
            piece = wb.at[copy, pl.ds(pl.multiple_of(row, 16), count)]

            @pl.when(x != source_x)
            def _():
                arrived(piece, w1_r.at[copy * 8 + index])
                send(piece, piece, w1s_s.at[copy, n], w1_r.at[copy * 8 + index], sibling)

    def w1_end(copy):
        for row, count, index, source, source_x in kinds(1 - c):
            piece = wb.at[copy, pl.ds(pl.multiple_of(row, 16), count)]
            arrived(piece, w1_r.at[copy * 8 + index])

    def w1_sent(copy):
        for n, (row, count, index, source, source_x) in enumerate(kinds(c)):
            piece = wb.at[copy, pl.ds(pl.multiple_of(row, 16), count)]

            @pl.when(x == source_x)
            def _():
                for k in range(3):
                    sent(piece, w1x_s.at[copy, n, k])

            sent(piece, w1s_s.at[copy, n])

    def g1_line(yk):
        for n in range(3):
            send(g1.at[c, x, yk], g1.at[c, x, yk], g1x_s.at[yk, n], g1x_r.at[x, yk], line[n])
        send(g1.at[c, x, yk], g1.at[c, x, yk], g1o_s.at[yk], g1o_r.at[yk], sibling)

    def g1_send(s, way):
        at = (yy + 9 - s if way == 0 else yy + s - 1) % 8
        piece = g1.at[c, x, at % 4]

        @pl.when(at >= 4)
        def _():
            send(piece, piece, g1y_s.at[way, s - 1], g1y_r.at[at % 4], column[0 if way == 0 else 6])

    def g1_take(s, way):
        at = (yy + 8 - s if way == 0 else yy + s) % 8

        @pl.when(at >= 4)
        def _():
            arrived(g1.at[c, x, at % 4], g1y_r.at[at % 4])
            if s < (4 if way == 0 else 3):
                g1_pass(s + 1, way)
            g1_line(at % 4)

    def g1_pass(s, way):
        at = (yy + 9 - s if way == 0 else yy + s - 1) % 8
        piece = g1.at[c, x, at % 4]
        send(piece, piece, g1y_s.at[way, s - 1], g1y_r.at[at % 4], column[0 if way == 0 else 6])

    def g1_y_sent():
        for way in range(2):
            for s in range(1, 5 - way):
                at = (yy + 9 - s if way == 0 else yy + s - 1) % 8

                @pl.when(at >= 4)
                def _():
                    sent(g1.at[c, x, at % 4], g1y_s.at[way, s - 1])

    def g1_core():
        for k in range(1, 4):
            xk = (x + k) % 4
            for yk in range(4):
                arrived(g1.at[c, xk, yk], g1x_r.at[xk, yk])
            send(g1.at[c, xk], g1.at[c, xk], g1s_s.at[k], g1s_r.at[xk], sibling)

    def g1_end():
        for yk in range(4):
            arrived(g1.at[1 - c, x, yk], g1o_r.at[yk])
        for k in range(1, 4):
            arrived(g1.at[1 - c, (x + k) % 4], g1s_r.at[(x + k) % 4])

    def g1_sent():
        for yk in range(4):
            for k in range(3):
                sent(g1.at[c, x, yk], g1x_s.at[yk, k])
            sent(g1.at[c, x, yk], g1o_s.at[yk])
        for k in range(1, 4):
            sent(g1.at[c, (x + k) % 4], g1s_s.at[k])

    def g0_line():
        for k in range(1, 4):
            yk = (y + k) % 4
            arrived(g0.at[c, x, yk], g0y_r.at[yk])
        for k in range(3):
            send(g0.at[c, x], g0.at[c, x], g0x_s.at[k], g0x_r.at[x], line[k])
        send(g0.at[c, x], g0.at[c, x], g0s_s.at[0], g0s_r.at[x], sibling)

    def g0_core():
        for k in range(1, 4):
            xk = (x + k) % 4
            arrived(g0.at[c, xk], g0x_r.at[xk])
            send(g0.at[c, xk], g0.at[c, xk], g0s_s.at[k], g0s_r.at[xk], sibling)

    def g0_end():
        for xk in range(4):
            arrived(g0.at[1 - c, xk], g0s_r.at[xk])

    def g0_sent():
        for k in range(3):
            sent(g0.at[c, x], g0x_s.at[k])
        for k in range(4):
            sent(g0.at[c, (x + k) % 4], g0s_s.at[k])

    side = 1 - 2 * (z % 2)
    order = [z // 2, (z // 2 + 4 - side) % 4, (z // 2 + 4 + side) % 4, (z // 2 + 2) % 4]

    def pack_query(copy):
        wq_s[...] = jnp.concatenate(
            [wb[copy, 32 * n : 32 * n + 32, :].astype(F32)[0:GP] for n in range(4)], axis=0
        ).astype(BF16)

    def project(copy, s):
        pair = order[s - 1]
        span = pl.ds(pl.multiple_of(128 * pair, 128), 128)
        tokens = gb[copy, span, :]
        kvo[copy, pair] = dot(wb[copy, 128:320, :], tokens, NT).astype(BF16)
        send(kvo.at[copy, pair], kvl.at[copy, pair], h_s.at[copy, 0, s - 1], h_r.at[copy, 0, s - 1], right)
        send(kvo.at[copy, pair], kvr.at[copy, pair], h_s.at[copy, 1, s - 1], h_r.at[copy, 1, s - 1], left)
        q_s[span, :] = dot(tokens, wq_s[...], NT).astype(BF16)

    def halo_end(copy):
        for s in range(4):
            arrived(kvl.at[copy, order[s]], h_r.at[copy, 0, s])
            arrived(kvr.at[copy, order[s]], h_r.at[copy, 1, s])

    def attend(copy):
        for block in range(4):
            first, last = max(block - 1, 0), min(block + 1, 3)
            lanes = (last - first + 1) * 128
            pieces = [ref[copy, n] for ref in (kvl, kvo, kvr) for n in range(first, last + 1)]
            keys = jnp.concatenate([piece[0:HP] for piece in pieces], axis=1)
            values = jnp.concatenate([piece[HP : 2 * HP] for piece in pieces], axis=1)
            scores = dot(q_s[block * 128 : block * 128 + 128, :], keys, NN) * (1.0 / math.sqrt(HD))
            scores = scores + bias[block, :, 0 : 3 * lanes]
            raised = jnp.exp(scores - jnp.max(scores, axis=-1, keepdims=True))
            weights = (raised * (1.0 / jnp.sum(raised, axis=-1, keepdims=True))).astype(BF16)
            ob[copy, block * 128 : block * 128 + 128, 0:HP] = dot(weights, values, NT).astype(BF16)
            for tile in (2 * block, 2 * block + 1):
                piece = ob.at[copy, pl.ds(64 * tile, 64)]
                if copy == 1:

                    @pl.when(z != tile)
                    def _():
                        send(piece, ab.at[z], a_s.at[copy, tile], a_r.at[z], (b, tile, t))
                else:

                    @pl.when((z != tile) | (b == 1))
                    def _():
                        send(piece, ab0.at[b, z], a_s.at[copy, tile], a0_r.at[b, z], (0, tile, t))

    def own_tile(copy):
        return ob[copy, pl.ds(pl.multiple_of(64 * z, 64), 64), :]

    def attended():
        ab[z] = own_tile(1)
        for k in range(1, 8):
            head = (z + k) % 8
            arrived(ab.at[head], a_r.at[head])

    def attended_base():
        ab0[0, z] = own_tile(0)
        for k in range(8):
            head = (z + k) % 8
            if k > 0:
                arrived(ab0.at[0, head], a0_r.at[0, head])
            arrived(ab0.at[1, head], a0_r.at[1, head])

    def attend_sent(copy):
        for s in range(4):
            sent(kvo.at[copy, order[s]], h_s.at[copy, 0, s])
            sent(kvo.at[copy, order[s]], h_s.at[copy, 1, s])
        for tile in range(8):

            @pl.when((z != tile) | ((b == 1) & (copy == 0)))
            def _():
                sent(ob.at[copy, pl.ds(64 * tile, 64)], a_s.at[copy, tile])

    def pack_out(copy):
        for head in range(8):
            parts = []
            for n in range(4):
                at = (n % 2, head // 2, 2 * (head % 2) + n // 2)
                if copy == 1:
                    parts.append(g1[at].astype(F32)[40:64])
                else:
                    parts.append(g0[at].astype(F32)[0:GP])
            wo_s[HP * head : HP * head + HP, :] = jnp.concatenate(parts, axis=0).astype(BF16)

    def out_project(copy):
        if copy == 1:
            mixed = jnp.concatenate([ab[head][:, 0:HP] for head in range(8)], axis=1)
        else:
            mixed = jnp.concatenate(
                [
                    jnp.concatenate([ab0[image, head][:, 0:HP] for head in range(8)], axis=1)
                    for image in range(2)
                ],
                axis=0,
            )
        return dot(mixed, wo_s[...], NN)

    def pack_zero():
        for pair in range(16):
            two = [g1[core, pair // 4, pair % 4].astype(F32)[0:40] for core in range(2)]
            wz_s[80 * pair : 80 * pair + 80, :] = jnp.concatenate(two, axis=0).astype(BF16)

    def zero_project(control):
        wide = dot(control, wz_s[...], NT)
        return jnp.concatenate([wide[:, 40 * n : 40 * n + 36] for n in range(32)], axis=1).astype(BF16)

    load.wait()
    for h in range(2):
        part = pl.ds(32 * h, 32)
        arrived(rlat.at[part], lat_r.at[h])
        control_in = lat[b, part, :].astype(F32) + rlat[part, :].astype(F32)
        hid[part, :] = control_in
        gb[1, pl.ds(pl.multiple_of(64 * z + 32 * h, 32), 32), :] = normed(control_in, 1)
        ring_start(1, h)

    w1_tree(1, True)
    g1_send(1, 0)
    g1_send(1, 1)

    @pl.when(b == 1)
    def _():
        g1_line(y)

    ring_step(1, 2)
    w1_line(1)
    ring_step(1, 3)
    g1_take(1, 0)
    g1_take(1, 1)
    ring_step(1, 4)
    g1_take(2, 0)
    g1_take(2, 1)
    w1_core(1)
    ring_end(1)
    w1_y(0, True)
    w1_end(1)
    pack_query(1)
    project(1, 1)
    project(1, 2)
    g1_take(3, 0)
    g1_take(3, 1)
    project(1, 3)
    project(1, 4)
    g1_take(4, 0)
    halo_end(1)
    w1_tree(0, True)
    g0_y(True)
    attend(1)
    w1_line(0)
    g1_core()
    g1_end()
    pack_out(1)
    pack_zero()
    attended()
    control = (hid[...] + mod[2, 1:2, :] * out_project(1)).astype(BF16)

    @pl.when(b == 0)
    def _():
        stage[...] = control
        send(stage, out.at[0], o_s.at[0], o_r.at[0], partner)

    @pl.when(b == 1)
    def _():
        out[1] = control

    residual = zero_project(control)
    base_in = jnp.where(b == 0, lat[b].astype(F32), rlat[...].astype(F32)) + residual.astype(F32)
    hid[...] = base_in
    gb[0, pl.ds(pl.multiple_of(64 * z, 64), 64), :] = normed(base_in, 0)
    ring_start(0, 0)
    ring_start(0, 1)
    w1_core(0)

    @pl.when(b == 0)
    def _():
        g0_line()


    @pl.when(b == 1)
    def _():
        res_s[...] = residual
        send(res_s, rres, r_s.at[0], r_r.at[0], partner)

    ring_step(0, 2)
    w1_end(0)
    pack_query(0)
    project(0, 1)
    ring_step(0, 3)
    project(0, 2)
    ring_step(0, 4)
    project(0, 3)
    ring_end(0)
    project(0, 4)

    @pl.when(b == 0)
    def _():
        g0_core()

    halo_end(0)
    attend(0)

    @pl.when(b == 0)
    def _():
        g0_end()
        pack_out(0)
        arrived(rres, r_r.at[0])
        attended_base()
        second = lat[1].astype(F32) + rres[...].astype(F32)
        gated = mod[2, 0:1, :] * out_project(0)
        out[0] = (hid[...] + gated[0:64]).astype(BF16)
        out[1] = (second + gated[64:128]).astype(BF16)
        sent(stage, o_s.at[0])
        g0_sent()

    @pl.when(b == 1)
    def _():
        arrived(out.at[0], o_r.at[0])
        sent(res_s, r_s.at[0])

    for copy in lat_copies:
        copy.wait_send()
    g1_y_sent()
    g0_y(False)
    g1_sent()
    for copy in (1, 0):
        w1_y(copy, False)
        w1_tree(copy, False)
        w1_sent(copy)
        ring_sent(copy)
        attend_sent(copy)


def on_device(latent, modulation, w_query, w_keyval, w_out, w_zero):
    dma = pltpu.SemaphoreType.DMA
    vmem = pltpu.VMEM
    result = pl.pallas_call(
        kernel,
        out_shape=jax.ShapeDtypeStruct((2, 64, D), BF16),
        in_specs=[pl.BlockSpec(memory_space=pl.ANY)] + [pl.BlockSpec(memory_space=pltpu.VMEM)] * 5,
        out_specs=pl.BlockSpec(memory_space=pltpu.VMEM),
        scratch_shapes=[
            vmem((2, 64, D), BF16),
            vmem((2, 320, D), BF16),
            vmem((2, 4, 4, 64, D), BF16),
            vmem((2, 4, 4, 32, D), BF16),
            vmem((2, 512, D), BF16),
            vmem((2, 4, 2 * HP, 128), BF16),
            vmem((2, 4, 2 * HP, 128), BF16),
            vmem((2, 4, 2 * HP, 128), BF16),
            vmem((2, 512, 128), BF16),
            vmem((8, 64, 128), BF16),
            vmem((2, 8, 64, 128), BF16),
            vmem((4, 128, D), F32),
            vmem((64, D), F32),
            vmem((64, D), BF16),
            vmem((64, D), BF16),
            vmem((64, D), BF16),
            vmem((64, D), BF16),
            vmem((512, HP), BF16),
            vmem((HP, D), BF16),
            vmem((8 * HP, D), BF16),
            vmem((1280, D), BF16),
            dma((1,)), dma((2,)), dma((2,)),
            dma((2, 4)), dma((2, 4, 2)), dma((2, 4, 3)), dma((2, 4)), dma((16,)),
            dma((2, 4)), dma((4, 3)), dma((4,)), dma((4,)), dma((4, 4)), dma((4,)), dma((4,)), dma((4,)),
            dma((3,)), dma((3,)), dma((4,)), dma((4,)), dma((4,)), dma((4,)),
            dma((2, 2, 4, 2)), dma((2, 2, 4, 2)), dma((2, 2, 4)), dma((2, 2, 4)),
            dma((2, 8)), dma((8,)), dma((2, 8)), dma((1,)), dma((1,)), dma((1,)), dma((1,)),
        ],
        compiler_params=pltpu.CompilerParams(
            collective_id=0, has_side_effects=True, vmem_limit_bytes=56 * 1024 * 1024
        ),
    )(
        latent.reshape(2, 64, D), modulation.swapaxes(0, 1), w_query[0].T, w_keyval[0].T, w_out[0], w_zero.T,
    )
    return result.reshape(latent.shape)


def solution(mesh):
    placed = (
        P("branch", None, "trow", "tcol", None),
        P(),
        P("branch", None, "tcol"),
        P("branch", None, "tcol"),
        P("branch", "tcol", None),
        P(None, "tcol"),
    )
    return jax.shard_map(
        on_device,
        mesh=mesh,
        in_specs=placed,
        out_specs=P("branch", None, "trow", "tcol", None),
        check_vma=False,
    )
```

```python
import math

import jax
import jax.numpy as jnp
from jax import lax
from jax.experimental import pallas as pl
from jax.experimental.pallas import tpu as pltpu
from jax.sharding import PartitionSpec as P

MESH = pl.DeviceIdType.MESH
F32 = jnp.float32
BF16 = jnp.bfloat16
D = 1152
HD = 72
GP = 24
HP = 96
NEG = -1e30
NT = (((1,), (1,)), ((), ()))
NN = (((1,), (0,)), ((), ()))


def dot(a, b, dims):
    return lax.dot_general(a, b, dims, preferred_element_type=F32)


def pick(rows, cols, pieces):
    r = lax.broadcasted_iota(jnp.int32, (rows, cols), 0)
    c = lax.broadcasted_iota(jnp.int32, (rows, cols), 1)
    hit = None
    for row0, col0, count in pieces:
        one = (r - row0 == c - col0) & (r >= row0) & (r < row0 + count)
        hit = one if hit is None else hit | one
    return jnp.where(hit, 1.0, 0.0).astype(BF16)


def kernel(
    lat_h, mod, wq, wkv, wo, wz, out,
    lat,
    wb, g1, g0, gb, kvo, kvl, kvr, ob, ab, ab0, bias, hid, rlat, rres, stage, res_s, q_s, wq_s, wo_s, wz_s,
    in_s, lat_s, lat_r, w1y_s, w1t_s, w1x_s, w1s_s, w1_r, g1y_s, g1x_s, g1s_s, g1y_r, g1x_r, g1s_r, g1o_s, g1o_r,
    g0y_s, g0x_s, g0s_s, g0y_r, g0x_r, g0s_r, z_s, z_r, h_s, h_r, a_s, a_r, a0_r, o_s, o_r, r_s, r_r,
):
    b = lax.axis_index("branch")
    z = lax.axis_index("trow")
    t = lax.axis_index("tcol")
    x, y, c = t // 8, (t // 2) % 4, t % 2
    yy = b * 4 + y
    partner = (1 - b, z, t)
    sibling = (b, z, t + 1 - 2 * c)
    left = (b, z, (t + 31) % 32)
    right = (b, z, (t + 1) % 32)
    column = []
    for k in range(1, 8):
        other = (yy + k) % 8
        column.append((other // 4, z, x * 8 + (other % 4) * 2 + c))
    line = [(b, z, ((x + k) % 4) * 8 + y * 2 + c) for k in range(1, 4)]
    ring = [(b, (z + k) % 8, t) for k in range(1, 8)]
    far = jnp.where(c == 0, (t + 31) % 32, (t + 1) % 32)

    def send(src, dst, ss, rs, dev):
        copy = pltpu.make_async_remote_copy(
            src_ref=src, dst_ref=dst, send_sem=ss, recv_sem=rs, device_id=dev, device_id_type=MESH
        )
        copy.start()
        return copy

    def arrived(dst, rs):
        pltpu.make_async_remote_copy(
            src_ref=dst, dst_ref=dst, send_sem=lat_s.at[0], recv_sem=rs, device_id=partner, device_id_type=MESH
        ).wait_recv()

    def sent(src, ss):
        pltpu.make_async_remote_copy(
            src_ref=src, dst_ref=src, send_sem=ss, recv_sem=lat_r.at[0], device_id=partner, device_id_type=MESH
        ).wait_send()

    barrier = pltpu.get_barrier_semaphore()
    near = [column[k - 1] for k in (1, 2, 4, 6, 7)]
    peers = near + line + [ring[0], ring[6], sibling, (b, z, far)]
    for dev in peers:
        pl.semaphore_signal(barrier, inc=1, device_id=dev, device_id_type=MESH)

    load = pltpu.make_async_copy(lat_h, lat, in_s.at[0])
    load.start()

    rows = (
        dot(pick(144, 18, [(0, 0, 18)]), wq[...], NN)
        + dot(pick(144, 36, [(32, 0, 18), (56, 18, 18)]), wkv[...], NN)
        + dot(pick(144, 36, [(80, 0, 36)]), wz[...], NN)
        + dot(pick(144, 18, [(120, 0, 18)]), wo[...], NN)
    ).astype(BF16)
    own_q, own_kv = t // 4 == z, (t // 2) % 8 == z
    q_row = pl.multiple_of(32 * (t % 4), 16)
    kv_row = pl.multiple_of(128 + 96 * (t // 16) + 48 * c, 16)
    kv_idx = 4 + 2 * (t // 16) + c

    @pl.when(own_q)
    def _():
        wb[b, pl.ds(q_row, 32), :] = rows[0:32]

    @pl.when(own_kv)
    def _():
        wb[b, pl.ds(kv_row, 48), :] = rows[32:80]

    @pl.when(b == 1)
    def _():
        g1[c, x, y] = rows[80:144]

    @pl.when(b == 0)
    def _():
        g0[c, x, y] = jnp.concatenate(
            [rows[120:144].astype(F32), jnp.zeros((8, D), F32)], axis=0
        ).astype(BF16)

    pl.semaphore_wait(barrier, len(peers))

    def lat_half(h):
        return send(
            lat_h.at[1 - b, pl.ds(32 * h, 32)], rlat.at[pl.ds(32 * h, 32)], lat_s.at[h], lat_r.at[h], partner
        )

    lat_copies = [lat_half(0), lat_half(1)]

    def w1_y(copy, start):
        @pl.when(own_q & (b == copy))
        def _():
            piece = wb.at[copy, pl.ds(q_row, 32)]
            for n, k in enumerate((2, 6, 1, 7)):
                if start:
                    send(piece, piece, w1y_s.at[0, n], w1_r.at[copy * 8 + t % 4], column[k - 1])
                else:
                    sent(piece, w1y_s.at[0, n])

        @pl.when(own_kv & (b == copy))
        def _():
            piece = wb.at[copy, pl.ds(kv_row, 48)]
            for n, k in enumerate((2, 6, 1, 7)):
                if start:
                    send(piece, piece, w1y_s.at[1, n], w1_r.at[copy * 8 + kv_idx], column[k - 1])
                else:
                    sent(piece, w1y_s.at[1, n])

    def g0_y(start):
        @pl.when(b == 0)
        def _():
            piece = g0.at[c, x, y]
            for k in range(1, 4):
                if start:
                    send(piece, piece, g0y_s.at[k - 1], g0y_r.at[y], (b, z, x * 8 + ((y + k) % 4) * 2 + c))
                else:
                    sent(piece, g0y_s.at[k - 1])

    w1_y(1, True)

    for block in range(4):
        first, last = max(block - 1, 0), min(block + 1, 3)
        lanes = (last - first + 1) * 128
        q = lax.broadcasted_iota(jnp.int32, (128, lanes), 0)
        k = lax.broadcasted_iota(jnp.int32, (128, lanes), 1)
        i, j = block * 16 + q // 8, t * 8 + q % 8
        row, col = first * 16 + k // 8, (t - 1) * 8 + k % 8
        row0, col0 = jnp.clip(i - 6, 0, 51), jnp.clip(j - 6, 0, 243)
        row_ok = (row >= row0) & (row < row0 + 13)
        for strip in range(3):
            here = col + 8 * strip
            ok = row_ok & (here >= col0) & (here < col0 + 13)
            bias[block, :, strip * lanes : (strip + 1) * lanes] = jnp.where(ok, 0.0, NEG)
    ob[...] = jnp.zeros_like(ob)

    def normed(hidden, copy):
        average = jnp.mean(hidden, axis=-1, keepdims=True)
        centred = hidden - average
        variance = jnp.mean(centred * centred, axis=-1, keepdims=True)
        shift, scale = mod[0, copy : copy + 1, :], mod[1, copy : copy + 1, :]
        return (centred * lax.rsqrt(variance + 1e-06) * (1.0 + scale) + shift).astype(BF16)

    def half_tile(copy, index, h):
        start = 64 * ((index + 8) % 8) + 32 * h
        return gb.at[copy, pl.ds(pl.multiple_of(start, 32), 32)]

    def ring_send(copy, s, way, h):
        tile = half_tile(copy, z - s + 1 if way == 0 else z + s - 1, h)
        send(tile, tile, z_s.at[copy, way, s - 1, h], z_r.at[copy, way, s - 1, h], ring[0] if way == 0 else ring[6])

    def ring_take(copy, s, way, h):
        arrived(half_tile(copy, z - s if way == 0 else z + s, h), z_r.at[copy, way, s - 1, h])

    def ring_start(copy, h):
        ring_send(copy, 1, 0, h)
        ring_send(copy, 1, 1, h)

    def ring_step(copy, s):
        for h in range(2):
            for way in range(2):
                ring_take(copy, s - 1, way, h)
                if s < 4 or h == way:
                    ring_send(copy, s, way, h)

    def ring_end(copy):
        ring_take(copy, 4, 0, 0)
        ring_take(copy, 4, 1, 1)

    def ring_sent(copy):
        for s in range(1, 5):
            for h in range(2):
                for way in range(2):
                    if s < 4 or h == way:
                        sent(half_tile(copy, z, h), z_s.at[copy, way, s - 1, h])

    def kinds(core):
        return (
            (32 * core, 32, core, 4 * z + core, z // 2),
            (32 * core + 64, 32, core + 2, 4 * z + core + 2, z // 2),
            (128 + 48 * core, 48, 4 + core, 2 * z + core, z // 4),
            (224 + 48 * core, 48, 6 + core, 16 + 2 * z + core, 2 + z // 4),
        )

    def w1_tree(copy, start):
        for n, (row, count, index, source, source_x) in enumerate(kinds(c)):
            piece = wb.at[copy, pl.ds(pl.multiple_of(row, 16), count)]
            away = (yy + 8 - (copy * 4 + (source // 2) % 4)) % 8
            for here, steps in ((2, (2, 1)), (6, (7,))):

                @pl.when((x == source_x) & (away == here))
                def _():
                    if start:
                        arrived(piece, w1_r.at[copy * 8 + index])
                    for m, k in enumerate(steps):
                        if start:
                            send(piece, piece, w1t_s.at[copy, n, m], w1_r.at[copy * 8 + index], column[k - 1])
                        else:
                            sent(piece, w1t_s.at[copy, n, m])

    def w1_line(copy):
        for n, (row, count, index, source, source_x) in enumerate(kinds(c)):
            piece = wb.at[copy, pl.ds(pl.multiple_of(row, 16), count)]
            away = (yy + 8 - (copy * 4 + (source // 2) % 4)) % 8

            @pl.when(x == source_x)
            def _():
                @pl.when((away != 0) & (away != 2) & (away != 6))
                def _():
                    arrived(piece, w1_r.at[copy * 8 + index])

                for k in range(3):
                    send(piece, piece, w1x_s.at[copy, n, k], w1_r.at[copy * 8 + index], line[k])
                send(piece, piece, w1s_s.at[copy, n], w1_r.at[copy * 8 + index], sibling)

    def w1_core(copy):
        for n, (row, count, index, source, source_x) in enumerate(kinds(c)):
            piece = wb.at[copy, pl.ds(pl.multiple_of(row, 16), count)]

            @pl.when(x != source_x)
            def _():
                arrived(piece, w1_r.at[copy * 8 + index])
                send(piece, piece, w1s_s.at[copy, n], w1_r.at[copy * 8 + index], sibling)

    def w1_end(copy):
        for row, count, index, source, source_x in kinds(1 - c):
            piece = wb.at[copy, pl.ds(pl.multiple_of(row, 16), count)]
            arrived(piece, w1_r.at[copy * 8 + index])

    def w1_sent(copy):
        for n, (row, count, index, source, source_x) in enumerate(kinds(c)):
            piece = wb.at[copy, pl.ds(pl.multiple_of(row, 16), count)]

            @pl.when(x == source_x)
            def _():
                for k in range(3):
                    sent(piece, w1x_s.at[copy, n, k])

            sent(piece, w1s_s.at[copy, n])

    def g1_line(yk):
        for n in range(3):
            send(g1.at[c, x, yk], g1.at[c, x, yk], g1x_s.at[yk, n], g1x_r.at[x, yk], line[n])
        send(g1.at[c, x, yk], g1.at[c, x, yk], g1o_s.at[yk], g1o_r.at[yk], sibling)

    def g1_send(s, way):
        at = (yy + 9 - s if way == 0 else yy + s - 1) % 8
        piece = g1.at[c, x, at % 4]

        @pl.when(at >= 4)
        def _():
            send(piece, piece, g1y_s.at[way, s - 1], g1y_r.at[at % 4], column[0 if way == 0 else 6])

    def g1_take(s, way):
        at = (yy + 8 - s if way == 0 else yy + s) % 8

        @pl.when(at >= 4)
        def _():
            arrived(g1.at[c, x, at % 4], g1y_r.at[at % 4])
            if s < (4 if way == 0 else 3):
                g1_pass(s + 1, way)
            g1_line(at % 4)

    def g1_pass(s, way):
        at = (yy + 9 - s if way == 0 else yy + s - 1) % 8
        piece = g1.at[c, x, at % 4]
        send(piece, piece, g1y_s.at[way, s - 1], g1y_r.at[at % 4], column[0 if way == 0 else 6])

    def g1_y_sent():
        for way in range(2):
            for s in range(1, 5 - way):
                at = (yy + 9 - s if way == 0 else yy + s - 1) % 8

                @pl.when(at >= 4)
                def _():
                    sent(g1.at[c, x, at % 4], g1y_s.at[way, s - 1])

    def g1_core():
        for k in range(1, 4):
            xk = (x + k) % 4
            for yk in range(4):
                arrived(g1.at[c, xk, yk], g1x_r.at[xk, yk])
            send(g1.at[c, xk], g1.at[c, xk], g1s_s.at[k], g1s_r.at[xk], sibling)

    def g1_end():
        for yk in range(4):
            arrived(g1.at[1 - c, x, yk], g1o_r.at[yk])
        for k in range(1, 4):
            arrived(g1.at[1 - c, (x + k) % 4], g1s_r.at[(x + k) % 4])

    def g1_sent():
        for yk in range(4):
            for k in range(3):
                sent(g1.at[c, x, yk], g1x_s.at[yk, k])
            sent(g1.at[c, x, yk], g1o_s.at[yk])
        for k in range(1, 4):
            sent(g1.at[c, (x + k) % 4], g1s_s.at[k])

    def g0_line():
        for k in range(1, 4):
            yk = (y + k) % 4
            arrived(g0.at[c, x, yk], g0y_r.at[yk])
        for k in range(3):
            send(g0.at[c, x], g0.at[c, x], g0x_s.at[k], g0x_r.at[x], line[k])
        send(g0.at[c, x], g0.at[c, x], g0s_s.at[0], g0s_r.at[x], sibling)

    def g0_core():
        for k in range(1, 4):
            xk = (x + k) % 4
            arrived(g0.at[c, xk], g0x_r.at[xk])
            send(g0.at[c, xk], g0.at[c, xk], g0s_s.at[k], g0s_r.at[xk], sibling)

    def g0_end():
        for xk in range(4):
            arrived(g0.at[1 - c, xk], g0s_r.at[xk])

    def g0_sent():
        for k in range(3):
            sent(g0.at[c, x], g0x_s.at[k])
        for k in range(4):
            sent(g0.at[c, (x + k) % 4], g0s_s.at[k])

    side = 1 - 2 * (z % 2)
    order = [z // 2, (z // 2 + 4 - side) % 4, (z // 2 + 4 + side) % 4, (z // 2 + 2) % 4]

    def pack_query(copy):
        wq_s[...] = jnp.concatenate(
            [wb[copy, 32 * n : 32 * n + 32, :].astype(F32)[0:GP] for n in range(4)], axis=0
        ).astype(BF16)

    def project(copy, s):
        pair = order[s - 1]
        span = pl.ds(pl.multiple_of(128 * pair, 128), 128)
        tokens = gb[copy, span, :]
        kvo[copy, pair] = dot(wb[copy, 128:320, :], tokens, NT).astype(BF16)
        send(kvo.at[copy, pair], kvl.at[copy, pair], h_s.at[copy, 0, s - 1], h_r.at[copy, 0, s - 1], right)
        send(kvo.at[copy, pair], kvr.at[copy, pair], h_s.at[copy, 1, s - 1], h_r.at[copy, 1, s - 1], left)
        q_s[span, :] = dot(tokens, wq_s[...], NT).astype(BF16)

    def halo_end(copy):
        for s in range(4):
            arrived(kvl.at[copy, order[s]], h_r.at[copy, 0, s])
            arrived(kvr.at[copy, order[s]], h_r.at[copy, 1, s])

    def attend(copy):
        for block in range(4):
            first, last = max(block - 1, 0), min(block + 1, 3)
            lanes = (last - first + 1) * 128
            pieces = [ref[copy, n] for ref in (kvl, kvo, kvr) for n in range(first, last + 1)]
            keys = jnp.concatenate([piece[0:HP] for piece in pieces], axis=1)
            values = jnp.concatenate([piece[HP : 2 * HP] for piece in pieces], axis=1)
            scores = dot(q_s[block * 128 : block * 128 + 128, :], keys, NN) * (1.0 / math.sqrt(HD))
            scores = scores + bias[block, :, 0 : 3 * lanes]
            raised = jnp.exp(scores - jnp.max(scores, axis=-1, keepdims=True))
            weights = (raised * (1.0 / jnp.sum(raised, axis=-1, keepdims=True))).astype(BF16)
            ob[copy, block * 128 : block * 128 + 128, 0:HP] = dot(weights, values, NT).astype(BF16)
            for tile in (2 * block, 2 * block + 1):
                piece = ob.at[copy, pl.ds(64 * tile, 64)]
                if copy == 1:

                    @pl.when(z != tile)
                    def _():
                        send(piece, ab.at[z], a_s.at[copy, tile], a_r.at[z], (b, tile, t))
                else:

                    @pl.when((z != tile) | (b == 1))
                    def _():
                        send(piece, ab0.at[b, z], a_s.at[copy, tile], a0_r.at[b, z], (0, tile, t))

    def own_tile(copy):
        return ob[copy, pl.ds(pl.multiple_of(64 * z, 64), 64), :]

    def attended():
        ab[z] = own_tile(1)
        for k in range(1, 8):
            head = (z + k) % 8
            arrived(ab.at[head], a_r.at[head])

    def attended_base():
        ab0[0, z] = own_tile(0)
        for k in range(8):
            head = (z + k) % 8
            if k > 0:
                arrived(ab0.at[0, head], a0_r.at[0, head])
            arrived(ab0.at[1, head], a0_r.at[1, head])

    def attend_sent(copy):
        for s in range(4):
            sent(kvo.at[copy, order[s]], h_s.at[copy, 0, s])
            sent(kvo.at[copy, order[s]], h_s.at[copy, 1, s])
        for tile in range(8):

            @pl.when((z != tile) | ((b == 1) & (copy == 0)))
            def _():
                sent(ob.at[copy, pl.ds(64 * tile, 64)], a_s.at[copy, tile])

    def pack_out(copy):
        for head in range(8):
            parts = []
            for n in range(4):
                at = (n % 2, head // 2, 2 * (head % 2) + n // 2)
                if copy == 1:
                    parts.append(g1[at].astype(F32)[40:64])
                else:
                    parts.append(g0[at].astype(F32)[0:GP])
            wo_s[HP * head : HP * head + HP, :] = jnp.concatenate(parts, axis=0).astype(BF16)

    def out_project(copy):
        if copy == 1:
            mixed = jnp.concatenate([ab[head][:, 0:HP] for head in range(8)], axis=1)
        else:
            mixed = jnp.concatenate(
                [
                    jnp.concatenate([ab0[image, head][:, 0:HP] for head in range(8)], axis=1)
                    for image in range(2)
                ],
                axis=0,
            )
        return dot(mixed, wo_s[...], NN)

    def pack_zero():
        for pair in range(16):
            two = [g1[core, pair // 4, pair % 4].astype(F32)[0:40] for core in range(2)]
            wz_s[80 * pair : 80 * pair + 80, :] = jnp.concatenate(two, axis=0).astype(BF16)

    def zero_project(control):
        wide = dot(control, wz_s[...], NT)
        return jnp.concatenate([wide[:, 40 * n : 40 * n + 36] for n in range(32)], axis=1).astype(BF16)

    load.wait()
    for h in range(2):
        part = pl.ds(32 * h, 32)
        arrived(rlat.at[part], lat_r.at[h])
        control_in = lat[b, part, :].astype(F32) + rlat[part, :].astype(F32)
        hid[part, :] = control_in
        gb[1, pl.ds(pl.multiple_of(64 * z + 32 * h, 32), 32), :] = normed(control_in, 1)
        ring_start(1, h)

    w1_tree(1, True)
    g1_send(1, 0)
    g1_send(1, 1)

    @pl.when(b == 1)
    def _():
        g1_line(y)

    ring_step(1, 2)
    w1_line(1)
    ring_step(1, 3)
    g1_take(1, 0)
    g1_take(1, 1)
    ring_step(1, 4)
    g1_take(2, 0)
    g1_take(2, 1)
    w1_core(1)
    ring_end(1)
    w1_y(0, True)
    w1_end(1)
    pack_query(1)
    project(1, 1)
    project(1, 2)
    g1_take(3, 0)
    g1_take(3, 1)
    project(1, 3)
    project(1, 4)
    g1_take(4, 0)
    halo_end(1)
    w1_tree(0, True)
    g0_y(True)
    attend(1)
    g1_core()
    w1_line(0)
    g1_end()
    pack_out(1)
    pack_zero()
    attended()
    control = (hid[...] + mod[2, 1:2, :] * out_project(1)).astype(BF16)

    @pl.when(b == 0)
    def _():
        stage[...] = control
        send(stage, out.at[0], o_s.at[0], o_r.at[0], partner)

    @pl.when(b == 1)
    def _():
        out[1] = control

    residual = zero_project(control)
    base_in = jnp.where(b == 0, lat[b].astype(F32), rlat[...].astype(F32)) + residual.astype(F32)
    hid[...] = base_in
    gb[0, pl.ds(pl.multiple_of(64 * z, 64), 64), :] = normed(base_in, 0)
    ring_start(0, 0)
    ring_start(0, 1)
    w1_core(0)

    @pl.when(b == 0)
    def _():
        g0_line()


    @pl.when(b == 1)
    def _():
        res_s[...] = residual
        send(res_s, rres, r_s.at[0], r_r.at[0], partner)

    ring_step(0, 2)
    w1_end(0)
    pack_query(0)
    project(0, 1)
    ring_step(0, 3)
    project(0, 2)
    ring_step(0, 4)
    project(0, 3)
    ring_end(0)
    project(0, 4)

    @pl.when(b == 0)
    def _():
        g0_core()

    halo_end(0)
    attend(0)

    @pl.when(b == 0)
    def _():
        g0_end()
        pack_out(0)
        arrived(rres, r_r.at[0])
        attended_base()
        second = lat[1].astype(F32) + rres[...].astype(F32)
        gated = mod[2, 0:1, :] * out_project(0)
        out[0] = (hid[...] + gated[0:64]).astype(BF16)
        out[1] = (second + gated[64:128]).astype(BF16)
        sent(stage, o_s.at[0])
        g0_sent()

    @pl.when(b == 1)
    def _():
        arrived(out.at[0], o_r.at[0])
        sent(res_s, r_s.at[0])

    for copy in lat_copies:
        copy.wait_send()
    g1_y_sent()
    g0_y(False)
    g1_sent()
    for copy in (1, 0):
        w1_y(copy, False)
        w1_tree(copy, False)
        w1_sent(copy)
        ring_sent(copy)
        attend_sent(copy)


def on_device(latent, modulation, w_query, w_keyval, w_out, w_zero):
    dma = pltpu.SemaphoreType.DMA
    vmem = pltpu.VMEM
    result = pl.pallas_call(
        kernel,
        out_shape=jax.ShapeDtypeStruct((2, 64, D), BF16),
        in_specs=[pl.BlockSpec(memory_space=pl.ANY)] + [pl.BlockSpec(memory_space=pltpu.VMEM)] * 5,
        out_specs=pl.BlockSpec(memory_space=pltpu.VMEM),
        scratch_shapes=[
            vmem((2, 64, D), BF16),
            vmem((2, 320, D), BF16),
            vmem((2, 4, 4, 64, D), BF16),
            vmem((2, 4, 4, 32, D), BF16),
            vmem((2, 512, D), BF16),
            vmem((2, 4, 2 * HP, 128), BF16),
            vmem((2, 4, 2 * HP, 128), BF16),
            vmem((2, 4, 2 * HP, 128), BF16),
            vmem((2, 512, 128), BF16),
            vmem((8, 64, 128), BF16),
            vmem((2, 8, 64, 128), BF16),
            vmem((4, 128, D), F32),
            vmem((64, D), F32),
            vmem((64, D), BF16),
            vmem((64, D), BF16),
            vmem((64, D), BF16),
            vmem((64, D), BF16),
            vmem((512, HP), BF16),
            vmem((HP, D), BF16),
            vmem((8 * HP, D), BF16),
            vmem((1280, D), BF16),
            dma((1,)), dma((2,)), dma((2,)),
            dma((2, 4)), dma((2, 4, 2)), dma((2, 4, 3)), dma((2, 4)), dma((16,)),
            dma((2, 4)), dma((4, 3)), dma((4,)), dma((4,)), dma((4, 4)), dma((4,)), dma((4,)), dma((4,)),
            dma((3,)), dma((3,)), dma((4,)), dma((4,)), dma((4,)), dma((4,)),
            dma((2, 2, 4, 2)), dma((2, 2, 4, 2)), dma((2, 2, 4)), dma((2, 2, 4)),
            dma((2, 8)), dma((8,)), dma((2, 8)), dma((1,)), dma((1,)), dma((1,)), dma((1,)),
        ],
        compiler_params=pltpu.CompilerParams(
            collective_id=0, has_side_effects=True, vmem_limit_bytes=56 * 1024 * 1024
        ),
    )(
        latent.reshape(2, 64, D), modulation.swapaxes(0, 1), w_query[0].T, w_keyval[0].T, w_out[0], w_zero.T,
    )
    return result.reshape(latent.shape)


def solution(mesh):
    placed = (
        P("branch", None, "trow", "tcol", None),
        P(),
        P("branch", None, "tcol"),
        P("branch", None, "tcol"),
        P("branch", "tcol", None),
        P(None, "tcol"),
    )
    return jax.shard_map(
        on_device,
        mesh=mesh,
        in_specs=placed,
        out_specs=P("branch", None, "trow", "tcol", None),
        check_vma=False,
    )
```
